32 devices in a mesh: dp: 8 (over y, x, core), seq: 4 (over z).
Axes of the slice: x: 2, y: 2, z: 4, core: 2. Of those that a mesh axis runs over, the one named last changes fastest.
Arguments:
- activations: bfloat16 [16, 1024, 768], P('dp', 'seq'), may hold values from -6 to 6
- cotangent: bfloat16 [16, 1024, 768], P('dp', 'seq'), may hold values from -6 to 6
- segment_ids: int32 [16, 1024], P('dp'), may hold values from 0 to 2, as said below
- inputs_weight: float32 [768, 2304], P('seq'), may hold values from -0.21875 to 0.21875
- inputs_moment: float32 [768, 2304], P('seq')
- inputs_second: float32 [768, 2304], P('seq'), as said below
- output_weight: float32 [768, 768], P('seq'), may hold values from -2.5 to 2.5
- output_moment: float32 [768, 768], P('seq')
- output_second: float32 [768, 768], P('seq'), as said below
- expand_weight: float32 [768, 3072], P('seq'), may hold values from -0.21875 to 0.21875
- expand_moment: float32 [768, 3072], P('seq')
- expand_second: float32 [768, 3072], P('seq'), as said below
- reduce_weight: float32 [3072, 768], P('seq'), may hold values from -0.109375 to 0.109375
- reduce_moment: float32 [3072, 768], P('seq')
- reduce_second: float32 [3072, 768], P('seq'), as said below
- vector_params: float32 [12, 768], P(None, 'seq')
- vector_moment: float32 [12, 768], P(None, 'seq')
- vector_second: float32 [12, 768], P(None, 'seq'), as said below
Outputs:
- layer_output: bfloat16 [16, 1024, 768], P('dp', 'seq')
- input_grad: bfloat16 [16, 1024, 768], P('dp', 'seq')
- renewed_inputs: float32 [768, 2304], P('seq')
- momentum_inputs: float32 [768, 2304], P('seq')
- variance_inputs: float32 [768, 2304], P('seq')
- renewed_output: float32 [768, 768], P('seq')
- momentum_output: float32 [768, 768], P('seq')
- variance_output: float32 [768, 768], P('seq')
- renewed_expand: float32 [768, 3072], P('seq')
- momentum_expand: float32 [768, 3072], P('seq')
- variance_expand: float32 [768, 3072], P('seq')
- renewed_reduce: float32 [3072, 768], P('seq')
- momentum_reduce: float32 [3072, 768], P('seq')
- variance_reduce: float32 [3072, 768], P('seq')
- renewed_vectors: float32 [12, 768], P(None, 'seq')
- momentum_vectors: float32 [12, 768], P(None, 'seq')
- variance_vectors: float32 [12, 768], P(None, 'seq')
The draws below stay inside these ranges and needn't reach their ends.
Inputs may be any that keep to these rules, and one draw needn't show every extreme that they name: `segment_ids`: in each sequence the segment number is 0 on a first run of positions, 1 on a middle run and 2 on a last run; the first and the last run each hold 204 to 255 positions. `inputs_second`: entries are positive. `output_second`: entries are positive. `expand_second`: entries are positive. `reduce_second`: entries are positive. `vector_second`: entries are positive.
All inputs are finite; a program needn't handle non-finite values.
Results may differ from the reference program's by a relative error of at most 0.014.
Values may be sent and summed in bfloat16 or wider, within the bound.
No kernel may reach another device: no remote copies, remote signals or barrier semaphores. Data moves between devices by JAX's collectives and lax.ppermute only.
A program may use at most 256 MiB of HBM per device.

```python
import math
import jax
import jax.numpy as jnp
from jax import lax

D = 768
HEADS = 12
HD = 64
FF = 3072
LEN = 1024
STEP = 10
VROWS = 12
SEQS = 16


def grad_size(factor):
    return factor * math.sqrt(SEQS * LEN)


def first_moment(key, array_shape, factor):
    return 0.11 * grad_size(factor) * jax.random.normal(key, array_shape, jnp.float32)


def second_moment(key, array_shape, factor):
    scale_sq = grad_size(factor) ** 2
    return 0.0526 * scale_sq * jnp.exp(jax.random.uniform(key, array_shape, jnp.float32, 0.0, math.log(4.0)))


def draw_segment_ids(key, part):
    key = jax.random.fold_in(key, 1)
    first_key, last_key = jax.random.split(key)
    first_len = jax.random.randint(first_key, (SEQS, 1), LEN // 5, LEN // 4)
    last_len = jax.random.randint(last_key, (SEQS, 1), LEN // 5, LEN // 4)
    places = jnp.arange(LEN, dtype=jnp.int32)[None, :]
    return (places >= first_len).astype(jnp.int32) + (places >= LEN - last_len).astype(jnp.int32)


def draw_vector_params(key, part):
    key = jax.random.fold_in(key, 2)
    gain_key, bias_key = jax.random.split(key)
    row_ids = jnp.arange(VROWS, dtype=jnp.int32)[:, None]
    gain_draw = 0.75 + 0.5 * jax.random.uniform(gain_key, (VROWS, D), jnp.float32)
    biases = 0.3 * jax.random.normal(bias_key, (VROWS, D), jnp.float32)
    is_gain = (row_ids == 0) | (row_ids == 2)
    return jnp.where(is_gain, gain_draw, biases)


def draw_inputs_moment(key, part):
    key = jax.random.fold_in(key, 3)
    return first_moment(key, (D, 3 * D), 0.4)


def draw_inputs_second(key, part):
    key = jax.random.fold_in(key, 4)
    return second_moment(key, (D, 3 * D), 0.4)


def draw_output_moment(key, part):
    key = jax.random.fold_in(key, 5)
    return first_moment(key, (D, D), 0.1)


def draw_output_second(key, part):
    key = jax.random.fold_in(key, 6)
    return second_moment(key, (D, D), 0.1)


def draw_expand_moment(key, part):
    key = jax.random.fold_in(key, 7)
    return first_moment(key, (D, FF), 0.3)


def draw_expand_second(key, part):
    key = jax.random.fold_in(key, 8)
    return second_moment(key, (D, FF), 0.3)


def draw_reduce_moment(key, part):
    key = jax.random.fold_in(key, 9)
    return first_moment(key, (FF, D), 0.6)


def draw_reduce_second(key, part):
    key = jax.random.fold_in(key, 10)
    return second_moment(key, (FF, D), 0.6)


def draw_vector_moment(key, part):
    key = jax.random.fold_in(key, 11)
    return first_moment(key, (VROWS, D), 0.5)


def draw_vector_second(key, part):
    key = jax.random.fold_in(key, 12)
    return second_moment(key, (VROWS, D), 0.5)


def steps_of(stream_key, shape, cuts, smallest, high):
    gain, own = 1.0, jax.random.fold_in(stream_key, 6)
    for dim, blocks in cuts:
        draws = jnp.exp(jax.random.uniform(jax.random.fold_in(own, dim), (blocks,), jnp.float32, smallest / len(cuts), high / len(cuts)))
        gain = gain * jnp.repeat(draws, shape[dim] // blocks).reshape([-1 if axis == dim else 1 for axis in range(len(shape))])
    return gain


def gaussian(own_key, dims, scale, bound, cuts=(), held_as=jnp.bfloat16):
    level = steps_of(own_key, dims, cuts, -0.22, 0.18) if cuts else 1.0
    entries = jax.random.normal(own_key, dims, jnp.float32) * scale * level
    return jnp.minimum(jnp.maximum(entries, -bound), bound).astype(held_as)


def setup_inputs(seed: int = 0) -> dict:
    streams_of = jax.random.split(jax.random.key(seed), 19)
    activations = gaussian(streams_of[0], (SEQS, LEN, D), 1.0, 6.0, ((0, 8), (1, 4)))
    cotangent = gaussian(streams_of[1], (SEQS, LEN, D), 1.0, 6.0, ((0, 8), (1, 4)))
    segment_ids = draw_segment_ids(jax.random.fold_in(streams_of[18], 71), 0)
    inputs_weight = gaussian(streams_of[3], (D, 3 * D), D ** -0.5, 0.21875, ((0, 4),), jnp.float32)
    inputs_moment = draw_inputs_moment(jax.random.fold_in(streams_of[18], 71), 0)
    inputs_second = draw_inputs_second(jax.random.fold_in(streams_of[18], 71), 0)
    output_weight = gaussian(streams_of[6], (D, D), (D * 8 // LEN) ** -0.5, 2.5, ((0, 4),), jnp.float32)
    output_moment = draw_output_moment(jax.random.fold_in(streams_of[18], 71), 0)
    output_second = draw_output_second(jax.random.fold_in(streams_of[18], 71), 0)
    expand_weight = gaussian(streams_of[9], (D, FF), D ** -0.5, 0.21875, ((0, 4),), jnp.float32)
    expand_moment = draw_expand_moment(jax.random.fold_in(streams_of[18], 71), 0)
    expand_second = draw_expand_second(jax.random.fold_in(streams_of[18], 71), 0)
    reduce_weight = gaussian(streams_of[12], (FF, D), FF ** -0.5, 0.109375, ((0, 4),), jnp.float32)
    reduce_moment = draw_reduce_moment(jax.random.fold_in(streams_of[18], 71), 0)
    reduce_second = draw_reduce_second(jax.random.fold_in(streams_of[18], 71), 0)
    vector_params = draw_vector_params(jax.random.fold_in(streams_of[18], 71), 0)
    vector_moment = draw_vector_moment(jax.random.fold_in(streams_of[18], 71), 0)
    vector_second = draw_vector_second(jax.random.fold_in(streams_of[18], 71), 0)
    return {"activations": activations, "cotangent": cotangent, "segment_ids": segment_ids, "inputs_weight": inputs_weight, "inputs_moment": inputs_moment, "inputs_second": inputs_second, "output_weight": output_weight, "output_moment": output_moment, "output_second": output_second, "expand_weight": expand_weight, "expand_moment": expand_moment, "expand_second": expand_second, "reduce_weight": reduce_weight, "reduce_moment": reduce_moment, "reduce_second": reduce_second, "vector_params": vector_params, "vector_moment": vector_moment, "vector_second": vector_second}


@jax.custom_vjp
def low(v):
    return lax.optimization_barrier(v.astype(jnp.bfloat16)).astype(jnp.float32)

@jax.custom_vjp
def low_back(v):
    return v

def low_keep(v):
    return (low(v), None)

def low_pass(kept, grad):
    return (grad,)

def back_keep(v):
    return (v, None)

def back_low(kept, grad):
    return (low(grad),)
low.defvjp(low_keep, low_pass)
low_back.defvjp(back_keep, back_low)
eps_norm = 1e-05
eps_adam = 1e-08
beta_one = 0.9
beta_two = 0.95
decay_rate = 0.1
mask_fill = -1e+30

def matmul(left_side, right_side):
    return jnp.dot(left_side, right_side, precision=lax.Precision.HIGHEST)

def layer_norm(values, norm_gain, norm_shift):
    center = lax.optimization_barrier(jnp.mean(values, axis=-1, keepdims=True))
    offsets = values - center
    spread = lax.optimization_barrier(jnp.mean(offsets * offsets, axis=-1, keepdims=True))
    return offsets * lax.rsqrt(spread + eps_norm) * norm_gain + norm_shift

def attend(operands):
    queries, keys_all, values_all, segments = operands
    key_count = queries.shape[0]
    places = jnp.arange(key_count, dtype=jnp.int32)
    allowed = (places[:, None] >= places[None, :]) & (segments[:, None] == segments[None, :])
    query_heads = queries.reshape(key_count, HEADS, HD)
    key_heads = keys_all.reshape(key_count, HEADS, HD)
    value_heads = values_all.reshape(key_count, HEADS, HD)
    scores = jnp.einsum('qhd,khd->hqk', query_heads, key_heads, precision=lax.Precision.HIGHEST) * HD ** (-0.5)
    scores = low_back(scores)
    masked = jnp.where(allowed[None], scores, mask_fill)
    softmax_out = low(jax.nn.softmax(masked, axis=-1))
    mixture = jnp.einsum('hqk,khd->qhd', softmax_out, value_heads, precision=lax.Precision.HIGHEST)
    return mixture.reshape(key_count, HEADS * HD)

def forward(params, inputs, segments):
    inputs_weight, output_weight, expand_weight, reduce_weight, vector_params = params
    vectors = low(vector_params)
    features = vectors.shape[1]
    seq_shape = inputs.shape
    token_count = seq_shape[0] * seq_shape[1]
    flat_rows = inputs.reshape(token_count, features)
    normed_one = low(layer_norm(flat_rows, vectors[0], vectors[1]))
    projected = matmul(normed_one, low(inputs_weight))
    queries = low(low_back(projected[:, :features] + vectors[4]))
    keys_here = low(low_back(projected[:, features:2 * features]))
    values_here = low(low_back(projected[:, 2 * features:] + vectors[5]))
    mixture = lax.map(jax.checkpoint(attend), (queries.reshape(seq_shape), keys_here.reshape(seq_shape), values_here.reshape(seq_shape), segments))
    mixture = low(low_back(mixture.reshape(token_count, features)))
    attended = low_back(matmul(mixture, low(output_weight)) + vectors[6])
    middle = flat_rows + attended
    normed_two = low(layer_norm(middle, vectors[2], vectors[3]))
    expanded = low_back(matmul(normed_two, low(expand_weight)) + vectors[8:].reshape(-1))
    hidden = low(jax.nn.gelu(expanded, approximate=False))
    reduced = low_back(matmul(hidden, low(reduce_weight)) + vectors[7])
    return (middle + reduced).reshape(seq_shape)

def adamw_step(weight, moment, second, gradient, step_rate, weight_decay):
    moment_new = beta_one * moment + (1.0 - beta_one) * gradient
    second_new = beta_two * second + (1.0 - beta_two) * gradient * gradient
    fix_one = 1.0 - beta_one ** STEP
    fix_two = 1.0 - beta_two ** STEP
    update = moment_new / fix_one / (jnp.sqrt(second_new / fix_two) + eps_adam)
    return (weight - step_rate * (update + weight_decay * weight), moment_new, second_new)

def reference(activations, cotangent, segment_ids, inputs_weight, inputs_moment, inputs_second, output_weight, output_moment, output_second, expand_weight, expand_moment, expand_second, reduce_weight, reduce_moment, reduce_second, vector_params, vector_moment, vector_second):
    params = (inputs_weight, output_weight, expand_weight, reduce_weight, vector_params)
    group_size = math.gcd(SEQS, max(1, 4096 // LEN))
    rounds = SEQS // group_size
    inputs_all = activations.astype(jnp.float32).reshape(rounds, group_size, LEN, D)
    cotangents = cotangent.astype(jnp.float32).reshape(rounds, group_size, LEN, D)
    segments_all = segment_ids.reshape(rounds, group_size, LEN)

    def scan_step(running, operands):
        inputs, grads_in, segments = operands
        outputs, pullback = jax.vjp(lambda weights, values: forward(weights, values, segments), params, inputs)
        grad_params, grad_inputs = pullback(grads_in)
        running = jax.tree.map(lambda earlier, addend: earlier + addend, running, grad_params)
        return (running, (outputs.astype(jnp.bfloat16), grad_inputs.astype(jnp.bfloat16)))
    zero_grads = jax.tree.map(jnp.zeros_like, params)
    totals, (outputs, grad_inputs) = lax.scan(scan_step, zero_grads, (inputs_all, cotangents, segments_all))
    grad_in, grad_out, grad_expand, grad_reduce, grad_vec = totals
    new_in = adamw_step(inputs_weight, inputs_moment, inputs_second, grad_in, 0.03, decay_rate)
    new_out = adamw_step(output_weight, output_moment, output_second, grad_out, 0.3, decay_rate)
    new_expand = adamw_step(expand_weight, expand_moment, expand_second, grad_expand, 0.03, decay_rate)
    new_reduce = adamw_step(reduce_weight, reduce_moment, reduce_second, grad_reduce, 0.02, decay_rate)
    new_vec = adamw_step(vector_params, vector_moment, vector_second, grad_vec, 0.5, 0.0)
    return (outputs.reshape(SEQS, LEN, D), grad_inputs.reshape(SEQS, LEN, D), new_in[0], new_in[1], new_in[2], new_out[0], new_out[1], new_out[2], new_expand[0], new_expand[1], new_expand[2], new_reduce[0], new_reduce[1], new_reduce[2], new_vec[0], new_vec[1], new_vec[2])
```

```python
from functools import partial

import jax
import jax.numpy as jnp
from jax import lax
from jax.experimental import pallas as pl
from jax.experimental.pallas import tpu as pltpu
from jax.sharding import PartitionSpec as P

HEADS = 12
HD = 64
STEP = 10
PAIR = 2 * HD
LANES = 128

eps_norm = 1e-05
eps_adam = 1e-08
beta_one = 0.9
beta_two = 0.95
decay_rate = 0.1
mask_fill = -1e30
vmem_bytes = 56 * 1024 * 1024

VISIBLE = (
    (0, 256, 0, 256),
    (256, 256, 128, 512),
    (512, 256, 128, 768),
    (768, 128, 128, 896),
    (896, 128, 768, 1024),
)
TILE_STARTS = []
tile_total = 0
for _first, _rows, _low, _high in VISIBLE:
    TILE_STARTS.append(tile_total)
    tile_total += _high - _low

low = jnp.bfloat16


def dot_nn(left_side, right_side):
    return lax.dot_general(
        left_side, right_side, (((1,), (0,)), ((), ())), preferred_element_type=jnp.float32
    )


def dot_tn(left_side, right_side):
    return lax.dot_general(
        left_side, right_side, (((0,), (0,)), ((), ())), preferred_element_type=jnp.float32
    )


def dot_nt(left_side, right_side):
    return lax.dot_general(
        left_side, right_side, (((1,), (1,)), ((), ())), preferred_element_type=jnp.float32
    )


def normalize(values):
    center = jnp.mean(values, axis=-1, keepdims=True)
    offsets = values - center
    spread = jnp.mean(offsets * offsets, axis=-1, keepdims=True)
    inverse = lax.rsqrt(spread + eps_norm)
    return offsets * inverse, inverse


def norm_back(grad_normed, gain, unit, inverse):
    scaled = grad_normed * gain
    mean_scaled = jnp.mean(scaled, axis=-1, keepdims=True)
    mean_cross = jnp.mean(scaled * unit, axis=-1, keepdims=True)
    return inverse * (scaled - mean_scaled - unit * mean_cross)


def adamw_step(weight, moment, second, gradient, step_rate, weight_decay):
    moment_new = beta_one * moment + (1.0 - beta_one) * gradient
    second_new = beta_two * second + (1.0 - beta_two) * gradient * gradient
    fix_one = 1.0 - beta_one**STEP
    fix_two = 1.0 - beta_two**STEP
    update = moment_new / fix_one / (jnp.sqrt(second_new / fix_two) + eps_adam)
    return (weight - step_rate * (update + weight_decay * weight), moment_new, second_new)


def column_sum(values):
    return jnp.sum(values.astype(jnp.float32), axis=0)


def fill_bias(seg_row, seg_col, bias):
    for (first, rows, key_low, key_high), start in zip(VISIBLE, TILE_STARTS):
        keys = key_high - key_low
        key_places = key_low + lax.broadcasted_iota(jnp.int32, (keys, rows), 0)
        query_places = first + lax.broadcasted_iota(jnp.int32, (keys, rows), 1)
        same = seg_col[key_low:key_high, :] == seg_row[:, first : first + rows]
        allowed = same & (key_places <= query_places)
        bias[start : start + keys, 0:rows] = jnp.where(allowed, 0.0, mask_fill)


def lane_masks(shape):
    lane = lax.broadcasted_iota(jnp.int32, shape, 1)
    return (lane < HD, lane >= HD)


def masked_to(values, mask):
    return jnp.where(mask, values, jnp.zeros_like(values))


def attend_forward_kernel(seg_row, seg_col, q_ref, k_ref, v_ref, out_ref, log_ref, bias):
    @pl.when(pl.program_id(0) == 0)
    def _():
        fill_bias(seg_row, seg_col, bias)

    masks = lane_masks((k_ref.shape[0], PAIR))
    keys_masked = [masked_to(k_ref[...], mask) for mask in masks]
    for (first, rows, key_low, key_high), start in zip(VISIBLE, TILE_STARTS):
        queries = q_ref[first : first + rows, :] * jnp.asarray(HD**-0.5, low)
        values = v_ref[key_low:key_high, :]
        mixed = []
        for head in range(2):
            scores = dot_nt(keys_masked[head][key_low:key_high], queries)
            scores = scores + bias[start : start + key_high - key_low, 0:rows]
            highest = jnp.max(scores, axis=0, keepdims=True)
            exponent = jnp.exp(scores - highest)
            totals = jnp.sum(exponent, axis=0, keepdims=True)
            soft = (exponent * (1.0 / totals)).astype(low)
            mixed.append(dot_tn(soft, values))
            log_ref[0, head : head + 1, first : first + rows] = highest + jnp.log(totals)
        half = lane_masks((rows, PAIR))[0]
        out_ref[first : first + rows, :] = jnp.where(half, mixed[0], mixed[1]).astype(low)


def attend_backward_kernel(
    seg_row, seg_col, q_ref, k_ref, v_ref, log_ref, do_ref, dq_ref, dk_ref, dv_ref, bias, dk_acc, dv_acc
):
    @pl.when(pl.program_id(0) == 0)
    def _():
        fill_bias(seg_row, seg_col, bias)

    masks = lane_masks((k_ref.shape[0], PAIR))
    keys_masked = [masked_to(k_ref[...], mask) for mask in masks]
    values_masked = [masked_to(v_ref[...], mask) for mask in masks]
    dk_acc[...] = jnp.zeros_like(dk_acc)
    dv_acc[...] = jnp.zeros_like(dv_acc)
    for (first, rows, key_low, key_high), start in zip(VISIBLE, TILE_STARTS):
        queries = q_ref[first : first + rows, :] * jnp.asarray(HD**-0.5, low)
        grads = do_ref[first : first + rows, :]
        grad_query = jnp.zeros((rows, PAIR), jnp.float32)
        row_masks = lane_masks((rows, PAIR))
        for head in range(2):
            keys = keys_masked[head][key_low:key_high]
            scores = dot_nt(keys, queries)
            scores = scores + bias[start : start + key_high - key_low, 0:rows]
            soft = jnp.exp(scores - log_ref[0, head : head + 1, first : first + rows])
            grad_soft = dot_nt(values_masked[head][key_low:key_high], grads)
            inner = jnp.sum(soft * grad_soft, axis=0, keepdims=True)
            grad_scores = (soft * (grad_soft - inner)).astype(low)
            dv_acc[key_low:key_high, :] += dot_nn(
                soft.astype(low), masked_to(grads, row_masks[head])
            )
            dk_acc[key_low:key_high, :] += dot_nn(
                grad_scores, masked_to(queries, row_masks[head])
            )
            grad_query = grad_query + dot_tn(grad_scores, keys)
        dq_ref[first : first + rows, :] = (grad_query * HD**-0.5).astype(low)
    dk_ref[...] = dk_acc[...].astype(low)
    dv_ref[...] = dv_acc[...].astype(low)


def attend_specs(length, pairs):
    whole = lambda shape: pl.BlockSpec(shape, lambda j: (0,) * len(shape))
    columns = lambda offset: pl.BlockSpec((length, PAIR), lambda j, offset=offset: (0, offset + j))
    logs = pl.BlockSpec((1, 8, length), lambda j: (j, 0, 0))
    return whole, columns, logs


def attend_forward(seg_row, seg_col, projected):
    length = projected.shape[0]
    pairs = projected.shape[1] // (3 * PAIR)
    whole, columns, logs = attend_specs(length, pairs)
    return pl.pallas_call(
        attend_forward_kernel,
        grid=(pairs,),
        in_specs=[
            whole((1, length)),
            whole((length, 1)),
            columns(0),
            columns(pairs),
            columns(2 * pairs),
        ],
        out_specs=[columns(0), logs],
        out_shape=[
            jax.ShapeDtypeStruct((length, pairs * PAIR), low),
            jax.ShapeDtypeStruct((pairs, 8, length), jnp.float32),
        ],
        scratch_shapes=[pltpu.VMEM((tile_total, 256), jnp.float32)],
        compiler_params=pltpu.CompilerParams(vmem_limit_bytes=vmem_bytes),
        cost_estimate=pl.CostEstimate(
            flops=4 * length * length * pairs * PAIR, bytes_accessed=8 * length * pairs * PAIR,
            transcendentals=length * length * pairs,
        ),
        name="attend_forward",
    )(seg_row, seg_col, projected, projected, projected)


def attend_backward(seg_row, seg_col, projected, logs_all, grad_mixture):
    length = projected.shape[0]
    pairs = projected.shape[1] // (3 * PAIR)
    whole, columns, logs = attend_specs(length, pairs)
    return pl.pallas_call(
        attend_backward_kernel,
        grid=(pairs,),
        in_specs=[
            whole((1, length)),
            whole((length, 1)),
            columns(0),
            columns(pairs),
            columns(2 * pairs),
            logs,
            columns(0),
        ],
        out_specs=[columns(0)] * 3,
        out_shape=[jax.ShapeDtypeStruct((length, pairs * PAIR), low)] * 3,
        scratch_shapes=[
            pltpu.VMEM((tile_total, 256), jnp.float32),
            pltpu.VMEM((length, PAIR), jnp.float32),
            pltpu.VMEM((length, PAIR), jnp.float32),
        ],
        compiler_params=pltpu.CompilerParams(vmem_limit_bytes=vmem_bytes),
        cost_estimate=pl.CostEstimate(
            flops=10 * length * length * pairs * PAIR, bytes_accessed=14 * length * pairs * PAIR,
            transcendentals=length * length * pairs,
        ),
        name="attend_backward",
    )(seg_row, seg_col, projected, projected, projected, logs_all, grad_mixture)


def feed_kernel(
    n2_ref, dy_ref, wu_ref, wd_ref, bu_ref, red_ref, dn2_ref, gu_ref, gd_ref, dbu_ref, n2_turned
):
    step = pl.program_id(0)

    @pl.when(step == 0)
    def _():
        n2_turned[...] = n2_ref[...].T
        red_ref[...] = jnp.zeros_like(red_ref)
        dn2_ref[...] = jnp.zeros_like(dn2_ref)

    normed = n2_ref[...]
    grad_top = dy_ref[...]
    expanded = dot_nn(normed, wu_ref[...]) + bu_ref[...]
    phi = 0.5 + 0.5 * lax.erf(expanded * (0.5**0.5))
    density = jnp.exp(-0.5 * expanded * expanded) * 0.3989422804014327
    hidden = (expanded * phi).astype(low)
    slope = phi + expanded * density
    grad_hidden = dot_nt(grad_top, wd_ref[...])
    grad_expanded = grad_hidden * slope
    grad_low = grad_expanded.astype(low)
    red_ref[...] += dot_nn(hidden, wd_ref[...])
    dn2_ref[...] += dot_nt(grad_low, wu_ref[...])
    gu_ref[...] = dot_nn(n2_turned[...], grad_low).astype(low)
    gd_ref[...] = dot_tn(hidden, grad_top).astype(low)
    dbu_ref[...] = jnp.sum(grad_low.astype(jnp.float32), axis=0, keepdims=True)


def feed_both(normed, grad_top, expand_low, reduce_low, expand_bias):
    rows, features = normed.shape
    hidden_count = reduce_low.shape[0]
    block = 512
    whole = pl.BlockSpec((rows, features), lambda j: (0, 0))
    across = pl.BlockSpec((features, block), lambda j: (0, j))
    down = pl.BlockSpec((block, features), lambda j: (j, 0))
    bias = pl.BlockSpec((1, block), lambda j: (0, j))
    return pl.pallas_call(
        feed_kernel,
        grid=(hidden_count // block,),
        in_specs=[whole, whole, across, down, bias],
        out_specs=[whole, whole, across, down, bias],
        out_shape=[
            jax.ShapeDtypeStruct((rows, features), jnp.float32),
            jax.ShapeDtypeStruct((rows, features), jnp.float32),
            jax.ShapeDtypeStruct((features, hidden_count), low),
            jax.ShapeDtypeStruct((hidden_count, features), low),
            jax.ShapeDtypeStruct((1, hidden_count), jnp.float32),
        ],
        scratch_shapes=[pltpu.VMEM((features, rows), low)],
        compiler_params=pltpu.CompilerParams(vmem_limit_bytes=vmem_bytes),
        cost_estimate=pl.CostEstimate(
            flops=12 * rows * features * hidden_count,
            bytes_accessed=8 * features * hidden_count,
            transcendentals=2 * rows * hidden_count,
        ),
        name="feed_both",
    )(normed, grad_top, expand_low, reduce_low, expand_bias)


def chip_routes(dp_count, seq_count):
    straight, crossed = [], []
    for place in range(dp_count):
        group, core = place - place % 2, place % 2
        for quarter in range(seq_count):
            source = place * seq_count + quarter
            holder = (group + quarter // 2) * seq_count
            straight.append((source, holder + 2 * core + quarter % 2))
            crossed.append((source, holder + 2 * core + 1 - quarter % 2))
    return straight, crossed


def on_device(
    dp_count,
    seq_count,
    activations,
    cotangent,
    segment_ids,
    inputs_weight,
    inputs_moment,
    inputs_second,
    output_weight,
    output_moment,
    output_second,
    expand_weight,
    expand_moment,
    expand_second,
    reduce_weight,
    reduce_moment,
    reduce_second,
    vector_params,
    vector_moment,
    vector_second,
):
    axes = ("dp", "seq")
    everyone = ("seq", "dp")
    dp_index = lax.axis_index("dp")
    seq_index = lax.axis_index("seq")
    core = dp_index % 2
    odd = seq_index % 2
    features = activations.shape[2]
    quarter = activations.shape[1]
    vector_rows = vector_params.shape[0]
    straight, crossed = chip_routes(dp_count, seq_count)
    core_pairs = [(place, place ^ 1) for place in range(dp_count)]

    def to_chip(values):
        near = lax.dynamic_index_in_dim(values, odd, 0, keepdims=False)
        far = lax.dynamic_index_in_dim(values, 1 - odd, 0, keepdims=False)
        near = lax.ppermute(near, axes, straight)
        far = lax.ppermute(far, axes, crossed)
        return jnp.concatenate(
            [jnp.where(odd == 0, near, far), jnp.where(odd == 0, far, near)], axis=0
        )

    def from_chip(values):
        near = lax.dynamic_slice_in_dim(values, odd * quarter, quarter, 0)
        far = lax.dynamic_slice_in_dim(values, (1 - odd) * quarter, quarter, 0)
        near = lax.ppermute(near, axes, [(there, here) for here, there in straight])
        far = lax.ppermute(far, axes, [(there, here) for here, there in crossed])
        return jnp.stack([jnp.where(odd == 0, near, far), jnp.where(odd == 0, far, near)])

    def swap_cores(values):
        return lax.ppermute(values, "dp", core_pairs)

    def own_piece(weight):
        rows = weight.shape[0] // dp_count
        return lax.dynamic_slice_in_dim(weight, dp_index * rows, rows, 0).astype(low)

    def spread(piece):
        return lax.all_gather(piece, everyone, axis=0, tiled=True)

    vector_piece = jnp.pad(own_piece(vector_params.T), ((0, 0), (0, LANES - vector_rows)))
    first_low = spread(
        jnp.concatenate([own_piece(inputs_weight), own_piece(output_weight), vector_piece], axis=1)
    )
    expand_low = spread(own_piece(expand_weight))
    reduce_low = spread(own_piece(reduce_weight))
    wide = 3 * features
    inputs_low = first_low[:, :wide]
    output_low = first_low[:, wide : wide + features]
    vectors = first_low[:, wide + features : wide + features + vector_rows].T.astype(jnp.float32)

    residual_low = to_chip(activations)
    grad_top = to_chip(cotangent)
    rows_here = residual_low.shape[0]
    other_segments = swap_cores(segment_ids)
    segment_pair = jnp.where(seq_index // 2 == core, segment_ids, other_segments)
    segments = lax.dynamic_index_in_dim(segment_pair, odd, 0, keepdims=False)
    seg_row, seg_col = segments[None, :], segments[:, None]

    residual = residual_low.astype(jnp.float32)
    unit_one, inverse_one = normalize(residual)
    normed_one = (unit_one * vectors[0] + vectors[1]).astype(low)
    projected = dot_nn(normed_one, inputs_low)
    queries = (projected[:, :features] + vectors[4]).astype(low)
    keys = projected[:, features : 2 * features].astype(low)
    values = (projected[:, 2 * features :] + vectors[5]).astype(low)
    half = features // 2
    group_low = jnp.concatenate([queries[:, :half], keys[:, :half], values[:, :half]], axis=1)
    group_high = jnp.concatenate([queries[:, half:], keys[:, half:], values[:, half:]], axis=1)

    def join_tokens(mine, theirs):
        return jnp.where(
            core == 0,
            jnp.concatenate([mine, theirs], axis=0),
            jnp.concatenate([theirs, mine], axis=0),
        )

    def tokens_of(values, which):
        return lax.dynamic_slice_in_dim(values, which * rows_here, rows_here, 0)

    mine = jnp.where(core == 0, group_low, group_high)
    theirs = swap_cores(jnp.where(core == 0, group_high, group_low))
    projected_heads = join_tokens(mine, theirs)
    mixture_heads, logs_all = attend_forward(seg_row, seg_col, projected_heads)
    mixture_mine = tokens_of(mixture_heads, core)
    mixture_theirs = swap_cores(tokens_of(mixture_heads, 1 - core))
    mixture = jnp.where(
        core == 0,
        jnp.concatenate([mixture_mine, mixture_theirs], axis=1),
        jnp.concatenate([mixture_theirs, mixture_mine], axis=1),
    )

    middle = residual + (dot_nn(mixture, output_low) + vectors[6])
    unit_two, inverse_two = normalize(middle)
    normed_two = (unit_two * vectors[2] + vectors[3]).astype(low)
    reduced, grad_normed_two, grad_expand, grad_reduce, bias_sums = feed_both(
        normed_two, grad_top, expand_low, reduce_low, vectors[8:].reshape(1, -1)
    )
    layer_output = from_chip((middle + (reduced + vectors[7])).astype(low))
    expand_part = lax.psum_scatter(grad_expand, everyone, scatter_dimension=0, tiled=True)
    reduce_part = lax.psum_scatter(grad_reduce, everyone, scatter_dimension=0, tiled=True)

    grad_middle = grad_top.astype(jnp.float32) + norm_back(
        grad_normed_two, vectors[2], unit_two, inverse_two
    )
    grad_attended = grad_middle.astype(low)
    grad_output = dot_tn(mixture, grad_attended).astype(low)
    grad_mixture = dot_nt(grad_attended, output_low).astype(low)
    grad_mine = jnp.where(core == 0, grad_mixture[:, :half], grad_mixture[:, half:])
    grad_theirs = swap_cores(jnp.where(core == 0, grad_mixture[:, half:], grad_mixture[:, :half]))
    grad_heads = attend_backward(
        seg_row, seg_col, projected_heads, logs_all, join_tokens(grad_mine, grad_theirs)
    )
    grad_all = jnp.concatenate(grad_heads, axis=1)
    back_mine = tokens_of(grad_all, core)
    back_theirs = swap_cores(tokens_of(grad_all, 1 - core))
    back_low = jnp.where(core == 0, back_mine, back_theirs)
    back_high = jnp.where(core == 0, back_theirs, back_mine)
    grad_projected = jnp.concatenate(
        [
            part[:, start : start + half]
            for start in (0, half, 2 * half)
            for part in (back_low, back_high)
        ],
        axis=1,
    )
    grad_inputs = dot_tn(normed_one, grad_projected).astype(low)
    grad_normed_one = dot_nt(grad_projected, inputs_low)
    grad_residual = norm_back(grad_normed_one, vectors[0], unit_one, inverse_one)
    input_grad = from_chip((grad_middle + grad_residual).astype(low))

    head_rows = jnp.stack(
        [
            column_sum(grad_normed_one * unit_one),
            column_sum(grad_normed_one),
            column_sum(grad_normed_two * unit_two),
            column_sum(grad_normed_two),
            column_sum(grad_projected[:, :features]),
            column_sum(grad_projected[:, 2 * features :]),
            column_sum(grad_attended),
            column_sum(grad_top),
        ]
    )
    grad_vectors = jnp.concatenate([head_rows, bias_sums.reshape(-1, features)], axis=0)
    vector_columns = jnp.pad(grad_vectors.T.astype(low), ((0, 0), (0, LANES - vector_rows)))
    first_part = lax.psum_scatter(
        jnp.concatenate([grad_inputs, grad_output, vector_columns], axis=1),
        everyone,
        scatter_dimension=0,
        tiled=True,
    )

    def regather(part):
        return lax.all_gather(part, "dp", axis=0, tiled=True).astype(jnp.float32)

    sum_expand = regather(expand_part)
    sum_reduce = regather(reduce_part)
    sum_first = regather(first_part)
    sum_inputs = sum_first[:, :wide]
    sum_output = sum_first[:, wide : wide + features]
    sum_vectors = sum_first[:, wide + features : wide + features + vector_rows].T

    new_inputs = adamw_step(
        inputs_weight, inputs_moment, inputs_second, sum_inputs, 0.03, decay_rate
    )
    new_output = adamw_step(
        output_weight, output_moment, output_second, sum_output, 0.3, decay_rate
    )
    new_expand = adamw_step(
        expand_weight, expand_moment, expand_second, sum_expand, 0.03, decay_rate
    )
    new_reduce = adamw_step(
        reduce_weight, reduce_moment, reduce_second, sum_reduce, 0.02, decay_rate
    )
    new_vectors = adamw_step(vector_params, vector_moment, vector_second, sum_vectors, 0.5, 0.0)
    return (
        layer_output,
        input_grad,
        *new_inputs,
        *new_output,
        *new_expand,
        *new_reduce,
        *new_vectors,
    )


def solution(mesh):
    tokens = P("dp", "seq", None)
    rows = P("seq", None)
    columns = P(None, "seq")
    in_specs = (tokens, tokens, P("dp", None)) + (rows,) * 12 + (columns,) * 3
    out_specs = (tokens, tokens) + (rows,) * 12 + (columns,) * 3
    return jax.shard_map(
        partial(on_device, mesh.shape["dp"], mesh.shape["seq"]),
        mesh=mesh,
        in_specs=in_specs,
        out_specs=out_specs,
        check_vma=False,
    )
```

```python
from functools import partial

import jax
import jax.numpy as jnp
from jax import lax
from jax.experimental import pallas as pl
from jax.experimental.pallas import tpu as pltpu
from jax.sharding import PartitionSpec as P

HEADS = 12
HD = 64
STEP = 10
PAIR = 2 * HD
LANES = 128

eps_norm = 1e-05
eps_adam = 1e-08
beta_one = 0.9
beta_two = 0.95
decay_rate = 0.1
mask_fill = -1e30
vmem_bytes = 56 * 1024 * 1024

VISIBLE = (
    (0, 256, 0, 256),
    (256, 256, 128, 512),
    (512, 256, 128, 768),
    (768, 128, 128, 896),
    (896, 128, 768, 1024),
)
TILE_STARTS = []
tile_total = 0
for _first, _rows, _low, _high in VISIBLE:
    TILE_STARTS.append(tile_total)
    tile_total += _high - _low

low = jnp.bfloat16


def dot_nn(left_side, right_side):
    return lax.dot_general(
        left_side, right_side, (((1,), (0,)), ((), ())), preferred_element_type=jnp.float32
    )


def dot_tn(left_side, right_side):
    return lax.dot_general(
        left_side, right_side, (((0,), (0,)), ((), ())), preferred_element_type=jnp.float32
    )


def dot_nt(left_side, right_side):
    return lax.dot_general(
        left_side, right_side, (((1,), (1,)), ((), ())), preferred_element_type=jnp.float32
    )


def normalize(values):
    center = jnp.mean(values, axis=-1, keepdims=True)
    offsets = values - center
    spread = jnp.mean(offsets * offsets, axis=-1, keepdims=True)
    inverse = lax.rsqrt(spread + eps_norm)
    return offsets * inverse, inverse


def norm_back(grad_normed, gain, unit, inverse):
    scaled = grad_normed * gain
    mean_scaled = jnp.mean(scaled, axis=-1, keepdims=True)
    mean_cross = jnp.mean(scaled * unit, axis=-1, keepdims=True)
    return inverse * (scaled - mean_scaled - unit * mean_cross)


def adamw_step(weight, moment, second, gradient, step_rate, weight_decay):
    moment_new = beta_one * moment + (1.0 - beta_one) * gradient
    second_new = beta_two * second + (1.0 - beta_two) * gradient * gradient
    fix_one = 1.0 - beta_one**STEP
    fix_two = 1.0 - beta_two**STEP
    update = moment_new / fix_one / (jnp.sqrt(second_new / fix_two) + eps_adam)
    return (weight - step_rate * (update + weight_decay * weight), moment_new, second_new)


def column_sum(values):
    return jnp.sum(values.astype(jnp.float32), axis=0)


def fill_bias(seg_row, seg_col, bias):
    for (first, rows, key_low, key_high), start in zip(VISIBLE, TILE_STARTS):
        keys = key_high - key_low
        key_places = key_low + lax.broadcasted_iota(jnp.int32, (keys, rows), 0)
        query_places = first + lax.broadcasted_iota(jnp.int32, (keys, rows), 1)
        same = seg_col[key_low:key_high, :] == seg_row[:, first : first + rows]
        allowed = same & (key_places <= query_places)
        bias[start : start + keys, 0:rows] = jnp.where(allowed, 0.0, mask_fill)


def lane_masks(shape):
    lane = lax.broadcasted_iota(jnp.int32, shape, 1)
    return (lane < HD, lane >= HD)


def masked_to(values, mask):
    return jnp.where(mask, values, jnp.zeros_like(values))


def attend_forward_kernel(seg_row, seg_col, q_ref, k_ref, v_ref, out_ref, log_ref, bias):
    @pl.when(pl.program_id(0) == 0)
    def _():
        fill_bias(seg_row, seg_col, bias)

    masks = lane_masks((k_ref.shape[0], PAIR))
    keys_masked = [masked_to(k_ref[...], mask) for mask in masks]
    for (first, rows, key_low, key_high), start in zip(VISIBLE, TILE_STARTS):
        queries = q_ref[first : first + rows, :] * jnp.asarray(HD**-0.5, low)
        values = v_ref[key_low:key_high, :]
        mixed = []
        for head in range(2):
            scores = dot_nt(keys_masked[head][key_low:key_high], queries)
            scores = scores + bias[start : start + key_high - key_low, 0:rows]
            highest = jnp.max(scores, axis=0, keepdims=True)
            exponent = jnp.exp(scores - highest)
            totals = jnp.sum(exponent, axis=0, keepdims=True)
            soft = (exponent * (1.0 / totals)).astype(low)
            mixed.append(dot_tn(soft, values))
            log_ref[0, head : head + 1, first : first + rows] = highest + jnp.log(totals)
        half = lane_masks((rows, PAIR))[0]
        out_ref[first : first + rows, :] = jnp.where(half, mixed[0], mixed[1]).astype(low)


def attend_backward_kernel(
    seg_row, seg_col, q_ref, k_ref, v_ref, log_ref, do_ref, dq_ref, dk_ref, dv_ref, bias, dk_acc, dv_acc
):
    @pl.when(pl.program_id(0) == 0)
    def _():
        fill_bias(seg_row, seg_col, bias)

    masks = lane_masks((k_ref.shape[0], PAIR))
    keys_masked = [masked_to(k_ref[...], mask) for mask in masks]
    values_masked = [masked_to(v_ref[...], mask) for mask in masks]
    dk_acc[...] = jnp.zeros_like(dk_acc)
    dv_acc[...] = jnp.zeros_like(dv_acc)
    for (first, rows, key_low, key_high), start in zip(VISIBLE, TILE_STARTS):
        queries = q_ref[first : first + rows, :] * jnp.asarray(HD**-0.5, low)
        grads = do_ref[first : first + rows, :]
        grad_query = jnp.zeros((rows, PAIR), jnp.float32)
        row_masks = lane_masks((rows, PAIR))
        for head in range(2):
            keys = keys_masked[head][key_low:key_high]
            scores = dot_nt(keys, queries)
            scores = scores + bias[start : start + key_high - key_low, 0:rows]
            soft = jnp.exp(scores - log_ref[0, head : head + 1, first : first + rows])
            grad_soft = dot_nt(values_masked[head][key_low:key_high], grads)
            inner = jnp.sum(soft * grad_soft, axis=0, keepdims=True)
            grad_scores = (soft * (grad_soft - inner)).astype(low)
            dv_acc[key_low:key_high, :] += dot_nn(
                soft.astype(low), masked_to(grads, row_masks[head])
            )
            dk_acc[key_low:key_high, :] += dot_nn(
                grad_scores, masked_to(queries, row_masks[head])
            )
            grad_query = grad_query + dot_tn(grad_scores, keys)
        dq_ref[first : first + rows, :] = (grad_query * HD**-0.5).astype(low)
    dk_ref[...] = dk_acc[...].astype(low)
    dv_ref[...] = dv_acc[...].astype(low)


def attend_specs(length, pairs):
    whole = lambda shape: pl.BlockSpec(shape, lambda j: (0,) * len(shape))
    columns = lambda offset: pl.BlockSpec((length, PAIR), lambda j, offset=offset: (0, offset + j))
    logs = pl.BlockSpec((1, 8, length), lambda j: (j, 0, 0))
    return whole, columns, logs


def attend_forward(seg_row, seg_col, projected):
    length = projected.shape[0]
    pairs = projected.shape[1] // (3 * PAIR)
    whole, columns, logs = attend_specs(length, pairs)
    return pl.pallas_call(
        attend_forward_kernel,
        grid=(pairs,),
        in_specs=[
            whole((1, length)),
            whole((length, 1)),
            columns(0),
            columns(pairs),
            columns(2 * pairs),
        ],
        out_specs=[columns(0), logs],
        out_shape=[
            jax.ShapeDtypeStruct((length, pairs * PAIR), low),
            jax.ShapeDtypeStruct((pairs, 8, length), jnp.float32),
        ],
        scratch_shapes=[pltpu.VMEM((tile_total, 256), jnp.float32)],
        compiler_params=pltpu.CompilerParams(vmem_limit_bytes=vmem_bytes),
        cost_estimate=pl.CostEstimate(
            flops=4 * length * length * pairs * PAIR, bytes_accessed=8 * length * pairs * PAIR,
            transcendentals=length * length * pairs,
        ),
        name="attend_forward",
    )(seg_row, seg_col, projected, projected, projected)


def attend_backward(seg_row, seg_col, projected, logs_all, grad_mixture):
    length = projected.shape[0]
    pairs = projected.shape[1] // (3 * PAIR)
    whole, columns, logs = attend_specs(length, pairs)
    return pl.pallas_call(
        attend_backward_kernel,
        grid=(pairs,),
        in_specs=[
            whole((1, length)),
            whole((length, 1)),
            columns(0),
            columns(pairs),
            columns(2 * pairs),
            logs,
            columns(0),
        ],
        out_specs=[columns(0)] * 3,
        out_shape=[jax.ShapeDtypeStruct((length, pairs * PAIR), low)] * 3,
        scratch_shapes=[
            pltpu.VMEM((tile_total, 256), jnp.float32),
            pltpu.VMEM((length, PAIR), jnp.float32),
            pltpu.VMEM((length, PAIR), jnp.float32),
        ],
        compiler_params=pltpu.CompilerParams(vmem_limit_bytes=vmem_bytes),
        cost_estimate=pl.CostEstimate(
            flops=10 * length * length * pairs * PAIR, bytes_accessed=14 * length * pairs * PAIR,
            transcendentals=length * length * pairs,
        ),
        name="attend_backward",
    )(seg_row, seg_col, projected, projected, projected, logs_all, grad_mixture)


def feed_kernel(block_parts, has_sums, *refs):
    refs = list(refs)
    take = lambda count: [refs.pop(0) for _ in range(count)]
    normed = [ref[...] for ref in take(2)]
    tops = [ref[...] for ref in take(2)]
    blocks = [(take(parts), take(parts), take(1)[0]) for parts in block_parts]
    earlier = take(4) if has_sums else None
    reduced = take(2)
    grad_normed = take(2)
    outs = [(take(2), take(2), take(1)[0]) for _ in block_parts]
    turned = take(1)[0]
    rows = normed[0].shape[0]
    for side in range(2):
        turned[:, side * rows : (side + 1) * rows] = normed[side].T
        if has_sums:
            reduced[side][...] = earlier[side][...]
            grad_normed[side][...] = earlier[2 + side][...]
    for index, ((wu_parts, wd_parts, bias), (gu_refs, gd_refs, dbu_ref)) in enumerate(
        zip(blocks, outs)
    ):
        expand = jnp.concatenate([ref[...] for ref in wu_parts], axis=0)
        reduce = jnp.concatenate([ref[...] for ref in wd_parts], axis=0)
        hiddens, grads = [], []
        for side in range(2):
            expanded = dot_nn(normed[side], expand) + bias[...]
            phi = 0.5 + 0.5 * lax.erf(expanded * (0.5**0.5))
            density = jnp.exp(-0.5 * expanded * expanded) * 0.3989422804014327
            hidden = (expanded * phi).astype(low)
            slope = phi + expanded * density
            grad_low = (dot_nt(tops[side], reduce) * slope).astype(low)
            down = dot_nn(hidden, reduce)
            back = dot_nt(grad_low, expand)
            if has_sums or index:
                reduced[side][...] += down
                grad_normed[side][...] += back
            else:
                reduced[side][...] = down
                grad_normed[side][...] = back
            hiddens.append(hidden)
            grads.append(grad_low)
        grad_both = jnp.concatenate(grads, axis=0)
        half = gu_refs[0].shape[0]
        for part in range(2):
            gu_refs[part][...] = dot_nn(
                turned[part * half : (part + 1) * half, :], grad_both
            ).astype(low)
        grad_reduce = sum(dot_tn(hiddens[side], tops[side]) for side in range(2)).astype(low)
        half = gd_refs[0].shape[0]
        for part in range(2):
            gd_refs[part][...] = grad_reduce[part * half : (part + 1) * half]
        dbu_ref[...] = jnp.sum(grad_both.astype(jnp.float32), axis=0, keepdims=True)


def feed_blocks(normed, tops, blocks, sums):
    rows, features = normed[0].shape
    units = blocks[0][1][0].shape[-2] * len(blocks[0][1])
    operands = [*normed, *tops]
    for wu_parts, wd_parts, bias in blocks:
        operands += [*wu_parts, *wd_parts, bias]
    sum_shape = jax.ShapeDtypeStruct((rows, features), jnp.float32)
    shapes = [sum_shape] * 4
    for _ in blocks:
        shapes += [jax.ShapeDtypeStruct((features // 2, units), low)] * 2
        shapes += [jax.ShapeDtypeStruct((units // 2, features), low)] * 2
        shapes += [jax.ShapeDtypeStruct((1, units), jnp.float32)]
    if sums is not None:
        operands += list(sums)
    in_vmem = pl.BlockSpec(memory_space=pltpu.VMEM)
    results = pl.pallas_call(
        partial(feed_kernel, [len(block[0]) for block in blocks], sums is not None),
        in_specs=[in_vmem] * len(operands),
        out_specs=[in_vmem] * len(shapes),
        out_shape=shapes,
        scratch_shapes=[pltpu.VMEM((features, 2 * rows), low)],
        compiler_params=pltpu.CompilerParams(vmem_limit_bytes=vmem_bytes),
        cost_estimate=pl.CostEstimate(
            flops=24 * rows * features * units * len(blocks),
            bytes_accessed=8 * features * units * len(blocks),
            transcendentals=4 * rows * units * len(blocks),
        ),
        name="feed_blocks",
    )(*operands)
    grads = [results[4 + 5 * index : 9 + 5 * index] for index in range(len(blocks))]
    return results[:4], grads


def chip_routes(dp_count, seq_count):
    straight, crossed = [], []
    for place in range(dp_count):
        group, core = place - place % 2, place % 2
        for quarter in range(seq_count):
            source = place * seq_count + quarter
            holder = (group + quarter // 2) * seq_count
            straight.append((source, holder + 2 * core + quarter % 2))
            crossed.append((source, holder + 2 * core + 1 - quarter % 2))
    return straight, crossed


def on_device(
    dp_count,
    seq_count,
    activations,
    cotangent,
    segment_ids,
    inputs_weight,
    inputs_moment,
    inputs_second,
    output_weight,
    output_moment,
    output_second,
    expand_weight,
    expand_moment,
    expand_second,
    reduce_weight,
    reduce_moment,
    reduce_second,
    vector_params,
    vector_moment,
    vector_second,
):
    axes = ("dp", "seq")
    dp_index = lax.axis_index("dp")
    seq_index = lax.axis_index("seq")
    core = dp_index % 2
    group = dp_index // 2
    groups = dp_count // 2
    four_chips = groups == 4
    odd = seq_index % 2
    features = activations.shape[2]
    quarter = activations.shape[1]
    half = features // 2
    owned = inputs_weight.shape[0]
    owned_units = reduce_weight.shape[0]
    rows_piece = owned // groups
    units_piece = owned_units // dp_count
    vector_rows = vector_params.shape[0]
    straight, crossed = chip_routes(dp_count, seq_count)
    core_pairs = [(place, place ^ 1) for place in range(dp_count)]
    x_pairs = [(place, place ^ 2) for place in range(dp_count)]
    y_pairs = [(place, place ^ 4) for place in range(dp_count)]
    far_pairs = [(place, place ^ 6) for place in range(dp_count)]
    same_core = [list(range(first, dp_count, 2)) for first in range(2)]

    def to_chip(values):
        near = lax.dynamic_index_in_dim(values, odd, 0, keepdims=False)
        far = lax.dynamic_index_in_dim(values, 1 - odd, 0, keepdims=False)
        near = lax.ppermute(near, axes, straight)
        far = lax.ppermute(far, axes, crossed)
        return jnp.concatenate(
            [jnp.where(odd == 0, near, far), jnp.where(odd == 0, far, near)], axis=0
        )

    def from_chip(values):
        near = lax.dynamic_slice_in_dim(values, odd * quarter, quarter, 0)
        far = lax.dynamic_slice_in_dim(values, (1 - odd) * quarter, quarter, 0)
        near = lax.ppermute(near, axes, [(there, here) for here, there in straight])
        far = lax.ppermute(far, axes, [(there, here) for here, there in crossed])
        return jnp.stack([jnp.where(odd == 0, near, far), jnp.where(odd == 0, far, near)])

    def swap_cores(values):
        return lax.ppermute(values, "dp", core_pairs)

    def via_x(values):
        return lax.ppermute(values, "dp", x_pairs)

    def via_y(values):
        return lax.ppermute(values, "dp", y_pairs)

    def by_core(mine, theirs, axis):
        return jnp.where(
            core == 0,
            jnp.concatenate([mine, theirs], axis=axis),
            jnp.concatenate([theirs, mine], axis=axis),
        )

    def add_low(*terms):
        return sum(term.astype(jnp.float32) for term in terms).astype(low)

    def gather_z(piece):
        return lax.all_gather(piece, "seq", axis=0, tiled=False)

    def gather_chips(block):
        middle = block.shape[0] // 2
        from_x = via_x(block)
        from_y = via_y(block)
        return block, from_x, from_y, via_y(from_x[:middle]), via_x(from_y[middle:])

    def in_order(own, from_x, from_y, from_far, axis):
        x_set = group % 2 == 1
        y_set = group // 2 == 1
        near_low = jnp.where(x_set, from_x, own)
        near_high = jnp.where(x_set, own, from_x)
        far_low = jnp.where(x_set, from_far, from_y)
        far_high = jnp.where(x_set, from_y, from_far)
        return jnp.stack(
            [
                jnp.where(y_set, far_low, near_low),
                jnp.where(y_set, far_high, near_high),
                jnp.where(y_set, near_low, far_low),
                jnp.where(y_set, near_high, far_high),
            ],
            axis=axis,
        )

    def scatter_chips(own, to_x, to_y, to_far):
        y_first = add_low(to_y[0], via_x(to_far[0]))
        x_second = add_low(to_x[1], via_y(to_far[1]))
        x_first, y_second = via_x(to_x[0]), via_y(to_y[1])
        first = add_low(own[0], x_first, via_y(y_first))
        second = add_low(own[1], via_x(x_second), y_second)
        return jnp.concatenate([first, second], axis=0)

    def scatter_z(blocks):
        total = lax.dynamic_index_in_dim(blocks, seq_index, 0, keepdims=False)
        total = total.astype(jnp.float32)
        for shift in range(1, seq_count):
            target = (seq_index + shift) % seq_count
            sent = lax.dynamic_index_in_dim(blocks, target, 0, keepdims=False)
            ring = [(place, (place + shift) % seq_count) for place in range(seq_count)]
            total = total + lax.ppermute(sent, "seq", ring).astype(jnp.float32)
        return total.astype(low)

    def regather(piece):
        if not four_chips:
            every = lax.all_gather(piece, "dp", axis=0, tiled=False)
            return every.reshape((groups, 2) + piece.shape)
        from_far = lax.ppermute(piece, "dp", far_pairs)
        mine = in_order(piece, via_x(piece), via_y(piece), from_far, 0)
        return by_core(mine[:, None], swap_cores(mine)[:, None], 1)

    def corner(weight, column):
        return lax.dynamic_slice(
            weight, (group * rows_piece, column + core * half), (rows_piece, half)
        ).astype(low)

    vector_piece = lax.dynamic_slice_in_dim(vector_params, group * rows_piece, rows_piece, 1)
    first_piece = jnp.concatenate(
        [
            corner(inputs_weight, 0),
            corner(inputs_weight, features),
            corner(inputs_weight, 2 * features),
            corner(output_weight, 0),
            jnp.pad(vector_piece.T.astype(low), ((0, 0), (0, LANES - vector_rows))),
        ],
        axis=1,
    )
    expand_piece = jnp.concatenate(
        [
            lax.dynamic_slice_in_dim(
                expand_weight, owner * owned_units + dp_index * units_piece, units_piece, 1
            ).astype(low)
            for owner in range(seq_count)
        ],
        axis=1,
    )
    reduce_piece = lax.dynamic_slice_in_dim(
        reduce_weight, dp_index * units_piece, units_piece, 0
    ).astype(low)

    residual_low = to_chip(activations)
    first_block = gather_z(first_piece)
    expand_block = gather_z(expand_piece)
    reduce_block = gather_z(reduce_piece)
    grad_top = to_chip(cotangent)
    rows_here = residual_low.shape[0]
    residual_other = swap_cores(residual_low)
    grad_top_other = swap_cores(grad_top)
    other_segments = swap_cores(segment_ids)
    segment_pair = jnp.where(seq_index // 2 == core, segment_ids, other_segments)
    segments = lax.dynamic_index_in_dim(segment_pair, odd, 0, keepdims=False)
    seg_row, seg_col = segments[None, :], segments[:, None]

    if four_chips:
        own, from_x, from_y, far_first, far_second = gather_chips(first_block)
        from_far = jnp.concatenate([far_first, far_second], axis=0)
        first_low = in_order(own, from_x, from_y, from_far, 1)
    else:
        first_low = lax.all_gather(
            first_block, "dp", axis=1, tiled=False, axis_index_groups=same_core
        )
    first_low = first_low.reshape(features, first_low.shape[-1])
    wide = 3 * half
    inputs_low = first_low[:, :wide]
    output_half = first_low[:, wide : wide + half]
    output_low = by_core(output_half, swap_cores(output_half), 1)
    vectors = first_low[:, wide + half : wide + half + vector_rows].T.astype(jnp.float32)

    expand_bias = vectors[8:].reshape(seq_count, dp_count, units_piece)
    block_units = seq_count * owned_units // 8
    if four_chips:
        expand_parts = gather_chips(expand_block.reshape(features, block_units))
        reduce_parts = gather_chips(reduce_block.reshape(block_units, features))
        blocks = []
        for offset in range(4):
            place = dp_index ^ (2 * offset)
            bias = lax.dynamic_index_in_dim(expand_bias, place, 1, keepdims=False)
            picked = slice(offset, offset + 1) if offset < 3 else slice(3, 5)
            blocks.append(
                (expand_parts[picked], reduce_parts[picked], bias.reshape(1, block_units))
            )
    else:
        expand_all = lax.all_gather(
            expand_block.reshape(features, -1), "dp", axis=1, axis_index_groups=same_core
        ).reshape(features, 4, block_units)
        reduce_all = lax.all_gather(
            reduce_block.reshape(-1, features), "dp", axis=0, axis_index_groups=same_core
        ).reshape(4, block_units, features)
        picked = lax.dynamic_index_in_dim(
            expand_bias.reshape(seq_count, groups, 2, units_piece), core, 2, keepdims=False
        )
        bias_all = picked.transpose(1, 0, 2).reshape(4, 1, block_units)
        blocks = [
            ((expand_all[:, index],), (reduce_all[index],), bias_all[index]) for index in range(4)
        ]

    def tokens_of(values, which):
        return lax.dynamic_slice_in_dim(values, which * rows_here, rows_here, 0)

    def heads_part(vector):
        return lax.dynamic_slice_in_dim(vector, core * half, half, 0)

    unit_all, _ = normalize(by_core(residual_low, residual_other, 0).astype(jnp.float32))
    normed_one = (unit_all * vectors[0] + vectors[1]).astype(low)
    input_bias = jnp.concatenate(
        [heads_part(vectors[4]), jnp.zeros((half,), jnp.float32), heads_part(vectors[5])]
    )
    projected = (dot_nn(normed_one, inputs_low) + input_bias).astype(low)
    mixture_heads, logs_all = attend_forward(seg_row, seg_col, projected)
    mixture_theirs = swap_cores(tokens_of(mixture_heads, 1 - core))
    mixture = by_core(tokens_of(mixture_heads, core), mixture_theirs, 1)

    residual = residual_low.astype(jnp.float32)
    middle = residual + (dot_nn(mixture, output_low) + vectors[6])
    unit_two, inverse_two = normalize(middle)
    normed_two = (unit_two * vectors[2] + vectors[3]).astype(low)
    normed_pair = (normed_two, swap_cores(normed_two))
    top_pair = (grad_top, grad_top_other)
    sums, grads = feed_blocks(normed_pair, top_pair, blocks[:3], None)
    sums, last_grads = feed_blocks(normed_pair, top_pair, blocks[3:], sums)
    grads = grads + last_grads
    reduced = sums[0] + swap_cores(sums[1])
    grad_normed_two = sums[2] + swap_cores(sums[3])
    layer_output = from_chip((middle + (reduced + vectors[7])).astype(low))

    if four_chips:
        expand_sum = scatter_chips(*[(grad[0], grad[1]) for grad in grads])
        reduce_sum = scatter_chips(*[(grad[2], grad[3]) for grad in grads])
        place = jnp.arange(dp_count)[None, :, None]
        bias_sums = sum(
            jnp.where(
                place == (dp_index ^ (2 * offset)),
                grads[offset][4].reshape(seq_count, 1, units_piece),
                0.0,
            )
            for offset in range(4)
        )
    else:
        expand_sum = jnp.concatenate(
            [jnp.concatenate([grad[0], grad[1]], axis=0) for grad in grads], axis=1
        )
        expand_sum = expand_sum.reshape(features, groups, -1).transpose(1, 0, 2)
        expand_sum = lax.psum_scatter(expand_sum, "dp", axis_index_groups=same_core)
        reduce_sum = jnp.concatenate([part for grad in grads for part in grad[2:4]], axis=0)
        reduce_sum = reduce_sum.reshape(groups, -1, features)
        reduce_sum = lax.psum_scatter(reduce_sum, "dp", axis_index_groups=same_core)
        bias_sums = jnp.concatenate([grad[4] for grad in grads], axis=1)
        bias_sums = bias_sums.reshape(groups, seq_count, units_piece).transpose(1, 0, 2)
        is_core = jnp.arange(2)[None, None, :, None] == core
        bias_sums = jnp.where(is_core, bias_sums[:, :, None, :], 0.0)
    sum_expand = regather(scatter_z(expand_sum.reshape(seq_count, owned, -1)))
    sum_reduce = regather(scatter_z(reduce_sum.reshape(seq_count, units_piece, features)))
    sum_expand = sum_expand.reshape(dp_count, owned, seq_count, units_piece)
    sum_expand = sum_expand.transpose(1, 2, 0, 3).reshape(expand_weight.shape)
    sum_reduce = sum_reduce.reshape(reduce_weight.shape)

    grad_middle = grad_top.astype(jnp.float32) + norm_back(
        grad_normed_two, vectors[2], unit_two, inverse_two
    )
    grad_attended = grad_middle.astype(low)
    grad_output = dot_tn(mixture, grad_attended).astype(low)
    grad_mixture = dot_nt(grad_attended, output_low).astype(low)

    def columns_of(values, which):
        return lax.dynamic_slice_in_dim(values, which * half, half, 1)

    grad_theirs = swap_cores(columns_of(grad_mixture, 1 - core))
    grad_heads = attend_backward(
        seg_row,
        seg_col,
        projected,
        logs_all,
        by_core(columns_of(grad_mixture, core), grad_theirs, 0),
    )
    output_sum = add_low(
        columns_of(grad_output, core), swap_cores(columns_of(grad_output, 1 - core))
    )
    grad_projected = jnp.concatenate(grad_heads, axis=1)
    grad_inputs = dot_tn(normed_one, grad_projected).astype(low)
    grad_normed_all = dot_nt(grad_projected, inputs_low)
    grad_normed_one = tokens_of(grad_normed_all, core) + swap_cores(
        tokens_of(grad_normed_all, 1 - core)
    )
    unit_one, inverse_one = normalize(residual)
    grad_residual = norm_back(grad_normed_one, vectors[0], unit_one, inverse_one)
    input_grad = from_chip((grad_middle + grad_residual).astype(low))

    def heads_sum(values):
        return lax.dynamic_update_slice_in_dim(
            jnp.zeros((features,), jnp.float32), column_sum(values), core * half, 0
        )

    head_rows = jnp.stack(
        [
            column_sum(grad_normed_one * unit_one),
            column_sum(grad_normed_one),
            column_sum(grad_normed_two * unit_two),
            column_sum(grad_normed_two),
            heads_sum(grad_heads[0]),
            heads_sum(grad_heads[2]),
            column_sum(grad_attended),
            column_sum(grad_top),
        ]
    )
    grad_vectors = jnp.concatenate([head_rows, bias_sums.reshape(-1, features)], axis=0)
    vector_columns = jnp.pad(grad_vectors.T.astype(low), ((0, 0), (0, LANES - vector_rows)))
    first_grad = jnp.concatenate([grad_inputs, output_sum, vector_columns], axis=1)
    first_grad = first_grad.reshape(seq_count, groups, rows_piece, -1)
    if four_chips:
        split = []
        for offset in range(4):
            block = lax.dynamic_index_in_dim(first_grad, group ^ offset, 1, keepdims=False)
            split.append((block[: seq_count // 2], block[seq_count // 2 :]))
        first_sum = scatter_chips(*split)
    else:
        first_sum = lax.psum_scatter(
            first_grad, "dp", scatter_dimension=1, axis_index_groups=same_core
        )
    sum_first = regather(scatter_z(first_sum)).transpose(0, 2, 1, 3)
    sum_inputs = sum_first[..., :wide].reshape(groups, rows_piece, 2, 3, half)
    sum_inputs = sum_inputs.transpose(0, 1, 3, 2, 4).reshape(inputs_weight.shape)
    sum_output = sum_first[..., wide : wide + half].reshape(output_weight.shape)
    sum_vectors = sum_first[..., wide + half : wide + half + vector_rows].astype(jnp.float32)
    sum_vectors = jnp.sum(sum_vectors, axis=2).reshape(owned, vector_rows).T

    def renew(weight, moment, second, gradient, step_rate, weight_decay):
        return adamw_step(
            weight, moment, second, gradient.astype(jnp.float32), step_rate, weight_decay
        )

    new_inputs = renew(inputs_weight, inputs_moment, inputs_second, sum_inputs, 0.03, decay_rate)
    new_output = renew(output_weight, output_moment, output_second, sum_output, 0.3, decay_rate)
    new_expand = renew(expand_weight, expand_moment, expand_second, sum_expand, 0.03, decay_rate)
    new_reduce = renew(reduce_weight, reduce_moment, reduce_second, sum_reduce, 0.02, decay_rate)
    new_vectors = renew(vector_params, vector_moment, vector_second, sum_vectors, 0.5, 0.0)
    return (
        layer_output,
        input_grad,
        *new_inputs,
        *new_output,
        *new_expand,
        *new_reduce,
        *new_vectors,
    )


def solution(mesh):
    tokens = P("dp", "seq", None)
    rows = P("seq", None)
    columns = P(None, "seq")
    in_specs = (tokens, tokens, P("dp", None)) + (rows,) * 12 + (columns,) * 3
    out_specs = (tokens, tokens) + (rows,) * 12 + (columns,) * 3
    return jax.shard_map(
        partial(on_device, mesh.shape["dp"], mesh.shape["seq"]),
        mesh=mesh,
        in_specs=in_specs,
        out_specs=out_specs,
        check_vma=False,
    )
```

```python
from functools import partial

import jax
import jax.numpy as jnp
from jax import lax
from jax.experimental import pallas as pl
from jax.experimental.pallas import tpu as pltpu
from jax.sharding import PartitionSpec as P

HEADS = 12
HD = 64
STEP = 10
PAIR = 2 * HD
LANES = 128

eps_norm = 1e-05
eps_adam = 1e-08
beta_one = 0.9
beta_two = 0.95
decay_rate = 0.1
mask_fill = -1e30
vmem_bytes = 56 * 1024 * 1024

VISIBLE = (
    (0, 256, 0, 256),
    (256, 256, 128, 512),
    (512, 256, 128, 768),
    (768, 128, 128, 896),
    (896, 128, 768, 1024),
)
TILE_STARTS = []
tile_total = 0
for _first, _rows, _low, _high in VISIBLE:
    TILE_STARTS.append(tile_total)
    tile_total += _high - _low

low = jnp.bfloat16


def dot_nn(left_side, right_side):
    return lax.dot_general(
        left_side, right_side, (((1,), (0,)), ((), ())), preferred_element_type=jnp.float32
    )


def dot_tn(left_side, right_side):
    return lax.dot_general(
        left_side, right_side, (((0,), (0,)), ((), ())), preferred_element_type=jnp.float32
    )


def dot_nt(left_side, right_side):
    return lax.dot_general(
        left_side, right_side, (((1,), (1,)), ((), ())), preferred_element_type=jnp.float32
    )


def normalize(values):
    center = jnp.mean(values, axis=-1, keepdims=True)
    offsets = values - center
    spread = jnp.mean(offsets * offsets, axis=-1, keepdims=True)
    inverse = lax.rsqrt(spread + eps_norm)
    return offsets * inverse, inverse


def norm_back(grad_normed, gain, unit, inverse):
    scaled = grad_normed * gain
    mean_scaled = jnp.mean(scaled, axis=-1, keepdims=True)
    mean_cross = jnp.mean(scaled * unit, axis=-1, keepdims=True)
    return inverse * (scaled - mean_scaled - unit * mean_cross)


def adamw_step(weight, moment, second, gradient, step_rate, weight_decay):
    moment_new = beta_one * moment + (1.0 - beta_one) * gradient
    second_new = beta_two * second + (1.0 - beta_two) * gradient * gradient
    fix_one = 1.0 - beta_one**STEP
    fix_two = 1.0 - beta_two**STEP
    update = moment_new / fix_one / (jnp.sqrt(second_new / fix_two) + eps_adam)
    return (weight - step_rate * (update + weight_decay * weight), moment_new, second_new)


def column_sum(values):
    return jnp.sum(values.astype(jnp.float32), axis=0)


def fill_bias(seg_row, seg_col, bias):
    for (first, rows, key_low, key_high), start in zip(VISIBLE, TILE_STARTS):
        keys = key_high - key_low
        key_places = key_low + lax.broadcasted_iota(jnp.int32, (keys, rows), 0)
        query_places = first + lax.broadcasted_iota(jnp.int32, (keys, rows), 1)
        same = seg_col[key_low:key_high, :] == seg_row[:, first : first + rows]
        allowed = same & (key_places <= query_places)
        bias[start : start + keys, 0:rows] = jnp.where(allowed, 0.0, mask_fill)


def lane_masks(shape):
    lane = lax.broadcasted_iota(jnp.int32, shape, 1)
    return (lane < HD, lane >= HD)


def masked_to(values, mask):
    return jnp.where(mask, values, jnp.zeros_like(values))


def attend_forward_kernel(seg_row, seg_col, q_ref, k_ref, v_ref, out_ref, log_ref, bias):
    @pl.when(pl.program_id(0) == 0)
    def _():
        fill_bias(seg_row, seg_col, bias)

    masks = lane_masks((k_ref.shape[0], PAIR))
    keys_masked = [masked_to(k_ref[...], mask) for mask in masks]
    for (first, rows, key_low, key_high), start in zip(VISIBLE, TILE_STARTS):
        queries = q_ref[first : first + rows, :] * jnp.asarray(HD**-0.5, low)
        values = v_ref[key_low:key_high, :]
        mixed = []
        for head in range(2):
            scores = dot_nt(keys_masked[head][key_low:key_high], queries)
            scores = scores + bias[start : start + key_high - key_low, 0:rows]
            highest = jnp.max(scores, axis=0, keepdims=True)
            exponent = jnp.exp(scores - highest)
            totals = jnp.sum(exponent, axis=0, keepdims=True)
            soft = (exponent * (1.0 / totals)).astype(low)
            mixed.append(dot_tn(soft, values))
            log_ref[0, head : head + 1, first : first + rows] = highest + jnp.log(totals)
        half = lane_masks((rows, PAIR))[0]
        out_ref[first : first + rows, :] = jnp.where(half, mixed[0], mixed[1]).astype(low)


def attend_backward_kernel(
    seg_row, seg_col, q_ref, k_ref, v_ref, log_ref, do_ref, dq_ref, dk_ref, dv_ref, bias, dk_acc, dv_acc
):
    @pl.when(pl.program_id(0) == 0)
    def _():
        fill_bias(seg_row, seg_col, bias)

    masks = lane_masks((k_ref.shape[0], PAIR))
    keys_masked = [masked_to(k_ref[...], mask) for mask in masks]
    values_masked = [masked_to(v_ref[...], mask) for mask in masks]
    dk_acc[...] = jnp.zeros_like(dk_acc)
    dv_acc[...] = jnp.zeros_like(dv_acc)
    for (first, rows, key_low, key_high), start in zip(VISIBLE, TILE_STARTS):
        queries = q_ref[first : first + rows, :] * jnp.asarray(HD**-0.5, low)
        grads = do_ref[first : first + rows, :]
        grad_query = jnp.zeros((rows, PAIR), jnp.float32)
        row_masks = lane_masks((rows, PAIR))
        for head in range(2):
            keys = keys_masked[head][key_low:key_high]
            scores = dot_nt(keys, queries)
            scores = scores + bias[start : start + key_high - key_low, 0:rows]
            soft = jnp.exp(scores - log_ref[0, head : head + 1, first : first + rows])
            grad_soft = dot_nt(values_masked[head][key_low:key_high], grads)
            inner = jnp.sum(soft * grad_soft, axis=0, keepdims=True)
            grad_scores = (soft * (grad_soft - inner)).astype(low)
            dv_acc[key_low:key_high, :] += dot_nn(
                soft.astype(low), masked_to(grads, row_masks[head])
            )
            dk_acc[key_low:key_high, :] += dot_nn(
                grad_scores, masked_to(queries, row_masks[head])
            )
            grad_query = grad_query + dot_tn(grad_scores, keys)
        dq_ref[first : first + rows, :] = (grad_query * HD**-0.5).astype(low)
    dk_ref[...] = dk_acc[...].astype(low)
    dv_ref[...] = dv_acc[...].astype(low)


def attend_specs(length, pairs):
    whole = lambda shape: pl.BlockSpec(shape, lambda j: (0,) * len(shape))
    columns = lambda offset: pl.BlockSpec((length, PAIR), lambda j, offset=offset: (0, offset + j))
    logs = pl.BlockSpec((1, 8, length), lambda j: (j, 0, 0))
    return whole, columns, logs


def attend_forward(seg_row, seg_col, projected):
    length = projected.shape[0]
    pairs = projected.shape[1] // (3 * PAIR)
    whole, columns, logs = attend_specs(length, pairs)
    return pl.pallas_call(
        attend_forward_kernel,
        grid=(pairs,),
        in_specs=[
            whole((1, length)),
            whole((length, 1)),
            columns(0),
            columns(pairs),
            columns(2 * pairs),
        ],
        out_specs=[columns(0), logs],
        out_shape=[
            jax.ShapeDtypeStruct((length, pairs * PAIR), low),
            jax.ShapeDtypeStruct((pairs, 8, length), jnp.float32),
        ],
        scratch_shapes=[pltpu.VMEM((tile_total, 256), jnp.float32)],
        compiler_params=pltpu.CompilerParams(vmem_limit_bytes=vmem_bytes),
        cost_estimate=pl.CostEstimate(
            flops=4 * length * length * pairs * PAIR, bytes_accessed=8 * length * pairs * PAIR,
            transcendentals=length * length * pairs,
        ),
        name="attend_forward",
    )(seg_row, seg_col, projected, projected, projected)


def attend_backward(seg_row, seg_col, projected, logs_all, grad_mixture):
    length = projected.shape[0]
    pairs = projected.shape[1] // (3 * PAIR)
    whole, columns, logs = attend_specs(length, pairs)
    return pl.pallas_call(
        attend_backward_kernel,
        grid=(pairs,),
        in_specs=[
            whole((1, length)),
            whole((length, 1)),
            columns(0),
            columns(pairs),
            columns(2 * pairs),
            logs,
            columns(0),
        ],
        out_specs=[columns(0)] * 3,
        out_shape=[jax.ShapeDtypeStruct((length, pairs * PAIR), low)] * 3,
        scratch_shapes=[
            pltpu.VMEM((tile_total, 256), jnp.float32),
            pltpu.VMEM((length, PAIR), jnp.float32),
            pltpu.VMEM((length, PAIR), jnp.float32),
        ],
        compiler_params=pltpu.CompilerParams(vmem_limit_bytes=vmem_bytes),
        cost_estimate=pl.CostEstimate(
            flops=10 * length * length * pairs * PAIR, bytes_accessed=14 * length * pairs * PAIR,
            transcendentals=length * length * pairs,
        ),
        name="attend_backward",
    )(seg_row, seg_col, projected, projected, projected, logs_all, grad_mixture)


def feed_kernel(block_count, has_sums, *refs):
    refs = list(refs)
    take = lambda count: [refs.pop(0) for _ in range(count)]
    normed = [ref[...] for ref in take(2)]
    tops = [ref[...] for ref in take(2)]
    blocks = [(take(2), take(1)[0]) for _ in range(block_count)]
    earlier = take(4) if has_sums else None
    reduced = take(2)
    grad_normed = take(2)
    outs = [(take(2), take(1)[0]) for _ in range(block_count)]
    turned = take(1)[0]
    rows = normed[0].shape[0]
    for side in range(2):
        turned[:, side * rows : (side + 1) * rows] = normed[side].T
        if has_sums:
            reduced[side][...] = earlier[side][...]
            grad_normed[side][...] = earlier[2 + side][...]
    for index, ((parts, bias), (grad_refs, dbu_ref)) in enumerate(zip(blocks, outs)):
        owners, depth, units = parts[0].shape
        split = depth - units // (2 * owners) * 2
        side_rows = units // (2 * owners)
        expand = jnp.concatenate(
            [part[owner, :split] for part in parts for owner in range(owners)], axis=0
        )
        reduce = jnp.concatenate(
            [
                jnp.concatenate(
                    [part[owner, split : split + side_rows], part[owner, split + side_rows :]],
                    axis=1,
                )
                for part in parts
                for owner in range(owners)
            ],
            axis=0,
        )
        hiddens, grads = [], []
        for side in range(2):
            expanded = dot_nn(normed[side], expand) + bias[...]
            phi = 0.5 + 0.5 * lax.erf(expanded * (0.5**0.5))
            density = jnp.exp(-0.5 * expanded * expanded) * 0.3989422804014327
            hidden = (expanded * phi).astype(low)
            slope = phi + expanded * density
            grad_low = (dot_nt(tops[side], reduce) * slope).astype(low)
            down = dot_nn(hidden, reduce)
            back = dot_nt(grad_low, expand)
            if has_sums or index:
                reduced[side][...] += down
                grad_normed[side][...] += back
            else:
                reduced[side][...] = down
                grad_normed[side][...] = back
            hiddens.append(hidden)
            grads.append(grad_low)
        grad_both = jnp.concatenate(grads, axis=0)
        grad_reduce = sum(dot_tn(hiddens[side], tops[side]) for side in range(2)).astype(low)
        for place in range(2 * owners):
            grad_ref, owner = grad_refs[place // owners], place % owners
            grad_ref[owner, :split] = dot_nn(
                turned[place * split : (place + 1) * split, :], grad_both
            ).astype(low)
            rows_down = grad_reduce[place * side_rows : (place + 1) * side_rows]
            grad_ref[owner, split : split + side_rows] = rows_down[:, :units]
            grad_ref[owner, split + side_rows :] = rows_down[:, units:]
        dbu_ref[...] = jnp.sum(grad_both.astype(jnp.float32), axis=0, keepdims=True)


def feed_blocks(normed, tops, blocks, sums):
    rows, features = normed[0].shape
    units = blocks[0][1].shape[1]
    operands = [*normed, *tops]
    for parts, bias in blocks:
        operands += [*parts, bias]
    sum_shape = jax.ShapeDtypeStruct((rows, features), jnp.float32)
    shapes = [sum_shape] * 4
    for parts, _ in blocks:
        shapes += [jax.ShapeDtypeStruct(part.shape, low) for part in parts]
        shapes += [jax.ShapeDtypeStruct((1, units), jnp.float32)]
    if sums is not None:
        operands += list(sums)
    in_vmem = pl.BlockSpec(memory_space=pltpu.VMEM)
    results = pl.pallas_call(
        partial(feed_kernel, len(blocks), sums is not None),
        in_specs=[in_vmem] * len(operands),
        out_specs=[in_vmem] * len(shapes),
        out_shape=shapes,
        scratch_shapes=[pltpu.VMEM((features, 2 * rows), low)],
        compiler_params=pltpu.CompilerParams(vmem_limit_bytes=vmem_bytes),
        cost_estimate=pl.CostEstimate(
            flops=24 * rows * features * units * len(blocks),
            bytes_accessed=8 * features * units * len(blocks),
            transcendentals=4 * rows * units * len(blocks),
        ),
        name="feed_blocks",
    )(*operands)
    grads = [results[4 + 3 * index : 7 + 3 * index] for index in range(len(blocks))]
    return results[:4], grads


def chip_routes(dp_count, seq_count):
    straight, crossed = [], []
    for place in range(dp_count):
        group, core = place - place % 2, place % 2
        for quarter in range(seq_count):
            source = place * seq_count + quarter
            holder = (group + quarter // 2) * seq_count
            straight.append((source, holder + 2 * core + quarter % 2))
            crossed.append((source, holder + 2 * core + 1 - quarter % 2))
    return straight, crossed


def on_device(
    dp_count,
    seq_count,
    activations,
    cotangent,
    segment_ids,
    inputs_weight,
    inputs_moment,
    inputs_second,
    output_weight,
    output_moment,
    output_second,
    expand_weight,
    expand_moment,
    expand_second,
    reduce_weight,
    reduce_moment,
    reduce_second,
    vector_params,
    vector_moment,
    vector_second,
):
    axes = ("dp", "seq")
    dp_index = lax.axis_index("dp")
    seq_index = lax.axis_index("seq")
    core = dp_index % 2
    group = dp_index // 2
    groups = dp_count // 2
    four_chips = groups == 4
    odd = seq_index % 2
    features = activations.shape[2]
    quarter = activations.shape[1]
    half = features // 2
    owned = inputs_weight.shape[0]
    owned_units = reduce_weight.shape[0]
    rows_piece = owned // groups
    units_piece = owned_units // dp_count
    vector_rows = vector_params.shape[0]
    straight, crossed = chip_routes(dp_count, seq_count)
    core_pairs = [(place, place ^ 1) for place in range(dp_count)]
    x_pairs = [(place, place ^ 2) for place in range(dp_count)]
    y_pairs = [(place, place ^ 4) for place in range(dp_count)]
    far_pairs = [(place, place ^ 6) for place in range(dp_count)]
    same_core = [list(range(first, dp_count, 2)) for first in range(2)]

    def to_chip(values):
        near = lax.dynamic_index_in_dim(values, odd, 0, keepdims=False)
        far = lax.dynamic_index_in_dim(values, 1 - odd, 0, keepdims=False)
        near = lax.ppermute(near, axes, straight)
        far = lax.ppermute(far, axes, crossed)
        return jnp.concatenate(
            [jnp.where(odd == 0, near, far), jnp.where(odd == 0, far, near)], axis=0
        )

    def from_chip(values):
        near = lax.dynamic_slice_in_dim(values, odd * quarter, quarter, 0)
        far = lax.dynamic_slice_in_dim(values, (1 - odd) * quarter, quarter, 0)
        near = lax.ppermute(near, axes, [(there, here) for here, there in straight])
        far = lax.ppermute(far, axes, [(there, here) for here, there in crossed])
        return jnp.stack([jnp.where(odd == 0, near, far), jnp.where(odd == 0, far, near)])

    def swap_cores(values):
        return lax.ppermute(values, "dp", core_pairs)

    def via_x(values):
        return lax.ppermute(values, "dp", x_pairs)

    def via_y(values):
        return lax.ppermute(values, "dp", y_pairs)

    def by_core(mine, theirs, axis):
        return jnp.where(
            core == 0,
            jnp.concatenate([mine, theirs], axis=axis),
            jnp.concatenate([theirs, mine], axis=axis),
        )

    def add_low(*terms):
        return sum(term.astype(jnp.float32) for term in terms).astype(low)

    def after(values, *gates):
        return lax.optimization_barrier((values, gates))[0]

    def gather_z(piece):
        parts = [piece]
        for shift in range(1, seq_count):
            ring = [(place, (place + shift) % seq_count) for place in range(seq_count)]
            parts.append(lax.ppermute(piece, "seq", ring))
        placed = [
            lax.select_n((seq_index - owner) % seq_count, *parts) for owner in range(seq_count)
        ]
        middle = seq_count // 2
        return jnp.stack(placed[:middle]), jnp.stack(placed[middle:])

    def gather_chips(halves):
        first, second = halves
        x_first, y_second = via_x(first), via_y(second)
        x_second, y_first = via_x(second), via_y(first)
        return halves, (x_first, x_second), (y_first, y_second), (via_y(x_first), via_x(y_second))

    def in_order(own, from_x, from_y, from_far, axis):
        x_set = group % 2 == 1
        y_set = group // 2 == 1
        near_low = jnp.where(x_set, from_x, own)
        near_high = jnp.where(x_set, own, from_x)
        far_low = jnp.where(x_set, from_far, from_y)
        far_high = jnp.where(x_set, from_y, from_far)
        return jnp.stack(
            [
                jnp.where(y_set, far_low, near_low),
                jnp.where(y_set, far_high, near_high),
                jnp.where(y_set, near_low, far_low),
                jnp.where(y_set, near_high, far_high),
            ],
            axis=axis,
        )

    def scatter_begin(own, to_x, to_y, to_far):
        far_first, far_second = via_x(to_far[0]), via_y(to_far[1])
        return (own, to_x, to_y, far_first, far_second, via_x(to_x[0]), via_y(to_y[1]))

    def scatter_middle(state, *gates):
        own, to_x, to_y, far_first, far_second, x_first, y_second = state
        far_first, far_second = after((far_first, far_second), *gates)
        y_first = add_low(to_y[0], far_first)
        x_second = add_low(to_x[1], far_second)
        return (own, x_first, via_x(x_second), via_y(y_first), y_second), (y_first, x_second)

    def scatter_end(state):
        own, x_first, x_second, y_first, y_second = state
        first = add_low(own[0], x_first, y_first)
        second = add_low(own[1], x_second, y_second)
        return jnp.concatenate([first, second], axis=0)

    def scatter_z_begin(blocks):
        parts = [lax.dynamic_index_in_dim(blocks, seq_index, 0, keepdims=False)]
        for shift in range(1, seq_count):
            target = (seq_index + shift) % seq_count
            sent = lax.dynamic_index_in_dim(blocks, target, 0, keepdims=False)
            ring = [(place, (place + shift) % seq_count) for place in range(seq_count)]
            parts.append(lax.ppermute(sent, "seq", ring))
        return parts

    def scatter_z(blocks):
        return add_low(*scatter_z_begin(blocks))

    def regather_begin(piece):
        return piece, via_x(piece), via_y(piece), lax.ppermute(piece, "dp", far_pairs)

    def regather_end(state):
        mine = in_order(*state, 0)
        return by_core(mine[:, None], swap_cores(mine)[:, None], 1)

    def regather(piece):
        every = lax.all_gather(piece, "dp", axis=0, tiled=False)
        return every.reshape((groups, 2) + piece.shape)

    def corner(weight, column):
        return lax.dynamic_slice(
            weight, (group * rows_piece, column + core * half), (rows_piece, half)
        ).astype(low)

    vector_piece = lax.dynamic_slice_in_dim(vector_params, group * rows_piece, rows_piece, 1)
    first_piece = jnp.concatenate(
        [
            corner(inputs_weight, 0),
            corner(inputs_weight, features),
            corner(inputs_weight, 2 * features),
            corner(output_weight, 0),
            jnp.pad(vector_piece.T.astype(low), ((0, 0), (0, LANES - vector_rows))),
        ],
        axis=1,
    )
    expand_piece = jnp.concatenate(
        [
            lax.dynamic_slice_in_dim(
                expand_weight, owner * owned_units + dp_index * units_piece, units_piece, 1
            ).astype(low)
            for owner in range(seq_count)
        ],
        axis=1,
    )
    reduce_piece = lax.dynamic_slice_in_dim(
        reduce_weight, dp_index * units_piece, units_piece, 0
    ).astype(low)

    def pack(expand, reduce):
        return jnp.concatenate([expand, reduce[..., :half], reduce[..., half:]], axis=-2)

    residual_low = to_chip(activations)
    first_block = gather_z(first_piece)
    grad_top = to_chip(cotangent)
    rows_here = residual_low.shape[0]
    residual_other = swap_cores(residual_low)
    grad_top_other = swap_cores(grad_top)
    other_segments = swap_cores(segment_ids)
    segment_pair = jnp.where(seq_index // 2 == core, segment_ids, other_segments)
    segments = lax.dynamic_index_in_dim(segment_pair, odd, 0, keepdims=False)
    seg_row, seg_col = segments[None, :], segments[:, None]

    if four_chips:
        every_first = gather_chips(first_block)
        first_low = jnp.concatenate(
            [in_order(*[block[part] for block in every_first], 1) for part in range(2)], axis=0
        )
    else:
        first_low = lax.all_gather(
            jnp.concatenate(first_block, axis=0),
            "dp",
            axis=1,
            tiled=False,
            axis_index_groups=same_core,
        )
    first_low = first_low.reshape(features, first_low.shape[-1])
    wide = 3 * half
    inputs_low = first_low[:, :wide]
    output_half = first_low[:, wide : wide + half]
    output_low = by_core(output_half, swap_cores(output_half), 1)
    vectors = first_low[:, wide + half : wide + half + vector_rows].T.astype(jnp.float32)

    expand_bias = vectors[8:].reshape(seq_count, dp_count, units_piece)
    block_units = seq_count * owned_units // 8
    if four_chips:
        blocks = []
        for offset, parts in enumerate(gather_chips(gather_z(pack(expand_piece, reduce_piece)))):
            place = dp_index ^ (2 * offset)
            bias = lax.dynamic_index_in_dim(expand_bias, place, 1, keepdims=False)
            blocks.append((parts, bias.reshape(1, block_units)))
    else:
        expand_all = lax.all_gather(
            jnp.concatenate(gather_z(expand_piece), axis=0).reshape(features, -1),
            "dp",
            axis=1,
            axis_index_groups=same_core,
        ).reshape(seq_count, owned, 4, block_units)
        reduce_all = lax.all_gather(
            jnp.concatenate(gather_z(reduce_piece), axis=0).reshape(-1, features),
            "dp",
            axis=0,
            axis_index_groups=same_core,
        ).reshape(4, seq_count, -1, features)
        picked = lax.dynamic_index_in_dim(
            expand_bias.reshape(seq_count, groups, 2, units_piece), core, 2, keepdims=False
        )
        bias_all = picked.transpose(1, 0, 2).reshape(4, 1, block_units)
        blocks = []
        for index in range(4):
            packed = pack(expand_all[:, :, index], reduce_all[index])
            blocks.append(
                ((packed[: seq_count // 2], packed[seq_count // 2 :]), bias_all[index])
            )

    def tokens_of(values, which):
        return lax.dynamic_slice_in_dim(values, which * rows_here, rows_here, 0)

    def heads_part(vector):
        return lax.dynamic_slice_in_dim(vector, core * half, half, 0)

    unit_all, _ = normalize(by_core(residual_low, residual_other, 0).astype(jnp.float32))
    normed_one = (unit_all * vectors[0] + vectors[1]).astype(low)
    input_bias = jnp.concatenate(
        [heads_part(vectors[4]), jnp.zeros((half,), jnp.float32), heads_part(vectors[5])]
    )
    projected = (dot_nn(normed_one, inputs_low) + input_bias).astype(low)
    mixture_heads, logs_all = attend_forward(seg_row, seg_col, projected)
    mixture_theirs = swap_cores(tokens_of(mixture_heads, 1 - core))
    mixture = by_core(tokens_of(mixture_heads, core), mixture_theirs, 1)

    residual = residual_low.astype(jnp.float32)
    middle = residual + (dot_nn(mixture, output_low) + vectors[6])
    unit_two, inverse_two = normalize(middle)
    normed_two = (unit_two * vectors[2] + vectors[3]).astype(low)
    normed_pair = (normed_two, swap_cores(normed_two))
    top_pair = (grad_top, grad_top_other)
    sums, grads = feed_blocks(normed_pair, top_pair, blocks[:3], None)
    sums, last_grads = feed_blocks(normed_pair, top_pair, blocks[3:], sums)
    grads = grads + last_grads
    reduced = sums[0] + swap_cores(sums[1])
    grad_normed_two = sums[2] + swap_cores(sums[3])
    layer_output = from_chip((middle + (reduced + vectors[7])).astype(low))

    if four_chips:
        feed_state = scatter_begin(*[grad[:2] for grad in grads])
        place = jnp.arange(dp_count)[None, :, None]
        bias_sums = sum(
            jnp.where(
                place == (dp_index ^ (2 * offset)),
                grads[offset][2].reshape(seq_count, 1, units_piece),
                0.0,
            )
            for offset in range(4)
        )
    else:
        packed = [jnp.concatenate(grad[:2], axis=0) for grad in grads]
        expand_sum = jnp.stack([part[:, :owned] for part in packed], axis=2)
        expand_sum = expand_sum.reshape(features, groups, -1).transpose(1, 0, 2)
        expand_sum = lax.psum_scatter(expand_sum, "dp", axis_index_groups=same_core)
        reduce_sum = [part[:, owned:].reshape(seq_count, 2, -1, half) for part in packed]
        reduce_sum = jnp.stack([part.transpose(0, 2, 1, 3) for part in reduce_sum])
        reduce_sum = reduce_sum.reshape(groups, -1, features)
        reduce_sum = lax.psum_scatter(reduce_sum, "dp", axis_index_groups=same_core)
        bias_sums = jnp.concatenate([grad[2] for grad in grads], axis=1)
        bias_sums = bias_sums.reshape(groups, seq_count, units_piece).transpose(1, 0, 2)
        is_core = jnp.arange(2)[None, None, :, None] == core
        bias_sums = jnp.where(is_core, bias_sums[:, :, None, :], 0.0)

    grad_middle = grad_top.astype(jnp.float32) + norm_back(
        grad_normed_two, vectors[2], unit_two, inverse_two
    )
    grad_attended = grad_middle.astype(low)
    grad_output = dot_tn(mixture, grad_attended).astype(low)
    grad_mixture = dot_nt(grad_attended, output_low).astype(low)

    def columns_of(values, which):
        return lax.dynamic_slice_in_dim(values, which * half, half, 1)

    grad_theirs = swap_cores(columns_of(grad_mixture, 1 - core))
    grad_joined = by_core(columns_of(grad_mixture, core), grad_theirs, 0)
    if four_chips:
        feed_state, gates = scatter_middle(feed_state, grad_mixture)
        grad_joined = after(grad_joined, *gates)
    grad_heads = attend_backward(seg_row, seg_col, projected, logs_all, grad_joined)
    output_sum = add_low(
        columns_of(grad_output, core), swap_cores(columns_of(grad_output, 1 - core))
    )
    grad_projected = jnp.concatenate(grad_heads, axis=1)
    grad_inputs = dot_tn(normed_one, grad_projected).astype(low)
    grad_normed_all = dot_nt(grad_projected, inputs_low)
    grad_normed_one = tokens_of(grad_normed_all, core) + swap_cores(
        tokens_of(grad_normed_all, 1 - core)
    )
    unit_one, inverse_one = normalize(residual)
    grad_residual = norm_back(grad_normed_one, vectors[0], unit_one, inverse_one)
    input_grad = from_chip((grad_middle + grad_residual).astype(low))

    def heads_sum(values):
        return lax.dynamic_update_slice_in_dim(
            jnp.zeros((features,), jnp.float32), column_sum(values), core * half, 0
        )

    head_rows = jnp.stack(
        [
            column_sum(grad_normed_one * unit_one),
            column_sum(grad_normed_one),
            column_sum(grad_normed_two * unit_two),
            column_sum(grad_normed_two),
            heads_sum(grad_heads[0]),
            heads_sum(grad_heads[2]),
            column_sum(grad_attended),
            column_sum(grad_top),
        ]
    )
    grad_vectors = jnp.concatenate([head_rows, bias_sums.reshape(-1, features)], axis=0)
    vector_columns = jnp.pad(grad_vectors.T.astype(low), ((0, 0), (0, LANES - vector_rows)))
    first_grad = jnp.concatenate([grad_inputs, output_sum, vector_columns], axis=1)
    first_grad = first_grad.reshape(seq_count, groups, rows_piece, -1)
    if four_chips:
        middle_owner = seq_count // 2
        split = []
        for offset in range(4):
            split.append(
                [
                    lax.dynamic_index_in_dim(part, group ^ offset, 1, keepdims=False)
                    for part in (first_grad[:middle_owner], first_grad[middle_owner:])
                ]
            )
        feed_parts = scatter_z_begin(scatter_end(after(feed_state, grad_normed_all, grad_inputs)))
        first_state = scatter_begin(*split)
        feed_parts = after(feed_parts, split)
        feed_state = regather_begin(add_low(*feed_parts))
        first_state, gates = scatter_middle(first_state, feed_state[0])
        feed_state = after(feed_state, *gates)
        every = regather_end(feed_state)
        first_parts = scatter_z_begin(scatter_end(first_state))
        sum_expand = every[:, :, :owned]
        sum_reduce = jnp.concatenate(
            [every[:, :, owned : owned + units_piece], every[:, :, owned + units_piece :]], axis=-1
        )
        every_first = regather_end(regather_begin(add_low(*first_parts)))
    else:
        first_sum = lax.psum_scatter(
            first_grad, "dp", scatter_dimension=1, axis_index_groups=same_core
        )
        every_first = regather(scatter_z(first_sum))
        sum_expand = regather(scatter_z(expand_sum.reshape(seq_count, owned, -1)))
        sum_reduce = regather(scatter_z(reduce_sum.reshape(seq_count, units_piece, features)))
    sum_expand = sum_expand.reshape(dp_count, owned, seq_count, units_piece)
    sum_expand = sum_expand.transpose(1, 2, 0, 3).reshape(expand_weight.shape)
    sum_reduce = sum_reduce.reshape(reduce_weight.shape)
    sum_first = every_first.transpose(0, 2, 1, 3)
    sum_inputs = sum_first[..., :wide].reshape(groups, rows_piece, 2, 3, half)
    sum_inputs = sum_inputs.transpose(0, 1, 3, 2, 4).reshape(inputs_weight.shape)
    sum_output = sum_first[..., wide : wide + half].reshape(output_weight.shape)
    sum_vectors = sum_first[..., wide + half : wide + half + vector_rows].astype(jnp.float32)
    sum_vectors = jnp.sum(sum_vectors, axis=2).reshape(owned, vector_rows).T

    def renew(weight, moment, second, gradient, step_rate, weight_decay):
        return adamw_step(
            weight, moment, second, gradient.astype(jnp.float32), step_rate, weight_decay
        )

    new_inputs = renew(inputs_weight, inputs_moment, inputs_second, sum_inputs, 0.03, decay_rate)
    new_output = renew(output_weight, output_moment, output_second, sum_output, 0.3, decay_rate)
    new_expand = renew(expand_weight, expand_moment, expand_second, sum_expand, 0.03, decay_rate)
    new_reduce = renew(reduce_weight, reduce_moment, reduce_second, sum_reduce, 0.02, decay_rate)
    new_vectors = renew(vector_params, vector_moment, vector_second, sum_vectors, 0.5, 0.0)
    return (
        layer_output,
        input_grad,
        *new_inputs,
        *new_output,
        *new_expand,
        *new_reduce,
        *new_vectors,
    )


def solution(mesh):
    tokens = P("dp", "seq", None)
    rows = P("seq", None)
    columns = P(None, "seq")
    in_specs = (tokens, tokens, P("dp", None)) + (rows,) * 12 + (columns,) * 3
    out_specs = (tokens, tokens) + (rows,) * 12 + (columns,) * 3
    return jax.shard_map(
        partial(on_device, mesh.shape["dp"], mesh.shape["seq"]),
        mesh=mesh,
        in_specs=in_specs,
        out_specs=out_specs,
        check_vma=False,
    )
```

```python
from functools import partial

import jax
import jax.numpy as jnp
from jax import lax
from jax.experimental import pallas as pl
from jax.experimental.pallas import tpu as pltpu
from jax.sharding import PartitionSpec as P

HEADS = 12
HD = 64
STEP = 10
PAIR = 2 * HD
LANES = 128

eps_norm = 1e-05
eps_adam = 1e-08
beta_one = 0.9
beta_two = 0.95
decay_rate = 0.1
mask_fill = -1e30
vmem_bytes = 56 * 1024 * 1024

VISIBLE = (
    (0, 256, 0, 256),
    (256, 256, 128, 512),
    (512, 256, 128, 768),
    (768, 128, 128, 896),
    (896, 128, 768, 1024),
)
TILE_STARTS = []
tile_total = 0
for _first, _rows, _low, _high in VISIBLE:
    TILE_STARTS.append(tile_total)
    tile_total += _high - _low

low = jnp.bfloat16


def dot_nn(left_side, right_side):
    return lax.dot_general(
        left_side, right_side, (((1,), (0,)), ((), ())), preferred_element_type=jnp.float32
    )


def dot_tn(left_side, right_side):
    return lax.dot_general(
        left_side, right_side, (((0,), (0,)), ((), ())), preferred_element_type=jnp.float32
    )


def dot_nt(left_side, right_side):
    return lax.dot_general(
        left_side, right_side, (((1,), (1,)), ((), ())), preferred_element_type=jnp.float32
    )


def normalize(values):
    center = jnp.mean(values, axis=-1, keepdims=True)
    offsets = values - center
    spread = jnp.mean(offsets * offsets, axis=-1, keepdims=True)
    inverse = lax.rsqrt(spread + eps_norm)
    return offsets * inverse, inverse


def norm_back(grad_normed, gain, unit, inverse):
    scaled = grad_normed * gain
    mean_scaled = jnp.mean(scaled, axis=-1, keepdims=True)
    mean_cross = jnp.mean(scaled * unit, axis=-1, keepdims=True)
    return inverse * (scaled - mean_scaled - unit * mean_cross)


def adamw_step(weight, moment, second, gradient, step_rate, weight_decay):
    moment_new = beta_one * moment + (1.0 - beta_one) * gradient
    second_new = beta_two * second + (1.0 - beta_two) * gradient * gradient
    fix_one = 1.0 - beta_one**STEP
    fix_two = 1.0 - beta_two**STEP
    update = moment_new / fix_one / (jnp.sqrt(second_new / fix_two) + eps_adam)
    return (weight - step_rate * (update + weight_decay * weight), moment_new, second_new)


def column_sum(values):
    return jnp.sum(values.astype(jnp.float32), axis=0)


def fill_bias(seg_row, seg_col, bias):
    for (first, rows, key_low, key_high), start in zip(VISIBLE, TILE_STARTS):
        keys = key_high - key_low
        key_places = key_low + lax.broadcasted_iota(jnp.int32, (keys, rows), 0)
        query_places = first + lax.broadcasted_iota(jnp.int32, (keys, rows), 1)
        same = seg_col[key_low:key_high, :] == seg_row[:, first : first + rows]
        allowed = same & (key_places <= query_places)
        bias[start : start + keys, 0:rows] = jnp.where(allowed, 0.0, mask_fill)


def lane_masks(shape):
    lane = lax.broadcasted_iota(jnp.int32, shape, 1)
    return (lane < HD, lane >= HD)


def masked_to(values, mask):
    return jnp.where(mask, values, jnp.zeros_like(values))


def attend_forward_kernel(seg_row, seg_col, q_ref, k_ref, v_ref, out_ref, log_ref, bias):
    @pl.when(pl.program_id(0) == 0)
    def _():
        fill_bias(seg_row, seg_col, bias)

    masks = lane_masks((k_ref.shape[0], PAIR))
    keys_masked = [masked_to(k_ref[...], mask) for mask in masks]
    for (first, rows, key_low, key_high), start in zip(VISIBLE, TILE_STARTS):
        queries = q_ref[first : first + rows, :] * jnp.asarray(HD**-0.5, low)
        values = v_ref[key_low:key_high, :]
        mixed = []
        for head in range(2):
            scores = dot_nt(keys_masked[head][key_low:key_high], queries)
            scores = scores + bias[start : start + key_high - key_low, 0:rows]
            highest = jnp.max(scores, axis=0, keepdims=True)
            exponent = jnp.exp(scores - highest)
            totals = jnp.sum(exponent, axis=0, keepdims=True)
            soft = (exponent * (1.0 / totals)).astype(low)
            mixed.append(dot_tn(soft, values))
            log_ref[0, head : head + 1, first : first + rows] = highest + jnp.log(totals)
        half = lane_masks((rows, PAIR))[0]
        out_ref[first : first + rows, :] = jnp.where(half, mixed[0], mixed[1]).astype(low)


def attend_backward_kernel(
    seg_row, seg_col, q_ref, k_ref, v_ref, log_ref, do_ref, dq_ref, dk_ref, dv_ref, bias, dk_acc, dv_acc
):
    @pl.when(pl.program_id(0) == 0)
    def _():
        fill_bias(seg_row, seg_col, bias)

    masks = lane_masks((k_ref.shape[0], PAIR))
    keys_masked = [masked_to(k_ref[...], mask) for mask in masks]
    values_masked = [masked_to(v_ref[...], mask) for mask in masks]
    dk_acc[...] = jnp.zeros_like(dk_acc)
    dv_acc[...] = jnp.zeros_like(dv_acc)
    for (first, rows, key_low, key_high), start in zip(VISIBLE, TILE_STARTS):
        queries = q_ref[first : first + rows, :] * jnp.asarray(HD**-0.5, low)
        grads = do_ref[first : first + rows, :]
        grad_query = jnp.zeros((rows, PAIR), jnp.float32)
        row_masks = lane_masks((rows, PAIR))
        for head in range(2):
            keys = keys_masked[head][key_low:key_high]
            scores = dot_nt(keys, queries)
            scores = scores + bias[start : start + key_high - key_low, 0:rows]
            soft = jnp.exp(scores - log_ref[0, head : head + 1, first : first + rows])
            grad_soft = dot_nt(values_masked[head][key_low:key_high], grads)
            inner = jnp.sum(soft * grad_soft, axis=0, keepdims=True)
            grad_scores = (soft * (grad_soft - inner)).astype(low)
            dv_acc[key_low:key_high, :] += dot_nn(
                soft.astype(low), masked_to(grads, row_masks[head])
            )
            dk_acc[key_low:key_high, :] += dot_nn(
                grad_scores, masked_to(queries, row_masks[head])
            )
            grad_query = grad_query + dot_tn(grad_scores, keys)
        dq_ref[first : first + rows, :] = (grad_query * HD**-0.5).astype(low)
    dk_ref[...] = dk_acc[...].astype(low)
    dv_ref[...] = dv_acc[...].astype(low)


def attend_specs(length, pairs):
    whole = lambda shape: pl.BlockSpec(shape, lambda j: (0,) * len(shape))
    columns = lambda offset: pl.BlockSpec((length, PAIR), lambda j, offset=offset: (0, offset + j))
    logs = pl.BlockSpec((1, 8, length), lambda j: (j, 0, 0))
    return whole, columns, logs


def attend_forward(seg_row, seg_col, projected):
    length = projected.shape[0]
    pairs = projected.shape[1] // (3 * PAIR)
    whole, columns, logs = attend_specs(length, pairs)
    return pl.pallas_call(
        attend_forward_kernel,
        grid=(pairs,),
        in_specs=[
            whole((1, length)),
            whole((length, 1)),
            columns(0),
            columns(pairs),
            columns(2 * pairs),
        ],
        out_specs=[columns(0), logs],
        out_shape=[
            jax.ShapeDtypeStruct((length, pairs * PAIR), low),
            jax.ShapeDtypeStruct((pairs, 8, length), jnp.float32),
        ],
        scratch_shapes=[pltpu.VMEM((tile_total, 256), jnp.float32)],
        compiler_params=pltpu.CompilerParams(vmem_limit_bytes=vmem_bytes),
        cost_estimate=pl.CostEstimate(
            flops=4 * length * length * pairs * PAIR, bytes_accessed=8 * length * pairs * PAIR,
            transcendentals=length * length * pairs,
        ),
        name="attend_forward",
    )(seg_row, seg_col, projected, projected, projected)


def attend_backward(seg_row, seg_col, projected, logs_all, grad_mixture):
    length = projected.shape[0]
    pairs = projected.shape[1] // (3 * PAIR)
    whole, columns, logs = attend_specs(length, pairs)
    return pl.pallas_call(
        attend_backward_kernel,
        grid=(pairs,),
        in_specs=[
            whole((1, length)),
            whole((length, 1)),
            columns(0),
            columns(pairs),
            columns(2 * pairs),
            logs,
            columns(0),
        ],
        out_specs=[columns(0)] * 3,
        out_shape=[jax.ShapeDtypeStruct((length, pairs * PAIR), low)] * 3,
        scratch_shapes=[
            pltpu.VMEM((tile_total, 256), jnp.float32),
            pltpu.VMEM((length, PAIR), jnp.float32),
            pltpu.VMEM((length, PAIR), jnp.float32),
        ],
        compiler_params=pltpu.CompilerParams(vmem_limit_bytes=vmem_bytes),
        cost_estimate=pl.CostEstimate(
            flops=10 * length * length * pairs * PAIR, bytes_accessed=14 * length * pairs * PAIR,
            transcendentals=length * length * pairs,
        ),
        name="attend_backward",
    )(seg_row, seg_col, projected, projected, projected, logs_all, grad_mixture)


def feed_kernel(block_count, *refs):
    refs = list(refs)
    take = lambda count: [refs.pop(0) for _ in range(count)]
    normed = [ref[...] for ref in take(2)]
    tops = [ref[...] for ref in take(2)]
    blocks = [(take(2), take(1)[0]) for _ in range(block_count)]
    reduced, reduced_out, back, back_out = take(4)
    outs = [(take(2), take(1)[0]) for _ in range(block_count)]
    turned, weights, grads, reduced_sum, back_sum, in_sems, out_sems = refs
    owners, depth, units = weights.shape[2:]
    side_rows = units // (2 * owners)
    split = depth - 2 * side_rows
    arrivals = [
        [
            pltpu.make_async_copy(parts[part], weights.at[index, part], in_sems.at[index, part])
            for part in range(2)
        ]
        for index, (parts, _) in enumerate(blocks)
    ]
    for copies in arrivals:
        for copy in copies:
            copy.start()
    rows = normed[0].shape[0]
    reduced_sums = (reduced, reduced_sum)
    back_sums = (back, back_sum)
    for side in range(2):
        turned[:, side * rows : (side + 1) * rows] = normed[side].T
    departures = []
    for index, ((_, bias), (grad_refs, dbu_ref)) in enumerate(zip(blocks, outs)):
        for copy in arrivals[index]:
            copy.wait()
        places = [(part, owner) for part in range(2) for owner in range(owners)]
        expand = jnp.concatenate([weights[index, part, owner, :split] for part, owner in places], axis=0)
        reduce = jnp.concatenate(
            [
                jnp.concatenate(
                    [
                        weights[index, part, owner, split : split + side_rows],
                        weights[index, part, owner, split + side_rows :],
                    ],
                    axis=1,
                )
                for part, owner in places
            ],
            axis=0,
        )
        hiddens, slopes = [], []
        for side in range(2):
            expanded = dot_nn(normed[side], expand) + bias[...]
            phi = 0.5 + 0.5 * lax.erf(expanded * (0.5**0.5))
            density = jnp.exp(-0.5 * expanded * expanded) * 0.3989422804014327
            hiddens.append((expanded * phi).astype(low))
            grad_hidden = dot_nt(tops[side], reduce)
            slopes.append((grad_hidden * (phi + expanded * density)).astype(low))
        for side in range(2):
            down = dot_nn(hiddens[side], reduce)
            up = dot_nt(slopes[side], expand)
            if index:
                reduced_sums[side][...] += down
                back_sums[side][...] += up
            else:
                reduced_sums[side][...] = down
                back_sums[side][...] = up
        grad_both = jnp.concatenate(slopes, axis=0)
        grad_reduce = sum(dot_tn(hiddens[side], tops[side]) for side in range(2)).astype(low)
        for place, (part, owner) in enumerate(places):
            grads[index, part, owner, :split] = dot_nn(
                turned[place * split : (place + 1) * split, :], grad_both
            ).astype(low)
            rows_down = grad_reduce[place * side_rows : (place + 1) * side_rows]
            grads[index, part, owner, split : split + side_rows] = rows_down[:, :units]
            grads[index, part, owner, split + side_rows :] = rows_down[:, units:]
        dbu_ref[...] = jnp.sum(grad_both.astype(jnp.float32), axis=0, keepdims=True)
        for part in range(2):
            departures.append(
                pltpu.make_async_copy(
                    grads.at[index, part], grad_refs[part], out_sems.at[index, part]
                )
            )
            departures[-1].start()
    reduced_out[...] = reduced_sum[...].astype(low)
    back_out[...] = back_sum[...].astype(low)
    for copy in departures:
        copy.wait()


def feed_blocks(normed, tops, blocks):
    rows, features = normed[0].shape
    count = len(blocks)
    units = blocks[0][1].shape[1]
    operands = [*normed, *tops]
    in_vmem = pl.BlockSpec(memory_space=pltpu.VMEM)
    anywhere = pl.BlockSpec(memory_space=pl.ANY)
    sum_shape = jax.ShapeDtypeStruct((rows, features), jnp.float32)
    sent_shape = jax.ShapeDtypeStruct((rows, features), low)
    shapes = [sum_shape, sent_shape, sum_shape, sent_shape]
    for parts, bias in blocks:
        operands += [*parts, bias]
        shapes += [jax.ShapeDtypeStruct(part.shape, low) for part in parts]
        shapes += [jax.ShapeDtypeStruct((1, units), jnp.float32)]
    part_shape = blocks[0][0][0].shape
    results = pl.pallas_call(
        partial(feed_kernel, count),
        in_specs=[in_vmem] * 4 + [anywhere, anywhere, in_vmem] * count,
        out_specs=[in_vmem] * 4 + [anywhere, anywhere, in_vmem] * count,
        out_shape=shapes,
        scratch_shapes=[
            pltpu.VMEM((features, 2 * rows), low),
            pltpu.VMEM((count, 2) + part_shape, low),
            pltpu.VMEM((count, 2) + part_shape, low),
            pltpu.VMEM((rows, features), jnp.float32),
            pltpu.VMEM((rows, features), jnp.float32),
            pltpu.SemaphoreType.DMA((count, 2)),
            pltpu.SemaphoreType.DMA((count, 2)),
        ],
        compiler_params=pltpu.CompilerParams(vmem_limit_bytes=vmem_bytes),
        cost_estimate=pl.CostEstimate(
            flops=24 * rows * features * units * count,
            bytes_accessed=8 * features * units * count,
            transcendentals=4 * rows * units * count,
        ),
        name="feed_blocks",
    )(*operands)
    grads = [results[4 + 3 * index : 7 + 3 * index] for index in range(count)]
    return results[:4], grads


def chip_routes(dp_count, seq_count):
    straight, crossed = [], []
    for place in range(dp_count):
        group, core = place - place % 2, place % 2
        for quarter in range(seq_count):
            source = place * seq_count + quarter
            holder = (group + quarter // 2) * seq_count
            straight.append((source, holder + 2 * core + quarter % 2))
            crossed.append((source, holder + 2 * core + 1 - quarter % 2))
    return straight, crossed


def on_device(
    dp_count,
    seq_count,
    activations,
    cotangent,
    segment_ids,
    inputs_weight,
    inputs_moment,
    inputs_second,
    output_weight,
    output_moment,
    output_second,
    expand_weight,
    expand_moment,
    expand_second,
    reduce_weight,
    reduce_moment,
    reduce_second,
    vector_params,
    vector_moment,
    vector_second,
):
    axes = ("dp", "seq")
    dp_index = lax.axis_index("dp")
    seq_index = lax.axis_index("seq")
    core = dp_index % 2
    group = dp_index // 2
    groups = dp_count // 2
    four_chips = groups == 4
    odd = seq_index % 2
    features = activations.shape[2]
    quarter = activations.shape[1]
    half = features // 2
    owned = inputs_weight.shape[0]
    owned_units = reduce_weight.shape[0]
    rows_piece = owned // groups
    units_piece = owned_units // dp_count
    vector_rows = vector_params.shape[0]
    straight, crossed = chip_routes(dp_count, seq_count)
    core_pairs = [(place, place ^ 1) for place in range(dp_count)]
    x_pairs = [(place, place ^ 2) for place in range(dp_count)]
    y_pairs = [(place, place ^ 4) for place in range(dp_count)]
    far_pairs = [(place, place ^ 6) for place in range(dp_count)]
    same_core = [list(range(first, dp_count, 2)) for first in range(2)]

    def to_chip(values):
        near = lax.dynamic_index_in_dim(values, odd, 0, keepdims=False)
        far = lax.dynamic_index_in_dim(values, 1 - odd, 0, keepdims=False)
        near = lax.ppermute(near, axes, straight)
        far = lax.ppermute(far, axes, crossed)
        return jnp.concatenate(
            [jnp.where(odd == 0, near, far), jnp.where(odd == 0, far, near)], axis=0
        )

    def from_chip(values):
        near = lax.dynamic_slice_in_dim(values, odd * quarter, quarter, 0)
        far = lax.dynamic_slice_in_dim(values, (1 - odd) * quarter, quarter, 0)
        near = lax.ppermute(near, axes, [(there, here) for here, there in straight])
        far = lax.ppermute(far, axes, [(there, here) for here, there in crossed])
        return jnp.stack([jnp.where(odd == 0, near, far), jnp.where(odd == 0, far, near)])

    def swap_cores(values):
        return lax.ppermute(values, "dp", core_pairs)

    def via_x(values):
        return lax.ppermute(values, "dp", x_pairs)

    def via_y(values):
        return lax.ppermute(values, "dp", y_pairs)

    def by_core(mine, theirs, axis):
        return jnp.where(
            core == 0,
            jnp.concatenate([mine, theirs], axis=axis),
            jnp.concatenate([theirs, mine], axis=axis),
        )

    def add_low(*terms):
        return sum(term.astype(jnp.float32) for term in terms).astype(low)

    def after(values, *gates):
        return lax.optimization_barrier((values, gates))[0]

    def gather_z(piece):
        parts = [piece]
        for shift in range(1, seq_count):
            ring = [(place, (place + shift) % seq_count) for place in range(seq_count)]
            parts.append(lax.ppermute(piece, "seq", ring))
        placed = [
            lax.select_n((seq_index - owner) % seq_count, *parts) for owner in range(seq_count)
        ]
        middle = seq_count // 2
        return jnp.stack(placed[:middle]), jnp.stack(placed[middle:])

    def gather_chips(halves):
        first, second = halves
        x_first, y_second = via_x(first), via_y(second)
        x_second, y_first = via_x(second), via_y(first)
        return halves, (x_first, x_second), (y_first, y_second), (via_y(x_first), via_x(y_second))

    def in_order(own, from_x, from_y, from_far, axis):
        x_set = group % 2 == 1
        y_set = group // 2 == 1
        near_low = jnp.where(x_set, from_x, own)
        near_high = jnp.where(x_set, own, from_x)
        far_low = jnp.where(x_set, from_far, from_y)
        far_high = jnp.where(x_set, from_y, from_far)
        return jnp.stack(
            [
                jnp.where(y_set, far_low, near_low),
                jnp.where(y_set, far_high, near_high),
                jnp.where(y_set, near_low, far_low),
                jnp.where(y_set, near_high, far_high),
            ],
            axis=axis,
        )

    def scatter_begin(own, to_x, to_y, to_far):
        far_first, far_second = via_x(to_far[0]), via_y(to_far[1])
        return (own, to_x, to_y, far_first, far_second, via_x(to_x[0]), via_y(to_y[1]))

    def scatter_middle(state, *gates):
        own, to_x, to_y, far_first, far_second, x_first, y_second = state
        far_first, far_second = after((far_first, far_second), *gates)
        y_first = add_low(to_y[0], far_first)
        x_second = add_low(to_x[1], far_second)
        return (own, x_first, via_x(x_second), via_y(y_first), y_second), (y_first, x_second)

    def scatter_end(state):
        own, x_first, x_second, y_first, y_second = state
        first = add_low(own[0], x_first, y_first)
        second = add_low(own[1], x_second, y_second)
        return jnp.concatenate([first, second], axis=0)

    def scatter_z_begin(blocks):
        parts = [lax.dynamic_index_in_dim(blocks, seq_index, 0, keepdims=False)]
        for shift in range(1, seq_count):
            target = (seq_index + shift) % seq_count
            sent = lax.dynamic_index_in_dim(blocks, target, 0, keepdims=False)
            ring = [(place, (place + shift) % seq_count) for place in range(seq_count)]
            parts.append(lax.ppermute(sent, "seq", ring))
        return parts

    def scatter_z(blocks):
        return add_low(*scatter_z_begin(blocks))

    def regather_begin(piece):
        return piece, via_x(piece), via_y(piece), lax.ppermute(piece, "dp", far_pairs)

    def regather_end(state):
        mine = in_order(*state, 0)
        return by_core(mine[:, None], swap_cores(mine)[:, None], 1)

    def regather(piece):
        every = lax.all_gather(piece, "dp", axis=0, tiled=False)
        return every.reshape((groups, 2) + piece.shape)

    def corner(weight, column):
        return lax.dynamic_slice(
            weight, (group * rows_piece, column + core * half), (rows_piece, half)
        ).astype(low)

    vector_piece = lax.dynamic_slice_in_dim(vector_params, group * rows_piece, rows_piece, 1)
    first_piece = jnp.concatenate(
        [
            corner(inputs_weight, 0),
            corner(inputs_weight, features),
            corner(inputs_weight, 2 * features),
            corner(output_weight, 0),
            jnp.pad(vector_piece.T.astype(low), ((0, 0), (0, LANES - vector_rows))),
        ],
        axis=1,
    )
    expand_piece = jnp.concatenate(
        [
            lax.dynamic_slice_in_dim(
                expand_weight, owner * owned_units + dp_index * units_piece, units_piece, 1
            ).astype(low)
            for owner in range(seq_count)
        ],
        axis=1,
    )
    reduce_piece = lax.dynamic_slice_in_dim(
        reduce_weight, dp_index * units_piece, units_piece, 0
    ).astype(low)

    def pack(expand, reduce):
        return jnp.concatenate([expand, reduce[..., :half], reduce[..., half:]], axis=-2)

    residual_low = to_chip(activations)
    first_block = gather_z(first_piece)
    if four_chips:
        feed_piece = after(pack(expand_piece, reduce_piece), first_block)
        feed_all = lax.all_gather(feed_piece, "seq", axis=0, tiled=False)
        feed_halves = (feed_all[: seq_count // 2], feed_all[seq_count // 2 :])
        cotangent = after(cotangent, feed_halves)
    grad_top = to_chip(cotangent)
    rows_here = residual_low.shape[0]
    residual_other = swap_cores(residual_low)
    grad_top_other = swap_cores(grad_top)
    other_segments = swap_cores(segment_ids)
    segment_pair = jnp.where(seq_index // 2 == core, segment_ids, other_segments)
    segments = lax.dynamic_index_in_dim(segment_pair, odd, 0, keepdims=False)
    seg_row, seg_col = segments[None, :], segments[:, None]

    if four_chips:
        every_first = gather_chips(first_block)
        first_low = jnp.concatenate(
            [in_order(*[block[part] for block in every_first], 1) for part in range(2)], axis=0
        )
    else:
        first_low = lax.all_gather(
            jnp.concatenate(first_block, axis=0),
            "dp",
            axis=1,
            tiled=False,
            axis_index_groups=same_core,
        )
    first_low = first_low.reshape(features, first_low.shape[-1])
    wide = 3 * half
    inputs_low = first_low[:, :wide]
    output_half = first_low[:, wide : wide + half]
    output_all = by_core(output_half, swap_cores(output_half), 1)
    vectors = first_low[:, wide + half : wide + half + vector_rows].T.astype(jnp.float32)

    expand_bias = vectors[8:].reshape(seq_count, dp_count, units_piece)
    block_units = seq_count * owned_units // 8
    if four_chips:
        blocks = []
        for offset, parts in enumerate(gather_chips(feed_halves)):
            place = dp_index ^ (2 * offset)
            bias = lax.dynamic_index_in_dim(expand_bias, place, 1, keepdims=False)
            blocks.append((parts, bias.reshape(1, block_units)))
    else:
        expand_all = lax.all_gather(
            jnp.concatenate(gather_z(expand_piece), axis=0).reshape(features, -1),
            "dp",
            axis=1,
            axis_index_groups=same_core,
        ).reshape(seq_count, owned, 4, block_units)
        reduce_all = lax.all_gather(
            jnp.concatenate(gather_z(reduce_piece), axis=0).reshape(-1, features),
            "dp",
            axis=0,
            axis_index_groups=same_core,
        ).reshape(4, seq_count, -1, features)
        picked = lax.dynamic_index_in_dim(
            expand_bias.reshape(seq_count, groups, 2, units_piece), core, 2, keepdims=False
        )
        bias_all = picked.transpose(1, 0, 2).reshape(4, 1, block_units)
        blocks = []
        for index in range(4):
            packed = pack(expand_all[:, :, index], reduce_all[index])
            blocks.append(
                ((packed[: seq_count // 2], packed[seq_count // 2 :]), bias_all[index])
            )

    def tokens_of(values, which):
        return lax.dynamic_slice_in_dim(values, which * rows_here, rows_here, 0)

    def heads_part(vector):
        return lax.dynamic_slice_in_dim(vector, core * half, half, 0)

    unit_all, _ = normalize(by_core(residual_low, residual_other, 0).astype(jnp.float32))
    normed_one = (unit_all * vectors[0] + vectors[1]).astype(low)
    input_bias = jnp.concatenate(
        [heads_part(vectors[4]), jnp.zeros((half,), jnp.float32), heads_part(vectors[5])]
    )
    projected = (dot_nn(normed_one, inputs_low) + input_bias).astype(low)
    if four_chips:
        projected = after(projected, feed_halves)
    mixture_heads, logs_all = attend_forward(seg_row, seg_col, projected)
    mixture_theirs = swap_cores(tokens_of(mixture_heads, 1 - core))
    mixture = by_core(tokens_of(mixture_heads, core), mixture_theirs, 1)

    residual = residual_low.astype(jnp.float32)
    middle = residual + (dot_nn(mixture, output_all) + vectors[6])
    unit_two, inverse_two = normalize(middle)
    normed_two = (unit_two * vectors[2] + vectors[3]).astype(low)
    normed_pair = (normed_two, swap_cores(normed_two))
    top_pair = (grad_top, grad_top_other)
    sums, grads = feed_blocks(normed_pair, top_pair, blocks)
    grad_normed_two = sums[2] + swap_cores(sums[3]).astype(jnp.float32)
    reduced = sums[0] + swap_cores(sums[1]).astype(jnp.float32)
    output_low = (middle + (reduced + vectors[7])).astype(low)

    if four_chips:
        feed_state = scatter_begin(*[grad[:2] for grad in grads])
        place = jnp.arange(dp_count)[None, :, None]
        bias_sums = sum(
            jnp.where(
                place == (dp_index ^ (2 * offset)),
                grads[offset][2].reshape(seq_count, 1, units_piece),
                0.0,
            )
            for offset in range(4)
        )
    else:
        packed = [jnp.concatenate(grad[:2], axis=0) for grad in grads]
        expand_sum = jnp.stack([part[:, :owned] for part in packed], axis=2)
        expand_sum = expand_sum.reshape(features, groups, -1).transpose(1, 0, 2)
        expand_sum = lax.psum_scatter(expand_sum, "dp", axis_index_groups=same_core)
        reduce_sum = [part[:, owned:].reshape(seq_count, 2, -1, half) for part in packed]
        reduce_sum = jnp.stack([part.transpose(0, 2, 1, 3) for part in reduce_sum])
        reduce_sum = reduce_sum.reshape(groups, -1, features)
        reduce_sum = lax.psum_scatter(reduce_sum, "dp", axis_index_groups=same_core)
        bias_sums = jnp.concatenate([grad[2] for grad in grads], axis=1)
        bias_sums = bias_sums.reshape(groups, seq_count, units_piece).transpose(1, 0, 2)
        is_core = jnp.arange(2)[None, None, :, None] == core
        bias_sums = jnp.where(is_core, bias_sums[:, :, None, :], 0.0)

    grad_middle = grad_top.astype(jnp.float32) + norm_back(
        grad_normed_two, vectors[2], unit_two, inverse_two
    )
    grad_attended = grad_middle.astype(low)
    grad_output = dot_tn(mixture, grad_attended).astype(low)
    grad_mixture = dot_nt(grad_attended, output_all).astype(low)

    def columns_of(values, which):
        return lax.dynamic_slice_in_dim(values, which * half, half, 1)

    grad_theirs = swap_cores(columns_of(grad_mixture, 1 - core))
    grad_joined = by_core(columns_of(grad_mixture, core), grad_theirs, 0)
    if four_chips:
        feed_state, gates = scatter_middle(feed_state, grad_mixture)
        grad_joined = after(grad_joined, *gates)
    grad_heads = attend_backward(seg_row, seg_col, projected, logs_all, grad_joined)
    output_sum = add_low(
        columns_of(grad_output, core), swap_cores(columns_of(grad_output, 1 - core))
    )
    layer_output = from_chip(after(output_low, grad_heads))
    grad_projected = jnp.concatenate(grad_heads, axis=1)
    grad_inputs = dot_tn(normed_one, grad_projected).astype(low)
    grad_normed_all = dot_nt(grad_projected, inputs_low)
    grad_normed_one = tokens_of(grad_normed_all, core) + swap_cores(
        tokens_of(grad_normed_all, 1 - core).astype(low)
    ).astype(jnp.float32)
    unit_one, inverse_one = normalize(residual)
    grad_residual = norm_back(grad_normed_one, vectors[0], unit_one, inverse_one)
    input_grad = from_chip((grad_middle + grad_residual).astype(low))

    def heads_sum(values):
        return lax.dynamic_update_slice_in_dim(
            jnp.zeros((features,), jnp.float32), column_sum(values), core * half, 0
        )

    head_rows = jnp.stack(
        [
            column_sum(grad_normed_one * unit_one),
            column_sum(grad_normed_one),
            column_sum(grad_normed_two * unit_two),
            column_sum(grad_normed_two),
            heads_sum(grad_heads[0]),
            heads_sum(grad_heads[2]),
            column_sum(grad_attended),
            column_sum(grad_top),
        ]
    )
    grad_vectors = jnp.concatenate([head_rows, bias_sums.reshape(-1, features)], axis=0)
    vector_columns = jnp.pad(grad_vectors.T.astype(low), ((0, 0), (0, LANES - vector_rows)))
    first_grad = jnp.concatenate([grad_inputs, output_sum, vector_columns], axis=1)
    first_grad = first_grad.reshape(seq_count, groups, rows_piece, -1)
    if four_chips:
        middle_owner = seq_count // 2
        split = []
        for offset in range(4):
            split.append(
                [
                    lax.dynamic_index_in_dim(part, group ^ offset, 1, keepdims=False)
                    for part in (first_grad[:middle_owner], first_grad[middle_owner:])
                ]
            )
        feed_parts = scatter_z_begin(scatter_end(after(feed_state, grad_normed_all, grad_inputs)))
        first_state = scatter_begin(*split)
        feed_parts = after(feed_parts, split)
        feed_state = regather_begin(add_low(*feed_parts))
        first_state, gates = scatter_middle(first_state, feed_state[0])
        feed_state = after(feed_state, *gates)
        every = regather_end(feed_state)
        first_parts = scatter_z_begin(scatter_end(first_state))
        sum_expand = every[:, :, :owned]
        sum_reduce = jnp.concatenate(
            [every[:, :, owned : owned + units_piece], every[:, :, owned + units_piece :]], axis=-1
        )
        every_first = regather_end(regather_begin(add_low(*first_parts)))
    else:
        first_sum = lax.psum_scatter(
            first_grad, "dp", scatter_dimension=1, axis_index_groups=same_core
        )
        every_first = regather(scatter_z(first_sum))
        sum_expand = regather(scatter_z(expand_sum.reshape(seq_count, owned, -1)))
        sum_reduce = regather(scatter_z(reduce_sum.reshape(seq_count, units_piece, features)))
    sum_expand = sum_expand.reshape(dp_count, owned, seq_count, units_piece)
    sum_expand = sum_expand.transpose(1, 2, 0, 3).reshape(expand_weight.shape)
    sum_reduce = sum_reduce.reshape(reduce_weight.shape)
    sum_first = every_first.transpose(0, 2, 1, 3)
    sum_inputs = sum_first[..., :wide].reshape(groups, rows_piece, 2, 3, half)
    sum_inputs = sum_inputs.transpose(0, 1, 3, 2, 4).reshape(inputs_weight.shape)
    sum_output = sum_first[..., wide : wide + half].reshape(output_weight.shape)
    sum_vectors = sum_first[..., wide + half : wide + half + vector_rows].astype(jnp.float32)
    sum_vectors = jnp.sum(sum_vectors, axis=2).reshape(owned, vector_rows).T

    def renew(weight, moment, second, gradient, step_rate, weight_decay):
        return adamw_step(
            weight, moment, second, gradient.astype(jnp.float32), step_rate, weight_decay
        )

    new_inputs = renew(inputs_weight, inputs_moment, inputs_second, sum_inputs, 0.03, decay_rate)
    new_output = renew(output_weight, output_moment, output_second, sum_output, 0.3, decay_rate)
    new_expand = renew(expand_weight, expand_moment, expand_second, sum_expand, 0.03, decay_rate)
    new_reduce = renew(reduce_weight, reduce_moment, reduce_second, sum_reduce, 0.02, decay_rate)
    new_vectors = renew(vector_params, vector_moment, vector_second, sum_vectors, 0.5, 0.0)
    return (
        layer_output,
        input_grad,
        *new_inputs,
        *new_output,
        *new_expand,
        *new_reduce,
        *new_vectors,
    )


def solution(mesh):
    tokens = P("dp", "seq", None)
    rows = P("seq", None)
    columns = P(None, "seq")
    in_specs = (tokens, tokens, P("dp", None)) + (rows,) * 12 + (columns,) * 3
    out_specs = (tokens, tokens) + (rows,) * 12 + (columns,) * 3
    return jax.shard_map(
        partial(on_device, mesh.shape["dp"], mesh.shape["seq"]),
        mesh=mesh,
        in_specs=in_specs,
        out_specs=out_specs,
        check_vma=False,
    )
```

```python
from functools import partial

import jax
import jax.numpy as jnp
from jax import lax
from jax.experimental import pallas as pl
from jax.experimental.pallas import tpu as pltpu
from jax.sharding import PartitionSpec as P

HEADS = 12
HD = 64
STEP = 10
PAIR = 2 * HD
LANES = 128

eps_norm = 1e-05
eps_adam = 1e-08
beta_one = 0.9
beta_two = 0.95
decay_rate = 0.1
mask_fill = -1e30
vmem_bytes = 56 * 1024 * 1024

VISIBLE = (
    (0, 256, 0, 256),
    (256, 256, 128, 512),
    (512, 256, 128, 768),
    (768, 128, 128, 896),
    (896, 128, 768, 1024),
)
TILE_STARTS = []
tile_total = 0
for _first, _rows, _low, _high in VISIBLE:
    TILE_STARTS.append(tile_total)
    tile_total += _high - _low

low = jnp.bfloat16


def dot_nn(left_side, right_side):
    return lax.dot_general(
        left_side, right_side, (((1,), (0,)), ((), ())), preferred_element_type=jnp.float32
    )


def dot_tn(left_side, right_side):
    return lax.dot_general(
        left_side, right_side, (((0,), (0,)), ((), ())), preferred_element_type=jnp.float32
    )


def dot_nt(left_side, right_side):
    return lax.dot_general(
        left_side, right_side, (((1,), (1,)), ((), ())), preferred_element_type=jnp.float32
    )


def normalize(values):
    center = jnp.mean(values, axis=-1, keepdims=True)
    offsets = values - center
    spread = jnp.mean(offsets * offsets, axis=-1, keepdims=True)
    inverse = lax.rsqrt(spread + eps_norm)
    return offsets * inverse, inverse


def norm_back(grad_normed, gain, unit, inverse):
    scaled = grad_normed * gain
    mean_scaled = jnp.mean(scaled, axis=-1, keepdims=True)
    mean_cross = jnp.mean(scaled * unit, axis=-1, keepdims=True)
    return inverse * (scaled - mean_scaled - unit * mean_cross)


def adamw_step(weight, moment, second, gradient, step_rate, weight_decay):
    moment_new = beta_one * moment + (1.0 - beta_one) * gradient
    second_new = beta_two * second + (1.0 - beta_two) * gradient * gradient
    fix_one = 1.0 - beta_one**STEP
    fix_two = 1.0 - beta_two**STEP
    update = moment_new / fix_one / (jnp.sqrt(second_new / fix_two) + eps_adam)
    return (weight - step_rate * (update + weight_decay * weight), moment_new, second_new)


def column_sum(values):
    return jnp.sum(values.astype(jnp.float32), axis=0)


def fill_bias(seg_row, seg_col, bias):
    for (first, rows, key_low, key_high), start in zip(VISIBLE, TILE_STARTS):
        keys = key_high - key_low
        key_places = key_low + lax.broadcasted_iota(jnp.int32, (keys, rows), 0)
        query_places = first + lax.broadcasted_iota(jnp.int32, (keys, rows), 1)
        same = seg_col[key_low:key_high, :] == seg_row[:, first : first + rows]
        allowed = same & (key_places <= query_places)
        bias[start : start + keys, 0:rows] = jnp.where(allowed, 0.0, mask_fill)


def lane_masks(shape):
    lane = lax.broadcasted_iota(jnp.int32, shape, 1)
    return (lane < HD, lane >= HD)


def masked_to(values, mask):
    return jnp.where(mask, values, jnp.zeros_like(values))


def attend_forward_kernel(seg_row, seg_col, q_ref, k_ref, v_ref, out_ref, log_ref, bias):
    @pl.when(pl.program_id(0) == 0)
    def _():
        fill_bias(seg_row, seg_col, bias)

    masks = lane_masks((k_ref.shape[0], PAIR))
    keys_masked = [masked_to(k_ref[...], mask) for mask in masks]
    for (first, rows, key_low, key_high), start in zip(VISIBLE, TILE_STARTS):
        queries = q_ref[first : first + rows, :] * jnp.asarray(HD**-0.5, low)
        values = v_ref[key_low:key_high, :]
        mixed = []
        for head in range(2):
            scores = dot_nt(keys_masked[head][key_low:key_high], queries)
            scores = scores + bias[start : start + key_high - key_low, 0:rows]
            highest = jnp.max(scores, axis=0, keepdims=True)
            exponent = jnp.exp(scores - highest)
            totals = jnp.sum(exponent, axis=0, keepdims=True)
            soft = (exponent * (1.0 / totals)).astype(low)
            mixed.append(dot_tn(soft, values))
            log_ref[0, head : head + 1, first : first + rows] = highest + jnp.log(totals)
        half = lane_masks((rows, PAIR))[0]
        out_ref[first : first + rows, :] = jnp.where(half, mixed[0], mixed[1]).astype(low)


def attend_backward_kernel(
    seg_row, seg_col, q_ref, k_ref, v_ref, log_ref, do_ref, dq_ref, dk_ref, dv_ref, bias, dk_acc, dv_acc
):
    @pl.when(pl.program_id(0) == 0)
    def _():
        fill_bias(seg_row, seg_col, bias)

    masks = lane_masks((k_ref.shape[0], PAIR))
    keys_masked = [masked_to(k_ref[...], mask) for mask in masks]
    values_masked = [masked_to(v_ref[...], mask) for mask in masks]
    dk_acc[...] = jnp.zeros_like(dk_acc)
    dv_acc[...] = jnp.zeros_like(dv_acc)
    for (first, rows, key_low, key_high), start in zip(VISIBLE, TILE_STARTS):
        queries = q_ref[first : first + rows, :] * jnp.asarray(HD**-0.5, low)
        grads = do_ref[first : first + rows, :]
        grad_query = jnp.zeros((rows, PAIR), jnp.float32)
        row_masks = lane_masks((rows, PAIR))
        for head in range(2):
            keys = keys_masked[head][key_low:key_high]
            scores = dot_nt(keys, queries)
            scores = scores + bias[start : start + key_high - key_low, 0:rows]
            soft = jnp.exp(scores - log_ref[0, head : head + 1, first : first + rows])
            grad_soft = dot_nt(values_masked[head][key_low:key_high], grads)
            inner = jnp.sum(soft * grad_soft, axis=0, keepdims=True)
            grad_scores = (soft * (grad_soft - inner)).astype(low)
            dv_acc[key_low:key_high, :] += dot_nn(
                soft.astype(low), masked_to(grads, row_masks[head])
            )
            dk_acc[key_low:key_high, :] += dot_nn(
                grad_scores, masked_to(queries, row_masks[head])
            )
            grad_query = grad_query + dot_tn(grad_scores, keys)
        dq_ref[first : first + rows, :] = (grad_query * HD**-0.5).astype(low)
    dk_ref[...] = dk_acc[...].astype(low)
    dv_ref[...] = dv_acc[...].astype(low)


def attend_specs(length, pairs):
    whole = lambda shape: pl.BlockSpec(shape, lambda j: (0,) * len(shape))
    columns = lambda offset: pl.BlockSpec((length, PAIR), lambda j, offset=offset: (0, offset + j))
    logs = pl.BlockSpec((1, 8, length), lambda j: (j, 0, 0))
    return whole, columns, logs


def attend_forward(seg_row, seg_col, projected):
    length = projected.shape[0]
    pairs = projected.shape[1] // (3 * PAIR)
    whole, columns, logs = attend_specs(length, pairs)
    return pl.pallas_call(
        attend_forward_kernel,
        grid=(pairs,),
        in_specs=[
            whole((1, length)),
            whole((length, 1)),
            columns(0),
            columns(pairs),
            columns(2 * pairs),
        ],
        out_specs=[columns(0), logs],
        out_shape=[
            jax.ShapeDtypeStruct((length, pairs * PAIR), low),
            jax.ShapeDtypeStruct((pairs, 8, length), jnp.float32),
        ],
        scratch_shapes=[pltpu.VMEM((tile_total, 256), jnp.float32)],
        compiler_params=pltpu.CompilerParams(vmem_limit_bytes=vmem_bytes),
        cost_estimate=pl.CostEstimate(
            flops=4 * length * length * pairs * PAIR, bytes_accessed=8 * length * pairs * PAIR,
            transcendentals=length * length * pairs,
        ),
        name="attend_forward",
    )(seg_row, seg_col, projected, projected, projected)


def attend_backward(seg_row, seg_col, projected, logs_all, grad_mixture):
    length = projected.shape[0]
    pairs = projected.shape[1] // (3 * PAIR)
    whole, columns, logs = attend_specs(length, pairs)
    return pl.pallas_call(
        attend_backward_kernel,
        grid=(pairs,),
        in_specs=[
            whole((1, length)),
            whole((length, 1)),
            columns(0),
            columns(pairs),
            columns(2 * pairs),
            logs,
            columns(0),
        ],
        out_specs=[columns(0)] * 3,
        out_shape=[jax.ShapeDtypeStruct((length, pairs * PAIR), low)] * 3,
        scratch_shapes=[
            pltpu.VMEM((tile_total, 256), jnp.float32),
            pltpu.VMEM((length, PAIR), jnp.float32),
            pltpu.VMEM((length, PAIR), jnp.float32),
        ],
        compiler_params=pltpu.CompilerParams(vmem_limit_bytes=vmem_bytes),
        cost_estimate=pl.CostEstimate(
            flops=10 * length * length * pairs * PAIR, bytes_accessed=14 * length * pairs * PAIR,
            transcendentals=length * length * pairs,
        ),
        name="attend_backward",
    )(seg_row, seg_col, projected, projected, projected, logs_all, grad_mixture)


def feed_kernel(block_count, *refs):
    refs = list(refs)
    take = lambda count: [refs.pop(0) for _ in range(count)]
    normed = [ref[...] for ref in take(2)]
    tops = [ref[...] for ref in take(2)]
    blocks = [take(2) for _ in range(block_count)]
    bias_ref = take(1)[0]
    reduced, reduced_out, back, back_out = take(4)
    outs = [take(2) for _ in range(block_count)]
    dbu_ref = take(1)[0]
    turned, weights, grads, reduced_sum, back_sum, in_sems, out_sems = refs
    owners, depth, units = weights.shape[2:]
    side_rows = units // (2 * owners)
    split = depth - 2 * side_rows
    arrivals = [
        [
            pltpu.make_async_copy(parts[part], weights.at[index, part], in_sems.at[index, part])
            for part in range(2)
        ]
        for index, parts in enumerate(blocks)
    ]
    for copies in arrivals:
        for copy in copies:
            copy.start()
    rows = normed[0].shape[0]
    reduced_sums = (reduced, reduced_sum)
    back_sums = (back, back_sum)
    for side in range(2):
        turned[:, side * rows : (side + 1) * rows] = normed[side].T
    departures = []
    for index, grad_refs in enumerate(outs):
        for copy in arrivals[index]:
            copy.wait()
        places = [(part, owner) for part in range(2) for owner in range(owners)]
        expand = jnp.concatenate([weights[index, part, owner, :split] for part, owner in places], axis=0)
        reduce = jnp.concatenate(
            [
                jnp.concatenate(
                    [
                        weights[index, part, owner, split : split + side_rows],
                        weights[index, part, owner, split + side_rows :],
                    ],
                    axis=1,
                )
                for part, owner in places
            ],
            axis=0,
        )
        hiddens, slopes = [], []
        for side in range(2):
            expanded = dot_nn(normed[side], expand) + bias_ref[index : index + 1, :]
            phi = 0.5 + 0.5 * lax.erf(expanded * (0.5**0.5))
            density = jnp.exp(-0.5 * expanded * expanded) * 0.3989422804014327
            hiddens.append((expanded * phi).astype(low))
            grad_hidden = dot_nt(tops[side], reduce)
            slopes.append((grad_hidden * (phi + expanded * density)).astype(low))
        for side in range(2):
            down = dot_nn(hiddens[side], reduce)
            up = dot_nt(slopes[side], expand)
            if index:
                reduced_sums[side][...] += down
                back_sums[side][...] += up
            else:
                reduced_sums[side][...] = down
                back_sums[side][...] = up
        grad_both = jnp.concatenate(slopes, axis=0)
        grad_reduce = sum(dot_tn(hiddens[side], tops[side]) for side in range(2)).astype(low)
        for place, (part, owner) in enumerate(places):
            grads[index, part, owner, :split] = dot_nn(
                turned[place * split : (place + 1) * split, :], grad_both
            ).astype(low)
            rows_down = grad_reduce[place * side_rows : (place + 1) * side_rows]
            grads[index, part, owner, split : split + side_rows] = rows_down[:, :units]
            grads[index, part, owner, split + side_rows :] = rows_down[:, units:]
        dbu_ref[index : index + 1, :] = jnp.sum(grad_both.astype(jnp.float32), axis=0, keepdims=True)
        for part in range(2):
            departures.append(
                pltpu.make_async_copy(
                    grads.at[index, part], grad_refs[part], out_sems.at[index, part]
                )
            )
            departures[-1].start()
    reduced_out[...] = reduced_sum[...].astype(low)
    back_out[...] = back_sum[...].astype(low)
    for copy in departures:
        copy.wait()


def feed_blocks(normed, tops, blocks, biases):
    rows, features = normed[0].shape
    count = len(blocks)
    units = biases.shape[1]
    operands = [*normed, *tops]
    in_vmem = pl.BlockSpec(memory_space=pltpu.VMEM)
    anywhere = pl.BlockSpec(memory_space=pl.ANY)
    sum_shape = jax.ShapeDtypeStruct((rows, features), jnp.float32)
    sent_shape = jax.ShapeDtypeStruct((rows, features), low)
    shapes = [sum_shape, sent_shape, sum_shape, sent_shape]
    for parts in blocks:
        operands += parts
        shapes += [jax.ShapeDtypeStruct(part.shape, low) for part in parts]
    operands += [biases]
    shapes += [jax.ShapeDtypeStruct(biases.shape, jnp.float32)]
    part_shape = blocks[0][0].shape
    results = pl.pallas_call(
        partial(feed_kernel, count),
        in_specs=[in_vmem] * 4 + [anywhere] * (2 * count) + [in_vmem],
        out_specs=[in_vmem] * 4 + [anywhere] * (2 * count) + [in_vmem],
        out_shape=shapes,
        scratch_shapes=[
            pltpu.VMEM((features, 2 * rows), low),
            pltpu.VMEM((count, 2) + part_shape, low),
            pltpu.VMEM((count, 2) + part_shape, low),
            pltpu.VMEM((rows, features), jnp.float32),
            pltpu.VMEM((rows, features), jnp.float32),
            pltpu.SemaphoreType.DMA((count, 2)),
            pltpu.SemaphoreType.DMA((count, 2)),
        ],
        compiler_params=pltpu.CompilerParams(vmem_limit_bytes=vmem_bytes),
        cost_estimate=pl.CostEstimate(
            flops=24 * rows * features * units * count,
            bytes_accessed=8 * features * units * count,
            transcendentals=4 * rows * units * count,
        ),
        name="feed_blocks",
    )(*operands)
    grads = [results[4 + 2 * index : 6 + 2 * index] for index in range(count)]
    return results[:4], grads, results[-1]


def renew_into(sources, targets, gradient, step_rate, place=Ellipsis):
    weight, moment, second = (ref[place] for ref in sources)
    results = adamw_step(weight, moment, second, gradient, step_rate, decay_rate)
    for ref, result in zip(targets, results):
        ref[place] = result


def renew_feed_kernel(place_ref, mine, other, *refs):
    expand_in, reduce_in, expand_out, reduce_out = (refs[3 * i : 3 * i + 3] for i in range(4))
    pieces, expand_grad = refs[12:]
    step = pl.program_id(0)
    groups, depth, units = mine.shape
    owners, owned, features = expand_grad.shape
    units_piece = units // owners

    @pl.when(step == 0)
    def _():
        group, core = place_ref[0], place_ref[1]
        for offset in range(groups):
            slot = 2 * (group ^ offset)
            pieces[slot + core] = mine[offset]
            pieces[slot + 1 - core] = other[offset]
        for owner in range(owners):
            expand_grad[owner] = jnp.concatenate(
                [
                    pieces[slot, :owned, owner * units_piece : (owner + 1) * units_piece].astype(
                        jnp.float32
                    )
                    for slot in range(2 * groups)
                ],
                axis=1,
            )

    renew_into(expand_in, expand_out, expand_grad[step], 0.03)
    slots = 2 * groups // owners
    for index in range(slots):
        slot = slots * step + index
        gradient = jnp.concatenate(
            [pieces[slot, owned : owned + units_piece], pieces[slot, owned + units_piece :]],
            axis=1,
        )
        rows = slice(index * units_piece, (index + 1) * units_piece)
        renew_into(reduce_in, reduce_out, gradient.astype(jnp.float32), 0.02, (rows, slice(None)))


def renew_feed(place, mine, other, expand_state, reduce_state):
    groups, depth, units = mine.shape
    owned, hidden_count = expand_state[0].shape
    owned_units, features = reduce_state[0].shape
    owners = hidden_count // owned_units
    whole = pl.BlockSpec(mine.shape, lambda j, _: (0, 0, 0))
    across = pl.BlockSpec((owned, owned_units), lambda j, _: (0, j))
    down = pl.BlockSpec((owned_units // owners, features), lambda j, _: (j, 0))
    shapes = [jax.ShapeDtypeStruct(array.shape, jnp.float32) for array in expand_state]
    shapes += [jax.ShapeDtypeStruct(array.shape, jnp.float32) for array in reduce_state]
    results = pl.pallas_call(
        renew_feed_kernel,
        grid_spec=pltpu.PrefetchScalarGridSpec(
            num_scalar_prefetch=1,
            grid=(owners,),
            in_specs=[whole] * 2 + [across] * 3 + [down] * 3,
            out_specs=[across] * 3 + [down] * 3,
            scratch_shapes=[
                pltpu.VMEM((2 * groups, depth, units), low),
                pltpu.VMEM((owners, owned, owned_units), jnp.float32),
            ],
        ),
        out_shape=shapes,
        compiler_params=pltpu.CompilerParams(vmem_limit_bytes=vmem_bytes),
        cost_estimate=pl.CostEstimate(
            flops=40 * owned * hidden_count, bytes_accessed=48 * owned * hidden_count,
            transcendentals=4 * owned * hidden_count,
        ),
        name="renew_feed",
    )(place, mine, other, *expand_state, *reduce_state)
    return results[:3], results[3:]


def renew_first_kernel(place_ref, mine, other, *refs):
    inputs_in, output_in, inputs_out, output_out = (refs[3 * i : 3 * i + 3] for i in range(4))
    (pieces,) = refs[12:]
    step = pl.program_id(0)
    groups = mine.shape[0]
    group, core = place_ref[0], place_ref[1]
    for offset in range(groups):
        pieces[core, group ^ offset] = mine[offset]
        pieces[1 - core, group ^ offset] = other[offset]
    rows, half = pieces.shape[2:]
    gradient = jnp.concatenate(
        [pieces[side].reshape(groups * rows, half) for side in range(2)], axis=1
    ).astype(jnp.float32)

    @pl.when(step < 3)
    def _():
        renew_into(inputs_in, inputs_out, gradient, 0.03)

    @pl.when(step == 3)
    def _():
        renew_into(output_in, output_out, gradient, 0.3)


def renew_first(place, mine, other, inputs_state, output_state):
    groups, rows, _ = mine.shape
    owned, features = output_state[0].shape
    half = features // 2
    piece = pl.BlockSpec((groups, rows, half), lambda j, _: (0, 0, j))
    across = pl.BlockSpec((owned, features), lambda j, _: (0, jnp.minimum(j, 2)))
    whole = pl.BlockSpec((owned, features), lambda j, _: (0, 0))
    shapes = [jax.ShapeDtypeStruct(array.shape, jnp.float32) for array in inputs_state]
    shapes += [jax.ShapeDtypeStruct(array.shape, jnp.float32) for array in output_state]
    results = pl.pallas_call(
        renew_first_kernel,
        grid_spec=pltpu.PrefetchScalarGridSpec(
            num_scalar_prefetch=1,
            grid=(4,),
            in_specs=[piece] * 2 + [across] * 3 + [whole] * 3,
            out_specs=[across] * 3 + [whole] * 3,
            scratch_shapes=[pltpu.VMEM((2, groups, rows, half), low)],
        ),
        out_shape=shapes,
        compiler_params=pltpu.CompilerParams(vmem_limit_bytes=vmem_bytes),
        cost_estimate=pl.CostEstimate(
            flops=80 * owned * features, bytes_accessed=96 * owned * features,
            transcendentals=8 * owned * features,
        ),
        name="renew_first",
    )(place, mine, other, *inputs_state, *output_state)
    return results[:3], results[3:]


def chip_routes(dp_count, seq_count):
    straight, crossed = [], []
    for place in range(dp_count):
        group, core = place - place % 2, place % 2
        for quarter in range(seq_count):
            source = place * seq_count + quarter
            holder = (group + quarter // 2) * seq_count
            straight.append((source, holder + 2 * core + quarter % 2))
            crossed.append((source, holder + 2 * core + 1 - quarter % 2))
    return straight, crossed


def on_device(
    dp_count,
    seq_count,
    activations,
    cotangent,
    segment_ids,
    inputs_weight,
    inputs_moment,
    inputs_second,
    output_weight,
    output_moment,
    output_second,
    expand_weight,
    expand_moment,
    expand_second,
    reduce_weight,
    reduce_moment,
    reduce_second,
    vector_params,
    vector_moment,
    vector_second,
):
    axes = ("dp", "seq")
    dp_index = lax.axis_index("dp")
    seq_index = lax.axis_index("seq")
    core = dp_index % 2
    group = dp_index // 2
    groups = dp_count // 2
    four_chips = groups == 4
    odd = seq_index % 2
    features = activations.shape[2]
    quarter = activations.shape[1]
    half = features // 2
    owned = inputs_weight.shape[0]
    owned_units = reduce_weight.shape[0]
    rows_piece = owned // groups
    units_piece = owned_units // dp_count
    vector_rows = vector_params.shape[0]
    straight, crossed = chip_routes(dp_count, seq_count)
    core_pairs = [(place, place ^ 1) for place in range(dp_count)]
    x_pairs = [(place, place ^ 2) for place in range(dp_count)]
    y_pairs = [(place, place ^ 4) for place in range(dp_count)]
    far_pairs = [(place, place ^ 6) for place in range(dp_count)]
    same_core = [list(range(first, dp_count, 2)) for first in range(2)]

    def to_chip(values):
        near = lax.dynamic_index_in_dim(values, odd, 0, keepdims=False)
        far = lax.dynamic_index_in_dim(values, 1 - odd, 0, keepdims=False)
        near = lax.ppermute(near, axes, straight)
        far = lax.ppermute(far, axes, crossed)
        return jnp.concatenate(
            [jnp.where(odd == 0, near, far), jnp.where(odd == 0, far, near)], axis=0
        )

    def from_chip(values):
        near = lax.dynamic_slice_in_dim(values, odd * quarter, quarter, 0)
        far = lax.dynamic_slice_in_dim(values, (1 - odd) * quarter, quarter, 0)
        near = lax.ppermute(near, axes, [(there, here) for here, there in straight])
        far = lax.ppermute(far, axes, [(there, here) for here, there in crossed])
        return jnp.stack([jnp.where(odd == 0, near, far), jnp.where(odd == 0, far, near)])

    def swap_cores(values):
        return lax.ppermute(values, "dp", core_pairs)

    def via_x(values):
        return lax.ppermute(values, "dp", x_pairs)

    def via_y(values):
        return lax.ppermute(values, "dp", y_pairs)

    def by_core(mine, theirs, axis):
        return jnp.where(
            core == 0,
            jnp.concatenate([mine, theirs], axis=axis),
            jnp.concatenate([theirs, mine], axis=axis),
        )

    def add_low(*terms):
        return sum(term.astype(jnp.float32) for term in terms).astype(low)

    def after(values, *gates):
        return lax.optimization_barrier((values, gates))[0]

    def gather_z(piece):
        parts = [piece]
        for shift in range(1, seq_count):
            ring = [(place, (place + shift) % seq_count) for place in range(seq_count)]
            parts.append(lax.ppermute(piece, "seq", ring))
        placed = [
            lax.select_n((seq_index - owner) % seq_count, *parts) for owner in range(seq_count)
        ]
        middle = seq_count // 2
        return jnp.stack(placed[:middle]), jnp.stack(placed[middle:])

    def gather_chips(halves):
        first, second = halves
        x_first, y_second = via_x(first), via_y(second)
        x_second, y_first = via_x(second), via_y(first)
        return halves, (x_first, x_second), (y_first, y_second), (via_y(x_first), via_x(y_second))

    def in_order(own, from_x, from_y, from_far, axis):
        x_set = group % 2 == 1
        y_set = group // 2 == 1
        near_low = jnp.where(x_set, from_x, own)
        near_high = jnp.where(x_set, own, from_x)
        far_low = jnp.where(x_set, from_far, from_y)
        far_high = jnp.where(x_set, from_y, from_far)
        return jnp.stack(
            [
                jnp.where(y_set, far_low, near_low),
                jnp.where(y_set, far_high, near_high),
                jnp.where(y_set, near_low, far_low),
                jnp.where(y_set, near_high, far_high),
            ],
            axis=axis,
        )

    def scatter_begin(own, to_x, to_y, to_far):
        far_first, far_second = via_x(to_far[0]), via_y(to_far[1])
        return (own, to_x, to_y, far_first, far_second, via_x(to_x[0]), via_y(to_y[1]))

    def scatter_middle(state, *gates):
        own, to_x, to_y, far_first, far_second, x_first, y_second = state
        far_first, far_second = after((far_first, far_second), *gates)
        y_first = add_low(to_y[0], far_first)
        x_second = add_low(to_x[1], far_second)
        return (own, x_first, via_x(x_second), via_y(y_first), y_second), (y_first, x_second)

    def scatter_end(state):
        own, x_first, x_second, y_first, y_second = state
        first = add_low(own[0], x_first, y_first)
        second = add_low(own[1], x_second, y_second)
        return jnp.concatenate([first, second], axis=0)

    def scatter_z_begin(blocks):
        parts = [lax.dynamic_index_in_dim(blocks, seq_index, 0, keepdims=False)]
        for shift in range(1, seq_count):
            target = (seq_index + shift) % seq_count
            sent = lax.dynamic_index_in_dim(blocks, target, 0, keepdims=False)
            ring = [(place, (place + shift) % seq_count) for place in range(seq_count)]
            parts.append(lax.ppermute(sent, "seq", ring))
        return parts

    def scatter_z(blocks):
        return add_low(*scatter_z_begin(blocks))

    def regather_begin(piece):
        return piece, via_x(piece), via_y(piece), lax.ppermute(piece, "dp", far_pairs)

    def regather_end(state):
        mine = in_order(*state, 0)
        return by_core(mine[:, None], swap_cores(mine)[:, None], 1)

    def regather(piece):
        every = lax.all_gather(piece, "dp", axis=0, tiled=False)
        return every.reshape((groups, 2) + piece.shape)

    def corner(weight, column):
        return lax.dynamic_slice(
            weight, (group * rows_piece, column + core * half), (rows_piece, half)
        ).astype(low)

    vector_piece = lax.dynamic_slice_in_dim(vector_params, group * rows_piece, rows_piece, 1)
    first_piece = jnp.concatenate(
        [
            corner(inputs_weight, 0),
            corner(inputs_weight, features),
            corner(inputs_weight, 2 * features),
            corner(output_weight, 0),
            jnp.pad(vector_piece.T.astype(low), ((0, 0), (0, LANES - vector_rows))),
        ],
        axis=1,
    )
    expand_piece = jnp.concatenate(
        [
            lax.dynamic_slice_in_dim(
                expand_weight, owner * owned_units + dp_index * units_piece, units_piece, 1
            ).astype(low)
            for owner in range(seq_count)
        ],
        axis=1,
    )
    reduce_piece = lax.dynamic_slice_in_dim(
        reduce_weight, dp_index * units_piece, units_piece, 0
    ).astype(low)

    def pack(expand, reduce):
        return jnp.concatenate([expand, reduce[..., :half], reduce[..., half:]], axis=-2)

    residual_low = to_chip(activations)
    first_block = gather_z(first_piece)
    if four_chips:
        feed_piece = after(pack(expand_piece, reduce_piece), first_block)
        feed_all = lax.all_gather(feed_piece, "seq", axis=0, tiled=False)
        feed_halves = (feed_all[: seq_count // 2], feed_all[seq_count // 2 :])
        cotangent = after(cotangent, feed_halves)
    grad_top = to_chip(cotangent)
    rows_here = residual_low.shape[0]
    residual_other = swap_cores(residual_low)
    grad_top_other = swap_cores(grad_top)
    other_segments = swap_cores(segment_ids)
    segment_pair = jnp.where(seq_index // 2 == core, segment_ids, other_segments)
    segments = lax.dynamic_index_in_dim(segment_pair, odd, 0, keepdims=False)
    seg_row, seg_col = segments[None, :], segments[:, None]

    if four_chips:
        every_first = gather_chips(first_block)
        first_low = jnp.concatenate(
            [in_order(*[block[part] for block in every_first], 1) for part in range(2)], axis=0
        )
    else:
        first_low = lax.all_gather(
            jnp.concatenate(first_block, axis=0),
            "dp",
            axis=1,
            tiled=False,
            axis_index_groups=same_core,
        )
    first_low = first_low.reshape(features, first_low.shape[-1])
    wide = 3 * half
    inputs_low = first_low[:, :wide]
    output_half = first_low[:, wide : wide + half]
    output_all = by_core(output_half, swap_cores(output_half), 1)
    vectors = first_low[:, wide + half : wide + half + vector_rows].T.astype(jnp.float32)

    expand_bias = vectors[8:].reshape(seq_count, dp_count, units_piece)
    block_units = seq_count * owned_units // 8
    if four_chips:
        blocks = gather_chips(feed_halves)
        biases = jnp.stack(
            [
                lax.dynamic_index_in_dim(
                    expand_bias, dp_index ^ (2 * offset), 1, keepdims=False
                ).reshape(block_units)
                for offset in range(4)
            ]
        )
    else:
        expand_all = lax.all_gather(
            jnp.concatenate(gather_z(expand_piece), axis=0).reshape(features, -1),
            "dp",
            axis=1,
            axis_index_groups=same_core,
        ).reshape(seq_count, owned, 4, block_units)
        reduce_all = lax.all_gather(
            jnp.concatenate(gather_z(reduce_piece), axis=0).reshape(-1, features),
            "dp",
            axis=0,
            axis_index_groups=same_core,
        ).reshape(4, seq_count, -1, features)
        picked = lax.dynamic_index_in_dim(
            expand_bias.reshape(seq_count, groups, 2, units_piece), core, 2, keepdims=False
        )
        biases = picked.transpose(1, 0, 2).reshape(4, block_units)
        blocks = []
        for index in range(4):
            packed = pack(expand_all[:, :, index], reduce_all[index])
            blocks.append((packed[: seq_count // 2], packed[seq_count // 2 :]))

    def tokens_of(values, which):
        return lax.dynamic_slice_in_dim(values, which * rows_here, rows_here, 0)

    def heads_part(vector):
        return lax.dynamic_slice_in_dim(vector, core * half, half, 0)

    unit_all, _ = normalize(by_core(residual_low, residual_other, 0).astype(jnp.float32))
    normed_one = (unit_all * vectors[0] + vectors[1]).astype(low)
    input_bias = jnp.concatenate(
        [heads_part(vectors[4]), jnp.zeros((half,), jnp.float32), heads_part(vectors[5])]
    )
    projected = (dot_nn(normed_one, inputs_low) + input_bias).astype(low)
    if four_chips:
        projected = after(projected, feed_halves)
    mixture_heads, logs_all = attend_forward(seg_row, seg_col, projected)
    if four_chips:
        mixture_heads = after(mixture_heads, grad_top, blocks[1][0], blocks[2][1])
    mixture_theirs = swap_cores(tokens_of(mixture_heads, 1 - core))
    mixture = by_core(tokens_of(mixture_heads, core), mixture_theirs, 1)

    residual = residual_low.astype(jnp.float32)
    middle = residual + (dot_nn(mixture, output_all) + vectors[6])
    unit_two, inverse_two = normalize(middle)
    normed_two = (unit_two * vectors[2] + vectors[3]).astype(low)
    normed_pair = (normed_two, swap_cores(normed_two))
    top_pair = (grad_top, grad_top_other)
    sums, grads, bias_grads = feed_blocks(normed_pair, top_pair, blocks, biases)
    grad_normed_two = sums[2] + swap_cores(sums[3]).astype(jnp.float32)
    reduced = sums[0] + swap_cores(sums[1]).astype(jnp.float32)
    output_low = (middle + (reduced + vectors[7])).astype(low)

    if four_chips:
        feed_state = scatter_begin(*grads)
        place = jnp.arange(dp_count)[None, :, None]
        bias_sums = sum(
            jnp.where(
                place == (dp_index ^ (2 * offset)),
                bias_grads[offset].reshape(seq_count, 1, units_piece),
                0.0,
            )
            for offset in range(4)
        )
    else:
        packed = [jnp.concatenate(grad, axis=0) for grad in grads]
        expand_sum = jnp.stack([part[:, :owned] for part in packed], axis=2)
        expand_sum = expand_sum.reshape(features, groups, -1).transpose(1, 0, 2)
        expand_sum = lax.psum_scatter(expand_sum, "dp", axis_index_groups=same_core)
        reduce_sum = [part[:, owned:].reshape(seq_count, 2, -1, half) for part in packed]
        reduce_sum = jnp.stack([part.transpose(0, 2, 1, 3) for part in reduce_sum])
        reduce_sum = reduce_sum.reshape(groups, -1, features)
        reduce_sum = lax.psum_scatter(reduce_sum, "dp", axis_index_groups=same_core)
        bias_sums = bias_grads.reshape(groups, seq_count, units_piece).transpose(1, 0, 2)
        is_core = jnp.arange(2)[None, None, :, None] == core
        bias_sums = jnp.where(is_core, bias_sums[:, :, None, :], 0.0)

    grad_middle = grad_top.astype(jnp.float32) + norm_back(
        grad_normed_two, vectors[2], unit_two, inverse_two
    )
    grad_attended = grad_middle.astype(low)
    grad_output = dot_tn(mixture, grad_attended).astype(low)
    grad_mixture = dot_nt(grad_attended, output_all).astype(low)

    def columns_of(values, which):
        return lax.dynamic_slice_in_dim(values, which * half, half, 1)

    grad_theirs = swap_cores(columns_of(grad_mixture, 1 - core))
    grad_joined = by_core(columns_of(grad_mixture, core), grad_theirs, 0)
    if four_chips:
        feed_state, gates = scatter_middle(feed_state, grad_mixture)
        grad_joined = after(grad_joined, *gates)
    layer_output = from_chip(output_low)
    grad_heads = attend_backward(seg_row, seg_col, projected, logs_all, grad_joined)
    output_sum = add_low(
        columns_of(grad_output, core), swap_cores(columns_of(grad_output, 1 - core))
    )
    grad_projected = jnp.concatenate(grad_heads, axis=1)
    if four_chips:
        feed_state, layer_output = after((feed_state, layer_output), grad_projected)
        feed_sum = scatter_end(feed_state)
        feed_parts = scatter_z_begin(feed_sum)
        grad_projected = after(grad_projected, feed_sum, layer_output)
    grad_inputs = dot_tn(normed_one, grad_projected).astype(low)
    grad_normed_all = dot_nt(grad_projected, inputs_low)
    grad_normed_one = tokens_of(grad_normed_all, core) + swap_cores(
        tokens_of(grad_normed_all, 1 - core).astype(low)
    ).astype(jnp.float32)
    unit_one, inverse_one = normalize(residual)
    grad_residual = norm_back(grad_normed_one, vectors[0], unit_one, inverse_one)
    input_grad = (grad_middle + grad_residual).astype(low)

    def heads_sum(values):
        return lax.dynamic_update_slice_in_dim(
            jnp.zeros((features,), jnp.float32), column_sum(values), core * half, 0
        )

    head_rows = jnp.stack(
        [
            column_sum(grad_normed_one * unit_one),
            column_sum(grad_normed_one),
            column_sum(grad_normed_two * unit_two),
            column_sum(grad_normed_two),
            heads_sum(grad_heads[0]),
            heads_sum(grad_heads[2]),
            column_sum(grad_attended),
            column_sum(grad_top),
        ]
    )
    grad_vectors = jnp.concatenate([head_rows, bias_sums.reshape(-1, features)], axis=0)
    vector_columns = jnp.pad(grad_vectors.T.astype(low), ((0, 0), (0, LANES - vector_rows)))
    first_grad = jnp.concatenate([grad_inputs, output_sum, vector_columns], axis=1)
    first_grad = first_grad.reshape(seq_count, groups, rows_piece, -1)
    if four_chips:
        middle_owner = seq_count // 2
        split = []
        for offset in range(4):
            split.append(
                [
                    lax.dynamic_index_in_dim(part, group ^ offset, 1, keepdims=False)
                    for part in (first_grad[:middle_owner], first_grad[middle_owner:])
                ]
            )
        first_state = scatter_begin(*after(split, feed_parts))
        feed_piece = add_low(*feed_parts)
        first_state, gates = scatter_middle(first_state, feed_piece)
        feed_pieces = regather_begin(after(feed_piece, *gates))
        first_parts = scatter_z_begin(scatter_end(first_state))
        feed_mine = jnp.stack(feed_pieces)
        feed_other = swap_cores(feed_mine)
        place = jnp.stack([group, core]).astype(jnp.int32)
        new_expand, new_reduce = renew_feed(
            place,
            feed_mine,
            feed_other,
            (expand_weight, expand_moment, expand_second),
            (reduce_weight, reduce_moment, reduce_second),
        )
        first_parts = after(first_parts, new_expand)
        first_piece_sum = add_low(*first_parts)
        first_pieces = regather_begin(first_piece_sum)
        input_grad = from_chip(after(input_grad, first_piece_sum))
        first_mine = jnp.stack(first_pieces)
        first_other = swap_cores(first_mine)
        new_inputs, new_output = renew_first(
            place,
            first_mine,
            first_other,
            (inputs_weight, inputs_moment, inputs_second),
            (output_weight, output_moment, output_second),
        )
        vector_slice = slice(wide + half, wide + half + vector_rows)
        vector_parts = first_mine[..., vector_slice].astype(jnp.float32) + first_other[
            ..., vector_slice
        ].astype(jnp.float32)
        sum_vectors = in_order(*[vector_parts[offset] for offset in range(4)], 0)
        sum_vectors = sum_vectors.reshape(owned, vector_rows).T
    else:
        first_sum = lax.psum_scatter(
            first_grad, "dp", scatter_dimension=1, axis_index_groups=same_core
        )
        input_grad = from_chip(input_grad)
        every_first = regather(scatter_z(first_sum))
        sum_expand = regather(scatter_z(expand_sum.reshape(seq_count, owned, -1)))
        sum_reduce = regather(scatter_z(reduce_sum.reshape(seq_count, units_piece, features)))
    def renew(weight, moment, second, gradient, step_rate, weight_decay):
        return adamw_step(
            weight, moment, second, gradient.astype(jnp.float32), step_rate, weight_decay
        )

    if not four_chips:
        sum_expand = sum_expand.reshape(dp_count, owned, seq_count, units_piece)
        sum_expand = sum_expand.transpose(1, 2, 0, 3).reshape(expand_weight.shape)
        sum_reduce = sum_reduce.reshape(reduce_weight.shape)
        sum_first = every_first.transpose(0, 2, 1, 3)
        sum_inputs = sum_first[..., :wide].reshape(groups, rows_piece, 2, 3, half)
        sum_inputs = sum_inputs.transpose(0, 1, 3, 2, 4).reshape(inputs_weight.shape)
        sum_output = sum_first[..., wide : wide + half].reshape(output_weight.shape)
        sum_vectors = sum_first[..., wide + half : wide + half + vector_rows].astype(jnp.float32)
        sum_vectors = jnp.sum(sum_vectors, axis=2).reshape(owned, vector_rows).T
        new_inputs = renew(inputs_weight, inputs_moment, inputs_second, sum_inputs, 0.03, decay_rate)
        new_output = renew(output_weight, output_moment, output_second, sum_output, 0.3, decay_rate)
        new_expand = renew(expand_weight, expand_moment, expand_second, sum_expand, 0.03, decay_rate)
        new_reduce = renew(reduce_weight, reduce_moment, reduce_second, sum_reduce, 0.02, decay_rate)
    new_vectors = renew(vector_params, vector_moment, vector_second, sum_vectors, 0.5, 0.0)
    return (
        layer_output,
        input_grad,
        *new_inputs,
        *new_output,
        *new_expand,
        *new_reduce,
        *new_vectors,
    )


def solution(mesh):
    tokens = P("dp", "seq", None)
    rows = P("seq", None)
    columns = P(None, "seq")
    in_specs = (tokens, tokens, P("dp", None)) + (rows,) * 12 + (columns,) * 3
    out_specs = (tokens, tokens) + (rows,) * 12 + (columns,) * 3
    return jax.shard_map(
        partial(on_device, mesh.shape["dp"], mesh.shape["seq"]),
        mesh=mesh,
        in_specs=in_specs,
        out_specs=out_specs,
        check_vma=False,
    )
```

```python
from functools import partial

import jax
import jax.numpy as jnp
from jax import lax
from jax.experimental import pallas as pl
from jax.experimental.pallas import tpu as pltpu
from jax.sharding import PartitionSpec as P

HEADS = 12
HD = 64
STEP = 10
PAIR = 2 * HD
LANES = 128

eps_norm = 1e-05
eps_adam = 1e-08
beta_one = 0.9
beta_two = 0.95
decay_rate = 0.1
mask_fill = -1e30
vmem_bytes = 56 * 1024 * 1024

VISIBLE = (
    (0, 256, 0, 256),
    (256, 256, 128, 512),
    (512, 256, 128, 768),
    (768, 128, 128, 896),
    (896, 128, 768, 1024),
)
TILE_STARTS = []
tile_total = 0
for _first, _rows, _low, _high in VISIBLE:
    TILE_STARTS.append(tile_total)
    tile_total += _high - _low

low = jnp.bfloat16


def dot_nn(left_side, right_side):
    return lax.dot_general(
        left_side, right_side, (((1,), (0,)), ((), ())), preferred_element_type=jnp.float32
    )


def dot_tn(left_side, right_side):
    return lax.dot_general(
        left_side, right_side, (((0,), (0,)), ((), ())), preferred_element_type=jnp.float32
    )


def dot_nt(left_side, right_side):
    return lax.dot_general(
        left_side, right_side, (((1,), (1,)), ((), ())), preferred_element_type=jnp.float32
    )


def normalize(values):
    center = jnp.mean(values, axis=-1, keepdims=True)
    offsets = values - center
    spread = jnp.mean(offsets * offsets, axis=-1, keepdims=True)
    inverse = lax.rsqrt(spread + eps_norm)
    return offsets * inverse, inverse


def norm_back(grad_normed, gain, unit, inverse):
    scaled = grad_normed * gain
    mean_scaled = jnp.mean(scaled, axis=-1, keepdims=True)
    mean_cross = jnp.mean(scaled * unit, axis=-1, keepdims=True)
    return inverse * (scaled - mean_scaled - unit * mean_cross)


def adamw_step(weight, moment, second, gradient, step_rate, weight_decay):
    moment_new = beta_one * moment + (1.0 - beta_one) * gradient
    second_new = beta_two * second + (1.0 - beta_two) * gradient * gradient
    fix_one = 1.0 - beta_one**STEP
    fix_two = 1.0 - beta_two**STEP
    update = moment_new / fix_one / (jnp.sqrt(second_new / fix_two) + eps_adam)
    return (weight - step_rate * (update + weight_decay * weight), moment_new, second_new)


def column_sum(values):
    return jnp.sum(values.astype(jnp.float32), axis=0)


def fill_bias(seg_row, seg_col, bias):
    for (first, rows, key_low, key_high), start in zip(VISIBLE, TILE_STARTS):
        keys = key_high - key_low
        key_places = key_low + lax.broadcasted_iota(jnp.int32, (keys, rows), 0)
        query_places = first + lax.broadcasted_iota(jnp.int32, (keys, rows), 1)
        same = seg_col[key_low:key_high, :] == seg_row[:, first : first + rows]
        allowed = same & (key_places <= query_places)
        bias[start : start + keys, 0:rows] = jnp.where(allowed, 0.0, mask_fill)


def lane_masks(shape):
    lane = lax.broadcasted_iota(jnp.int32, shape, 1)
    return (lane < HD, lane >= HD)


def masked_to(values, mask):
    return jnp.where(mask, values, jnp.zeros_like(values))


def attend_forward_kernel(seg_row, seg_col, q_ref, k_ref, v_ref, out_ref, log_ref, bias):
    @pl.when(pl.program_id(0) == 0)
    def _():
        fill_bias(seg_row, seg_col, bias)

    masks = lane_masks((k_ref.shape[0], PAIR))
    keys_masked = [masked_to(k_ref[...], mask) for mask in masks]
    for (first, rows, key_low, key_high), start in zip(VISIBLE, TILE_STARTS):
        queries = q_ref[first : first + rows, :] * jnp.asarray(HD**-0.5, low)
        values = v_ref[key_low:key_high, :]
        mixed = []
        for head in range(2):
            scores = dot_nt(keys_masked[head][key_low:key_high], queries)
            scores = scores + bias[start : start + key_high - key_low, 0:rows]
            highest = jnp.max(scores, axis=0, keepdims=True)
            exponent = jnp.exp(scores - highest)
            totals = jnp.sum(exponent, axis=0, keepdims=True)
            soft = (exponent * (1.0 / totals)).astype(low)
            mixed.append(dot_tn(soft, values))
            log_ref[0, head : head + 1, first : first + rows] = highest + jnp.log(totals)
        half = lane_masks((rows, PAIR))[0]
        out_ref[first : first + rows, :] = jnp.where(half, mixed[0], mixed[1]).astype(low)


def attend_backward_kernel(
    seg_row, seg_col, q_ref, k_ref, v_ref, log_ref, do_ref, dq_ref, dk_ref, dv_ref, bias, dk_acc, dv_acc
):
    @pl.when(pl.program_id(0) == 0)
    def _():
        fill_bias(seg_row, seg_col, bias)

    masks = lane_masks((k_ref.shape[0], PAIR))
    keys_masked = [masked_to(k_ref[...], mask) for mask in masks]
    values_masked = [masked_to(v_ref[...], mask) for mask in masks]
    dk_acc[...] = jnp.zeros_like(dk_acc)
    dv_acc[...] = jnp.zeros_like(dv_acc)
    for (first, rows, key_low, key_high), start in zip(VISIBLE, TILE_STARTS):
        queries = q_ref[first : first + rows, :] * jnp.asarray(HD**-0.5, low)
        grads = do_ref[first : first + rows, :]
        grad_query = jnp.zeros((rows, PAIR), jnp.float32)
        row_masks = lane_masks((rows, PAIR))
        for head in range(2):
            keys = keys_masked[head][key_low:key_high]
            scores = dot_nt(keys, queries)
            scores = scores + bias[start : start + key_high - key_low, 0:rows]
            soft = jnp.exp(scores - log_ref[0, head : head + 1, first : first + rows])
            grad_soft = dot_nt(values_masked[head][key_low:key_high], grads)
            inner = jnp.sum(soft * grad_soft, axis=0, keepdims=True)
            grad_scores = (soft * (grad_soft - inner)).astype(low)
            dv_acc[key_low:key_high, :] += dot_nn(
                soft.astype(low), masked_to(grads, row_masks[head])
            )
            dk_acc[key_low:key_high, :] += dot_nn(
                grad_scores, masked_to(queries, row_masks[head])
            )
            grad_query = grad_query + dot_tn(grad_scores, keys)
        dq_ref[first : first + rows, :] = (grad_query * HD**-0.5).astype(low)
    dk_ref[...] = dk_acc[...].astype(low)
    dv_ref[...] = dv_acc[...].astype(low)


def attend_specs(length, pairs):
    whole = lambda shape: pl.BlockSpec(shape, lambda j: (0,) * len(shape))
    columns = lambda offset: pl.BlockSpec((length, PAIR), lambda j, offset=offset: (0, offset + j))
    logs = pl.BlockSpec((1, 8, length), lambda j: (j, 0, 0))
    return whole, columns, logs


def attend_forward(seg_row, seg_col, projected):
    length = projected.shape[0]
    pairs = projected.shape[1] // (3 * PAIR)
    whole, columns, logs = attend_specs(length, pairs)
    return pl.pallas_call(
        attend_forward_kernel,
        grid=(pairs,),
        in_specs=[
            whole((1, length)),
            whole((length, 1)),
            columns(0),
            columns(pairs),
            columns(2 * pairs),
        ],
        out_specs=[columns(0), logs],
        out_shape=[
            jax.ShapeDtypeStruct((length, pairs * PAIR), low),
            jax.ShapeDtypeStruct((pairs, 8, length), jnp.float32),
        ],
        scratch_shapes=[pltpu.VMEM((tile_total, 256), jnp.float32)],
        compiler_params=pltpu.CompilerParams(vmem_limit_bytes=vmem_bytes),
        cost_estimate=pl.CostEstimate(
            flops=4 * length * length * pairs * PAIR, bytes_accessed=8 * length * pairs * PAIR,
            transcendentals=length * length * pairs,
        ),
        name="attend_forward",
    )(seg_row, seg_col, projected, projected, projected)


def attend_backward(seg_row, seg_col, projected, logs_all, grad_mixture):
    length = projected.shape[0]
    pairs = projected.shape[1] // (3 * PAIR)
    whole, columns, logs = attend_specs(length, pairs)
    return pl.pallas_call(
        attend_backward_kernel,
        grid=(pairs,),
        in_specs=[
            whole((1, length)),
            whole((length, 1)),
            columns(0),
            columns(pairs),
            columns(2 * pairs),
            logs,
            columns(0),
        ],
        out_specs=[columns(0)] * 3,
        out_shape=[jax.ShapeDtypeStruct((length, pairs * PAIR), low)] * 3,
        scratch_shapes=[
            pltpu.VMEM((tile_total, 256), jnp.float32),
            pltpu.VMEM((length, PAIR), jnp.float32),
            pltpu.VMEM((length, PAIR), jnp.float32),
        ],
        compiler_params=pltpu.CompilerParams(vmem_limit_bytes=vmem_bytes),
        cost_estimate=pl.CostEstimate(
            flops=10 * length * length * pairs * PAIR, bytes_accessed=14 * length * pairs * PAIR,
            transcendentals=length * length * pairs,
        ),
        name="attend_backward",
    )(seg_row, seg_col, projected, projected, projected, logs_all, grad_mixture)


def feed_kernel(part_counts, *refs):
    refs = list(refs)
    take = lambda count: [refs.pop(0) for _ in range(count)]
    normed = [ref[...] for ref in take(2)]
    tops = [ref[...] for ref in take(2)]
    blocks = [take(count) for count in part_counts]
    bias_ref = take(1)[0]
    reduced, reduced_out, back, back_out = take(4)
    outs = [take(2) for _ in part_counts]
    dbu_ref = take(1)[0]
    turned, weights, grads, reduced_sum, back_sum, in_sems, out_sems = refs
    owners, depth, units = weights.shape[2:]
    side_rows = units // (2 * owners)
    split = depth - 2 * side_rows
    arrivals = [
        [
            pltpu.make_async_copy(
                parts[part] if len(parts) == 2 else parts[0].at[pl.ds(part * owners, owners)],
                weights.at[index, part],
                in_sems.at[index, part],
            )
            for part in range(2)
        ]
        for index, parts in enumerate(blocks)
    ]
    for copies in arrivals:
        for copy in copies:
            copy.start()
    rows = normed[0].shape[0]
    reduced_sums = (reduced, reduced_sum)
    back_sums = (back, back_sum)
    for side in range(2):
        turned[:, side * rows : (side + 1) * rows] = normed[side].T
    departures = []
    for index, grad_refs in enumerate(outs):
        for copy in arrivals[index]:
            copy.wait()
        places = [(part, owner) for part in range(2) for owner in range(owners)]
        expand = jnp.concatenate([weights[index, part, owner, :split] for part, owner in places], axis=0)
        reduce = jnp.concatenate(
            [
                jnp.concatenate(
                    [
                        weights[index, part, owner, split : split + side_rows],
                        weights[index, part, owner, split + side_rows :],
                    ],
                    axis=1,
                )
                for part, owner in places
            ],
            axis=0,
        )
        bias_rows = range(2 * owners * index, 2 * owners * (index + 1))
        bias = jnp.concatenate([bias_ref[row : row + 1, :] for row in bias_rows], axis=1)
        hiddens, slopes = [], []
        for side in range(2):
            expanded = dot_nn(normed[side], expand) + bias
            phi = 0.5 + 0.5 * lax.erf(expanded * (0.5**0.5))
            density = jnp.exp(-0.5 * expanded * expanded) * 0.3989422804014327
            hiddens.append((expanded * phi).astype(low))
            grad_hidden = dot_nt(tops[side], reduce)
            slopes.append((grad_hidden * (phi + expanded * density)).astype(low))
        for side in range(2):
            down = dot_nn(hiddens[side], reduce)
            up = dot_nt(slopes[side], expand)
            if index:
                reduced_sums[side][...] += down
                back_sums[side][...] += up
            else:
                reduced_sums[side][...] = down
                back_sums[side][...] = up
        grad_both = jnp.concatenate(slopes, axis=0)
        grad_reduce = sum(dot_tn(hiddens[side], tops[side]) for side in range(2)).astype(low)
        for place, (part, owner) in enumerate(places):
            grads[index, part, owner, :split] = dot_nn(
                turned[place * split : (place + 1) * split, :], grad_both
            ).astype(low)
            rows_down = grad_reduce[place * side_rows : (place + 1) * side_rows]
            grads[index, part, owner, split : split + side_rows] = rows_down[:, :units]
            grads[index, part, owner, split + side_rows :] = rows_down[:, units:]
        bias_grad = jnp.sum(grad_both.astype(jnp.float32), axis=0, keepdims=True)
        for place, row in enumerate(bias_rows):
            dbu_ref[row : row + 1, :] = bias_grad[:, place * side_rows : (place + 1) * side_rows]
        for part in range(2):
            departures.append(
                pltpu.make_async_copy(
                    grads.at[index, part], grad_refs[part], out_sems.at[index, part]
                )
            )
            departures[-1].start()
    reduced_out[...] = reduced_sum[...].astype(low)
    back_out[...] = back_sum[...].astype(low)
    for copy in departures:
        copy.wait()


def feed_blocks(normed, tops, blocks, biases):
    rows, features = normed[0].shape
    count = len(blocks)
    units = biases.shape[0] * biases.shape[1] // count
    operands = [*normed, *tops]
    in_vmem = pl.BlockSpec(memory_space=pltpu.VMEM)
    anywhere = pl.BlockSpec(memory_space=pl.ANY)
    sum_shape = jax.ShapeDtypeStruct((rows, features), jnp.float32)
    sent_shape = jax.ShapeDtypeStruct((rows, features), low)
    shapes = [sum_shape, sent_shape, sum_shape, sent_shape]
    part_shape = blocks[-1][0].shape
    for parts in blocks:
        operands += parts
        shapes += [jax.ShapeDtypeStruct(part_shape, low)] * 2
    operands += [biases]
    shapes += [jax.ShapeDtypeStruct(biases.shape, jnp.float32)]
    part_counts = [len(parts) for parts in blocks]
    results = pl.pallas_call(
        partial(feed_kernel, part_counts),
        in_specs=[in_vmem] * 4 + [anywhere] * sum(part_counts) + [in_vmem],
        out_specs=[in_vmem] * 4 + [anywhere] * (2 * count) + [in_vmem],
        out_shape=shapes,
        scratch_shapes=[
            pltpu.VMEM((features, 2 * rows), low),
            pltpu.VMEM((count, 2) + part_shape, low),
            pltpu.VMEM((count, 2) + part_shape, low),
            pltpu.VMEM((rows, features), jnp.float32),
            pltpu.VMEM((rows, features), jnp.float32),
            pltpu.SemaphoreType.DMA((count, 2)),
            pltpu.SemaphoreType.DMA((count, 2)),
        ],
        compiler_params=pltpu.CompilerParams(vmem_limit_bytes=vmem_bytes),
        cost_estimate=pl.CostEstimate(
            flops=24 * rows * features * units * count,
            bytes_accessed=8 * features * units * count,
            transcendentals=4 * rows * units * count,
        ),
        name="feed_blocks",
    )(*operands)
    grads = [results[4 + 2 * index : 6 + 2 * index] for index in range(count)]
    return results[:4], grads, results[-1]


def renew_into(sources, targets, gradient, step_rate, place=Ellipsis):
    weight, moment, second = (ref[place] for ref in sources)
    results = adamw_step(weight, moment, second, gradient, step_rate, decay_rate)
    for ref, result in zip(targets, results):
        ref[place] = result


def renew_feed_kernel(place_ref, mine, other, *refs):
    expand_in, reduce_in, expand_out, reduce_out = (refs[3 * i : 3 * i + 3] for i in range(4))
    pieces, expand_grad = refs[12:]
    step = pl.program_id(0)
    groups, depth, units = mine.shape
    owners, owned, features = expand_grad.shape
    units_piece = units // owners

    @pl.when(step == 0)
    def _():
        group, core = place_ref[0], place_ref[1]
        for offset in range(groups):
            slot = 2 * (group ^ offset)
            pieces[slot + core] = mine[offset]
            pieces[slot + 1 - core] = other[offset]
        for owner in range(owners):
            expand_grad[owner] = jnp.concatenate(
                [
                    pieces[slot, :owned, owner * units_piece : (owner + 1) * units_piece].astype(
                        jnp.float32
                    )
                    for slot in range(2 * groups)
                ],
                axis=1,
            )

    renew_into(expand_in, expand_out, expand_grad[step], 0.03)
    slots = 2 * groups // owners
    for index in range(slots):
        slot = slots * step + index
        gradient = jnp.concatenate(
            [pieces[slot, owned : owned + units_piece], pieces[slot, owned + units_piece :]],
            axis=1,
        )
        rows = slice(index * units_piece, (index + 1) * units_piece)
        renew_into(reduce_in, reduce_out, gradient.astype(jnp.float32), 0.02, (rows, slice(None)))


def renew_feed(place, mine, other, expand_state, reduce_state):
    groups, depth, units = mine.shape
    owned, hidden_count = expand_state[0].shape
    owned_units, features = reduce_state[0].shape
    owners = hidden_count // owned_units
    whole = pl.BlockSpec(mine.shape, lambda j, _: (0, 0, 0))
    across = pl.BlockSpec((owned, owned_units), lambda j, _: (0, j))
    down = pl.BlockSpec((owned_units // owners, features), lambda j, _: (j, 0))
    shapes = [jax.ShapeDtypeStruct(array.shape, jnp.float32) for array in expand_state]
    shapes += [jax.ShapeDtypeStruct(array.shape, jnp.float32) for array in reduce_state]
    results = pl.pallas_call(
        renew_feed_kernel,
        grid_spec=pltpu.PrefetchScalarGridSpec(
            num_scalar_prefetch=1,
            grid=(owners,),
            in_specs=[whole] * 2 + [across] * 3 + [down] * 3,
            out_specs=[across] * 3 + [down] * 3,
            scratch_shapes=[
                pltpu.VMEM((2 * groups, depth, units), low),
                pltpu.VMEM((owners, owned, owned_units), jnp.float32),
            ],
        ),
        out_shape=shapes,
        compiler_params=pltpu.CompilerParams(vmem_limit_bytes=vmem_bytes),
        cost_estimate=pl.CostEstimate(
            flops=40 * owned * hidden_count, bytes_accessed=48 * owned * hidden_count,
            transcendentals=4 * owned * hidden_count,
        ),
        name="renew_feed",
    )(place, mine, other, *expand_state, *reduce_state)
    return results[:3], results[3:]


def renew_first_kernel(place_ref, mine, other, *refs):
    inputs_in, output_in, inputs_out, output_out = (refs[3 * i : 3 * i + 3] for i in range(4))
    (pieces,) = refs[12:]
    step = pl.program_id(0)
    groups = mine.shape[0]
    group, core = place_ref[0], place_ref[1]
    for offset in range(groups):
        pieces[core, group ^ offset] = mine[offset]
        pieces[1 - core, group ^ offset] = other[offset]
    rows, half = pieces.shape[2:]
    gradient = jnp.concatenate(
        [pieces[side].reshape(groups * rows, half) for side in range(2)], axis=1
    ).astype(jnp.float32)

    @pl.when(step < 3)
    def _():
        renew_into(inputs_in, inputs_out, gradient, 0.03)

    @pl.when(step == 3)
    def _():
        renew_into(output_in, output_out, gradient, 0.3)


def renew_first(place, mine, other, inputs_state, output_state):
    groups, rows, _ = mine.shape
    owned, features = output_state[0].shape
    half = features // 2
    piece = pl.BlockSpec((groups, rows, half), lambda j, _: (0, 0, j))
    across = pl.BlockSpec((owned, features), lambda j, _: (0, jnp.minimum(j, 2)))
    whole = pl.BlockSpec((owned, features), lambda j, _: (0, 0))
    shapes = [jax.ShapeDtypeStruct(array.shape, jnp.float32) for array in inputs_state]
    shapes += [jax.ShapeDtypeStruct(array.shape, jnp.float32) for array in output_state]
    results = pl.pallas_call(
        renew_first_kernel,
        grid_spec=pltpu.PrefetchScalarGridSpec(
            num_scalar_prefetch=1,
            grid=(4,),
            in_specs=[piece] * 2 + [across] * 3 + [whole] * 3,
            out_specs=[across] * 3 + [whole] * 3,
            scratch_shapes=[pltpu.VMEM((2, groups, rows, half), low)],
        ),
        out_shape=shapes,
        compiler_params=pltpu.CompilerParams(vmem_limit_bytes=vmem_bytes),
        cost_estimate=pl.CostEstimate(
            flops=80 * owned * features, bytes_accessed=96 * owned * features,
            transcendentals=8 * owned * features,
        ),
        name="renew_first",
    )(place, mine, other, *inputs_state, *output_state)
    return results[:3], results[3:]


def chip_routes(dp_count, seq_count):
    straight, crossed = [], []
    for place in range(dp_count):
        group, core = place - place % 2, place % 2
        for quarter in range(seq_count):
            source = place * seq_count + quarter
            holder = (group + quarter // 2) * seq_count
            straight.append((source, holder + 2 * core + quarter % 2))
            crossed.append((source, holder + 2 * core + 1 - quarter % 2))
    return straight, crossed


def on_device(
    dp_count,
    seq_count,
    activations,
    cotangent,
    segment_ids,
    inputs_weight,
    inputs_moment,
    inputs_second,
    output_weight,
    output_moment,
    output_second,
    expand_weight,
    expand_moment,
    expand_second,
    reduce_weight,
    reduce_moment,
    reduce_second,
    vector_params,
    vector_moment,
    vector_second,
):
    axes = ("dp", "seq")
    dp_index = lax.axis_index("dp")
    seq_index = lax.axis_index("seq")
    core = dp_index % 2
    group = dp_index // 2
    groups = dp_count // 2
    four_chips = groups == 4
    odd = seq_index % 2
    features = activations.shape[2]
    quarter = activations.shape[1]
    half = features // 2
    owned = inputs_weight.shape[0]
    owned_units = reduce_weight.shape[0]
    rows_piece = owned // groups
    units_piece = owned_units // dp_count
    vector_rows = vector_params.shape[0]
    straight, crossed = chip_routes(dp_count, seq_count)
    core_pairs = [(place, place ^ 1) for place in range(dp_count)]
    x_pairs = [(place, place ^ 2) for place in range(dp_count)]
    y_pairs = [(place, place ^ 4) for place in range(dp_count)]
    far_pairs = [(place, place ^ 6) for place in range(dp_count)]
    same_core = [list(range(first, dp_count, 2)) for first in range(2)]

    def to_chip(values):
        near = lax.dynamic_index_in_dim(values, odd, 0, keepdims=False)
        far = lax.dynamic_index_in_dim(values, 1 - odd, 0, keepdims=False)
        near = lax.ppermute(near, axes, straight)
        far = lax.ppermute(far, axes, crossed)
        return jnp.concatenate(
            [jnp.where(odd == 0, near, far), jnp.where(odd == 0, far, near)], axis=0
        )

    def from_chip(values):
        near = lax.dynamic_slice_in_dim(values, odd * quarter, quarter, 0)
        far = lax.dynamic_slice_in_dim(values, (1 - odd) * quarter, quarter, 0)
        near = lax.ppermute(near, axes, [(there, here) for here, there in straight])
        far = lax.ppermute(far, axes, [(there, here) for here, there in crossed])
        return jnp.stack([jnp.where(odd == 0, near, far), jnp.where(odd == 0, far, near)])

    def swap_cores(values):
        return lax.ppermute(values, "dp", core_pairs)

    def via_x(values):
        return lax.ppermute(values, "dp", x_pairs)

    def via_y(values):
        return lax.ppermute(values, "dp", y_pairs)

    def by_core(mine, theirs, axis):
        return jnp.where(
            core == 0,
            jnp.concatenate([mine, theirs], axis=axis),
            jnp.concatenate([theirs, mine], axis=axis),
        )

    def add_low(*terms):
        return sum(term.astype(jnp.float32) for term in terms).astype(low)

    def after(values, *gates):
        return lax.optimization_barrier((values, gates))[0]

    def gather_z(piece):
        parts = [piece]
        for shift in range(1, seq_count):
            ring = [(place, (place + shift) % seq_count) for place in range(seq_count)]
            parts.append(lax.ppermute(piece, "seq", ring))
        placed = [
            lax.select_n((seq_index - owner) % seq_count, *parts) for owner in range(seq_count)
        ]
        middle = seq_count // 2
        return jnp.stack(placed[:middle]), jnp.stack(placed[middle:])

    def gather_chips(halves):
        first, second = halves
        x_first, y_second = via_x(first), via_y(second)
        x_second, y_first = via_x(second), via_y(first)
        return halves, (x_first, x_second), (y_first, y_second), (via_y(x_first), via_x(y_second))

    def in_order(own, from_x, from_y, from_far, axis):
        x_set = group % 2 == 1
        y_set = group // 2 == 1
        near_low = jnp.where(x_set, from_x, own)
        near_high = jnp.where(x_set, own, from_x)
        far_low = jnp.where(x_set, from_far, from_y)
        far_high = jnp.where(x_set, from_y, from_far)
        return jnp.stack(
            [
                jnp.where(y_set, far_low, near_low),
                jnp.where(y_set, far_high, near_high),
                jnp.where(y_set, near_low, far_low),
                jnp.where(y_set, near_high, far_high),
            ],
            axis=axis,
        )

    def scatter_begin(own, to_x, to_y, to_far):
        far_first, far_second = via_x(to_far[0]), via_y(to_far[1])
        return (own, to_x, to_y, far_first, far_second, via_x(to_x[0]), via_y(to_y[1]))

    def scatter_middle(state, near_too, *gates):
        own, to_x, to_y, far_first, far_second, x_first, y_second = state
        if near_too:
            far_first, far_second, x_first, y_second = after(
                (far_first, far_second, x_first, y_second), *gates
            )
        else:
            far_first, far_second = after((far_first, far_second), *gates)
        y_first = add_low(to_y[0], far_first)
        x_second = add_low(to_x[1], far_second)
        return (own, x_first, via_x(x_second), via_y(y_first), y_second), (y_first, x_second)

    def scatter_end(state):
        own, x_first, x_second, y_first, y_second = state
        first = add_low(own[0], x_first, y_first)
        second = add_low(own[1], x_second, y_second)
        return first, second

    def scatter_z_begin(blocks):
        parts = [lax.dynamic_index_in_dim(blocks, seq_index, 0, keepdims=False)]
        for shift in range(1, seq_count):
            target = (seq_index + shift) % seq_count
            sent = lax.dynamic_index_in_dim(blocks, target, 0, keepdims=False)
            ring = [(place, (place + shift) % seq_count) for place in range(seq_count)]
            parts.append(lax.ppermute(sent, "seq", ring))
        return parts

    def scatter_z(blocks):
        return add_low(*scatter_z_begin(blocks))

    def regather_begin(piece):
        return piece, via_x(piece), via_y(piece), lax.ppermute(piece, "dp", far_pairs)

    def regather_end(state):
        mine = in_order(*state, 0)
        return by_core(mine[:, None], swap_cores(mine)[:, None], 1)

    def regather(piece):
        every = lax.all_gather(piece, "dp", axis=0, tiled=False)
        return every.reshape((groups, 2) + piece.shape)

    def corner(weight, column):
        return lax.dynamic_slice(
            weight, (group * rows_piece, column + core * half), (rows_piece, half)
        ).astype(low)

    vector_piece = lax.dynamic_slice_in_dim(vector_params, group * rows_piece, rows_piece, 1)
    first_piece = jnp.concatenate(
        [
            corner(inputs_weight, 0),
            corner(inputs_weight, features),
            corner(inputs_weight, 2 * features),
            corner(output_weight, 0),
            jnp.pad(vector_piece.T.astype(low), ((0, 0), (0, LANES - vector_rows))),
        ],
        axis=1,
    )
    expand_piece = jnp.concatenate(
        [
            lax.dynamic_slice_in_dim(
                expand_weight, owner * owned_units + dp_index * units_piece, units_piece, 1
            ).astype(low)
            for owner in range(seq_count)
        ],
        axis=1,
    )
    reduce_piece = lax.dynamic_slice_in_dim(
        reduce_weight, dp_index * units_piece, units_piece, 0
    ).astype(low)

    def pack(expand, reduce):
        return jnp.concatenate([expand, reduce[..., :half], reduce[..., half:]], axis=-2)

    residual_low = to_chip(activations)
    first_block = gather_z(first_piece)
    if four_chips:
        feed_block = lax.all_gather(
            pack(expand_piece, reduce_piece), "seq", axis=0, tiled=False
        )
        cotangent = after(cotangent, feed_block)
    grad_top = to_chip(cotangent)
    rows_here = residual_low.shape[0]
    residual_other = swap_cores(residual_low)
    grad_top_other = swap_cores(grad_top)
    other_segments = swap_cores(segment_ids)
    segment_pair = jnp.where(seq_index // 2 == core, segment_ids, other_segments)
    segments = lax.dynamic_index_in_dim(segment_pair, odd, 0, keepdims=False)
    seg_row, seg_col = segments[None, :], segments[:, None]

    if four_chips:
        every_first = gather_chips(first_block)
        first_low = jnp.concatenate(
            [in_order(*[block[part] for block in every_first], 1) for part in range(2)], axis=0
        )
    else:
        first_low = lax.all_gather(
            jnp.concatenate(first_block, axis=0),
            "dp",
            axis=1,
            tiled=False,
            axis_index_groups=same_core,
        )
    first_low = first_low.reshape(features, first_low.shape[-1])
    wide = 3 * half
    inputs_low = first_low[:, :wide]
    output_half = first_low[:, wide : wide + half]
    output_all = by_core(output_half, swap_cores(output_half), 1)
    vectors = first_low[:, wide + half : wide + half + vector_rows].T.astype(jnp.float32)

    expand_bias = vectors[8:].reshape(seq_count, dp_count, units_piece)
    block_units = seq_count * owned_units // 8
    if four_chips:
        feed_x, feed_y = via_x(feed_block), via_y(feed_block)
        middle_owner = seq_count // 2
        feed_far = (via_y(feed_x[:middle_owner]), via_x(feed_y[middle_owner:]))
        blocks = [(feed_block,), (feed_x,), (feed_y,), feed_far]
        biases = jnp.concatenate(
            [
                lax.dynamic_index_in_dim(expand_bias, dp_index ^ (2 * offset), 1, keepdims=False)
                for offset in range(4)
            ],
            axis=0,
        )
    else:
        expand_all = lax.all_gather(
            jnp.concatenate(gather_z(expand_piece), axis=0).reshape(features, -1),
            "dp",
            axis=1,
            axis_index_groups=same_core,
        ).reshape(seq_count, owned, 4, block_units)
        reduce_all = lax.all_gather(
            jnp.concatenate(gather_z(reduce_piece), axis=0).reshape(-1, features),
            "dp",
            axis=0,
            axis_index_groups=same_core,
        ).reshape(4, seq_count, -1, features)
        picked = lax.dynamic_index_in_dim(
            expand_bias.reshape(seq_count, groups, 2, units_piece), core, 2, keepdims=False
        )
        biases = picked.transpose(1, 0, 2).reshape(4 * seq_count, block_units // seq_count)
        blocks = []
        for index in range(4):
            packed = pack(expand_all[:, :, index], reduce_all[index])
            blocks.append((packed[: seq_count // 2], packed[seq_count // 2 :]))

    def tokens_of(values, which):
        return lax.dynamic_slice_in_dim(values, which * rows_here, rows_here, 0)

    def heads_part(vector):
        return lax.dynamic_slice_in_dim(vector, core * half, half, 0)

    unit_all, _ = normalize(by_core(residual_low, residual_other, 0).astype(jnp.float32))
    normed_one = (unit_all * vectors[0] + vectors[1]).astype(low)
    input_bias = jnp.concatenate(
        [heads_part(vectors[4]), jnp.zeros((half,), jnp.float32), heads_part(vectors[5])]
    )
    projected = (dot_nn(normed_one, inputs_low) + input_bias).astype(low)
    if four_chips:
        projected = after(projected, feed_block)
    mixture_heads, logs_all = attend_forward(seg_row, seg_col, projected)
    if four_chips:
        mixture_heads = after(mixture_heads, grad_top, feed_x, feed_y)
    mixture_theirs = swap_cores(tokens_of(mixture_heads, 1 - core))
    mixture = by_core(tokens_of(mixture_heads, core), mixture_theirs, 1)

    residual = residual_low.astype(jnp.float32)
    middle = residual + (dot_nn(mixture, output_all) + vectors[6])
    unit_two, inverse_two = normalize(middle)
    normed_two = (unit_two * vectors[2] + vectors[3]).astype(low)
    if four_chips:
        normed_two = after(normed_two, feed_far)
    normed_pair = (normed_two, swap_cores(normed_two))
    top_pair = (grad_top, grad_top_other)
    sums, grads, bias_grads = feed_blocks(normed_pair, top_pair, blocks, biases)
    grad_normed_two = sums[2] + swap_cores(sums[3]).astype(jnp.float32)
    reduced = sums[0] + swap_cores(sums[1]).astype(jnp.float32)
    output_low = (middle + (reduced + vectors[7])).astype(low)

    if four_chips:
        feed_state = scatter_begin(*grads)
        place = jnp.arange(dp_count)[None, :, None]
        bias_sums = sum(
            jnp.where(
                place == (dp_index ^ (2 * offset)),
                bias_grads[seq_count * offset : seq_count * (offset + 1), None, :],
                0.0,
            )
            for offset in range(4)
        )
    else:
        packed = [jnp.concatenate(grad, axis=0) for grad in grads]
        expand_sum = jnp.stack([part[:, :owned] for part in packed], axis=2)
        expand_sum = expand_sum.reshape(features, groups, -1).transpose(1, 0, 2)
        expand_sum = lax.psum_scatter(expand_sum, "dp", axis_index_groups=same_core)
        reduce_sum = [part[:, owned:].reshape(seq_count, 2, -1, half) for part in packed]
        reduce_sum = jnp.stack([part.transpose(0, 2, 1, 3) for part in reduce_sum])
        reduce_sum = reduce_sum.reshape(groups, -1, features)
        reduce_sum = lax.psum_scatter(reduce_sum, "dp", axis_index_groups=same_core)
        bias_sums = bias_grads.reshape(groups, seq_count, units_piece).transpose(1, 0, 2)
        is_core = jnp.arange(2)[None, None, :, None] == core
        bias_sums = jnp.where(is_core, bias_sums[:, :, None, :], 0.0)

    grad_middle = grad_top.astype(jnp.float32) + norm_back(
        grad_normed_two, vectors[2], unit_two, inverse_two
    )
    grad_attended = grad_middle.astype(low)
    grad_output = dot_tn(mixture, grad_attended).astype(low)
    grad_mixture = dot_nt(grad_attended, output_all).astype(low)

    def columns_of(values, which):
        return lax.dynamic_slice_in_dim(values, which * half, half, 1)

    grad_theirs = swap_cores(columns_of(grad_mixture, 1 - core))
    grad_joined = by_core(columns_of(grad_mixture, core), grad_theirs, 0)
    if four_chips:
        feed_state, gates = scatter_middle(feed_state, False, grad_mixture)
        grad_joined = after(grad_joined, *gates)
    grad_heads = attend_backward(seg_row, seg_col, projected, logs_all, grad_joined)
    output_sum = add_low(
        columns_of(grad_output, core), swap_cores(columns_of(grad_output, 1 - core))
    )
    grad_projected = jnp.concatenate(grad_heads, axis=1)
    if four_chips:
        feed_sum = scatter_end(after(feed_state, grad_projected))
        feed_parts = scatter_z_begin(jnp.concatenate(feed_sum, axis=0))
        grad_projected = after(grad_projected, *feed_sum)
    grad_inputs = dot_tn(normed_one, grad_projected).astype(low)
    grad_normed_all = dot_nt(grad_projected, inputs_low)
    grad_normed_one = tokens_of(grad_normed_all, core) + swap_cores(
        tokens_of(grad_normed_all, 1 - core).astype(low)
    ).astype(jnp.float32)
    unit_one, inverse_one = normalize(residual)
    grad_residual = norm_back(grad_normed_one, vectors[0], unit_one, inverse_one)
    input_grad = (grad_middle + grad_residual).astype(low)

    def heads_sum(values):
        return lax.dynamic_update_slice_in_dim(
            jnp.zeros((features,), jnp.float32), column_sum(values), core * half, 0
        )

    head_rows = jnp.stack(
        [
            column_sum(grad_normed_one * unit_one),
            column_sum(grad_normed_one),
            column_sum(grad_normed_two * unit_two),
            column_sum(grad_normed_two),
            heads_sum(grad_heads[0]),
            heads_sum(grad_heads[2]),
            column_sum(grad_attended),
            column_sum(grad_top),
        ]
    )
    grad_vectors = jnp.concatenate([head_rows, bias_sums.reshape(-1, features)], axis=0)
    vector_columns = jnp.pad(grad_vectors.T.astype(low), ((0, 0), (0, LANES - vector_rows)))
    first_grad = jnp.concatenate([grad_inputs, output_sum, vector_columns], axis=1)
    first_grad = first_grad.reshape(seq_count, groups, rows_piece, -1)
    if four_chips:
        middle_owner = seq_count // 2
        split = []
        for offset in range(4):
            split.append(
                [
                    lax.dynamic_index_in_dim(part, group ^ offset, 1, keepdims=False)
                    for part in (first_grad[:middle_owner], first_grad[middle_owner:])
                ]
            )
        feed_pieces = regather_begin(add_low(*feed_parts))
        split, feed_pieces = after((split, feed_pieces))
        first_state = scatter_begin(*split)
        layer_output = from_chip(after(output_low, split))
        input_grad = from_chip(after(input_grad, split))
        first_state, _ = scatter_middle(first_state, True)
        first_state, layer_output, input_grad = after((first_state, layer_output, input_grad))
        first_parts = scatter_z_begin(jnp.concatenate(scatter_end(first_state), axis=0))
        feed_mine = jnp.stack(feed_pieces)
        feed_other = swap_cores(feed_mine)
        place = jnp.stack([group, core]).astype(jnp.int32)
        new_expand, new_reduce = renew_feed(
            place,
            feed_mine,
            feed_other,
            (expand_weight, expand_moment, expand_second),
            (reduce_weight, reduce_moment, reduce_second),
        )
        first_parts, new_expand = after((first_parts, new_expand))
        first_pieces = regather_begin(add_low(*first_parts))
        first_mine = jnp.stack(first_pieces)
        first_other = swap_cores(first_mine)
        new_inputs, new_output = renew_first(
            place,
            first_mine,
            first_other,
            (inputs_weight, inputs_moment, inputs_second),
            (output_weight, output_moment, output_second),
        )
        vector_slice = slice(wide + half, wide + half + vector_rows)
        vector_parts = first_mine[..., vector_slice].astype(jnp.float32) + first_other[
            ..., vector_slice
        ].astype(jnp.float32)
        sum_vectors = in_order(*[vector_parts[offset] for offset in range(4)], 0)
        sum_vectors = sum_vectors.reshape(owned, vector_rows).T
    else:
        first_sum = lax.psum_scatter(
            first_grad, "dp", scatter_dimension=1, axis_index_groups=same_core
        )
        layer_output, input_grad = from_chip(output_low), from_chip(input_grad)
        every_first = regather(scatter_z(first_sum))
        sum_expand = regather(scatter_z(expand_sum.reshape(seq_count, owned, -1)))
        sum_reduce = regather(scatter_z(reduce_sum.reshape(seq_count, units_piece, features)))
    def renew(weight, moment, second, gradient, step_rate, weight_decay):
        return adamw_step(
            weight, moment, second, gradient.astype(jnp.float32), step_rate, weight_decay
        )

    if not four_chips:
        sum_expand = sum_expand.reshape(dp_count, owned, seq_count, units_piece)
        sum_expand = sum_expand.transpose(1, 2, 0, 3).reshape(expand_weight.shape)
        sum_reduce = sum_reduce.reshape(reduce_weight.shape)
        sum_first = every_first.transpose(0, 2, 1, 3)
        sum_inputs = sum_first[..., :wide].reshape(groups, rows_piece, 2, 3, half)
        sum_inputs = sum_inputs.transpose(0, 1, 3, 2, 4).reshape(inputs_weight.shape)
        sum_output = sum_first[..., wide : wide + half].reshape(output_weight.shape)
        sum_vectors = sum_first[..., wide + half : wide + half + vector_rows].astype(jnp.float32)
        sum_vectors = jnp.sum(sum_vectors, axis=2).reshape(owned, vector_rows).T
        new_inputs = renew(inputs_weight, inputs_moment, inputs_second, sum_inputs, 0.03, decay_rate)
        new_output = renew(output_weight, output_moment, output_second, sum_output, 0.3, decay_rate)
        new_expand = renew(expand_weight, expand_moment, expand_second, sum_expand, 0.03, decay_rate)
        new_reduce = renew(reduce_weight, reduce_moment, reduce_second, sum_reduce, 0.02, decay_rate)
    new_vectors = renew(vector_params, vector_moment, vector_second, sum_vectors, 0.5, 0.0)
    return (
        layer_output,
        input_grad,
        *new_inputs,
        *new_output,
        *new_expand,
        *new_reduce,
        *new_vectors,
    )


def solution(mesh):
    tokens = P("dp", "seq", None)
    rows = P("seq", None)
    columns = P(None, "seq")
    in_specs = (tokens, tokens, P("dp", None)) + (rows,) * 12 + (columns,) * 3
    out_specs = (tokens, tokens) + (rows,) * 12 + (columns,) * 3
    return jax.shard_map(
        partial(on_device, mesh.shape["dp"], mesh.shape["seq"]),
        mesh=mesh,
        in_specs=in_specs,
        out_specs=out_specs,
        check_vma=False,
    )
```

```python
from functools import partial

import jax
import jax.numpy as jnp
from jax import lax
from jax.experimental import pallas as pl
from jax.experimental.pallas import tpu as pltpu
from jax.sharding import PartitionSpec as P

HEADS = 12
HD = 64
STEP = 10
PAIR = 2 * HD
LANES = 128

eps_norm = 1e-05
eps_adam = 1e-08
beta_one = 0.9
beta_two = 0.95
decay_rate = 0.1
mask_fill = -1e30
vmem_bytes = 56 * 1024 * 1024

VISIBLE = (
    (0, 256, 0, 256),
    (256, 256, 128, 512),
    (512, 256, 128, 768),
    (768, 128, 128, 896),
    (896, 128, 768, 1024),
)
TILE_STARTS = []
tile_total = 0
for _first, _rows, _low, _high in VISIBLE:
    TILE_STARTS.append(tile_total)
    tile_total += _high - _low

low = jnp.bfloat16


def dot_nn(left_side, right_side):
    return lax.dot_general(
        left_side, right_side, (((1,), (0,)), ((), ())), preferred_element_type=jnp.float32
    )


def dot_tn(left_side, right_side):
    return lax.dot_general(
        left_side, right_side, (((0,), (0,)), ((), ())), preferred_element_type=jnp.float32
    )


def dot_nt(left_side, right_side):
    return lax.dot_general(
        left_side, right_side, (((1,), (1,)), ((), ())), preferred_element_type=jnp.float32
    )


def normalize(values):
    center = jnp.mean(values, axis=-1, keepdims=True)
    offsets = values - center
    spread = jnp.mean(offsets * offsets, axis=-1, keepdims=True)
    inverse = lax.rsqrt(spread + eps_norm)
    return offsets * inverse, inverse


def norm_back(grad_normed, gain, unit, inverse):
    scaled = grad_normed * gain
    mean_scaled = jnp.mean(scaled, axis=-1, keepdims=True)
    mean_cross = jnp.mean(scaled * unit, axis=-1, keepdims=True)
    return inverse * (scaled - mean_scaled - unit * mean_cross)


def adamw_step(weight, moment, second, gradient, step_rate, weight_decay):
    moment_new = beta_one * moment + (1.0 - beta_one) * gradient
    second_new = beta_two * second + (1.0 - beta_two) * gradient * gradient
    fix_one = 1.0 - beta_one**STEP
    fix_two = 1.0 - beta_two**STEP
    update = moment_new / fix_one / (jnp.sqrt(second_new / fix_two) + eps_adam)
    return (weight - step_rate * (update + weight_decay * weight), moment_new, second_new)


def column_sum(values):
    return jnp.sum(values.astype(jnp.float32), axis=0)


def fill_bias(seg_row, seg_col, bias):
    for (first, rows, key_low, key_high), start in zip(VISIBLE, TILE_STARTS):
        keys = key_high - key_low
        key_places = key_low + lax.broadcasted_iota(jnp.int32, (keys, rows), 0)
        query_places = first + lax.broadcasted_iota(jnp.int32, (keys, rows), 1)
        same = seg_col[key_low:key_high, :] == seg_row[:, first : first + rows]
        allowed = same & (key_places <= query_places)
        bias[start : start + keys, 0:rows] = jnp.where(allowed, 0.0, mask_fill)


def lane_masks(shape):
    lane = lax.broadcasted_iota(jnp.int32, shape, 1)
    return (lane < HD, lane >= HD)


def masked_to(values, mask):
    return jnp.where(mask, values, jnp.zeros_like(values))


def attend_forward_kernel(seg_row, seg_col, q_ref, k_ref, v_ref, out_ref, log_ref, bias):
    @pl.when(pl.program_id(0) == 0)
    def _():
        fill_bias(seg_row, seg_col, bias)

    masks = lane_masks((k_ref.shape[0], PAIR))
    keys_masked = [masked_to(k_ref[...], mask) for mask in masks]
    for (first, rows, key_low, key_high), start in zip(VISIBLE, TILE_STARTS):
        queries = q_ref[first : first + rows, :] * jnp.asarray(HD**-0.5, low)
        values = v_ref[key_low:key_high, :]
        mixed = []
        for head in range(2):
            scores = dot_nt(keys_masked[head][key_low:key_high], queries)
            scores = scores + bias[start : start + key_high - key_low, 0:rows]
            highest = jnp.max(scores, axis=0, keepdims=True)
            exponent = jnp.exp(scores - highest)
            totals = jnp.sum(exponent, axis=0, keepdims=True)
            soft = (exponent * (1.0 / totals)).astype(low)
            mixed.append(dot_tn(soft, values))
            log_ref[0, head : head + 1, first : first + rows] = highest + jnp.log(totals)
        half = lane_masks((rows, PAIR))[0]
        out_ref[first : first + rows, :] = jnp.where(half, mixed[0], mixed[1]).astype(low)


def attend_backward_kernel(
    seg_row, seg_col, q_ref, k_ref, v_ref, log_ref, do_ref, dq_ref, dk_ref, dv_ref, bias, dk_acc, dv_acc
):
    @pl.when(pl.program_id(0) == 0)
    def _():
        fill_bias(seg_row, seg_col, bias)

    masks = lane_masks((k_ref.shape[0], PAIR))
    keys_masked = [masked_to(k_ref[...], mask) for mask in masks]
    values_masked = [masked_to(v_ref[...], mask) for mask in masks]
    dk_acc[...] = jnp.zeros_like(dk_acc)
    dv_acc[...] = jnp.zeros_like(dv_acc)
    for (first, rows, key_low, key_high), start in zip(VISIBLE, TILE_STARTS):
        queries = q_ref[first : first + rows, :] * jnp.asarray(HD**-0.5, low)
        grads = do_ref[first : first + rows, :]
        grad_query = jnp.zeros((rows, PAIR), jnp.float32)
        row_masks = lane_masks((rows, PAIR))
        for head in range(2):
            keys = keys_masked[head][key_low:key_high]
            scores = dot_nt(keys, queries)
            scores = scores + bias[start : start + key_high - key_low, 0:rows]
            soft = jnp.exp(scores - log_ref[0, head : head + 1, first : first + rows])
            grad_soft = dot_nt(values_masked[head][key_low:key_high], grads)
            inner = jnp.sum(soft * grad_soft, axis=0, keepdims=True)
            grad_scores = (soft * (grad_soft - inner)).astype(low)
            dv_acc[key_low:key_high, :] += dot_nn(
                soft.astype(low), masked_to(grads, row_masks[head])
            )
            dk_acc[key_low:key_high, :] += dot_nn(
                grad_scores, masked_to(queries, row_masks[head])
            )
            grad_query = grad_query + dot_tn(grad_scores, keys)
        dq_ref[first : first + rows, :] = (grad_query * HD**-0.5).astype(low)
    dk_ref[...] = dk_acc[...].astype(low)
    dv_ref[...] = dv_acc[...].astype(low)


def attend_specs(length, pairs):
    whole = lambda shape: pl.BlockSpec(shape, lambda j: (0,) * len(shape))
    columns = lambda offset: pl.BlockSpec((length, PAIR), lambda j, offset=offset: (0, offset + j))
    logs = pl.BlockSpec((1, 8, length), lambda j: (j, 0, 0))
    return whole, columns, logs


def attend_forward(seg_row, seg_col, projected):
    length = projected.shape[0]
    pairs = projected.shape[1] // (3 * PAIR)
    whole, columns, logs = attend_specs(length, pairs)
    return pl.pallas_call(
        attend_forward_kernel,
        grid=(pairs,),
        in_specs=[
            whole((1, length)),
            whole((length, 1)),
            columns(0),
            columns(pairs),
            columns(2 * pairs),
        ],
        out_specs=[columns(0), logs],
        out_shape=[
            jax.ShapeDtypeStruct((length, pairs * PAIR), low),
            jax.ShapeDtypeStruct((pairs, 8, length), jnp.float32),
        ],
        scratch_shapes=[pltpu.VMEM((tile_total, 256), jnp.float32)],
        compiler_params=pltpu.CompilerParams(vmem_limit_bytes=vmem_bytes),
        cost_estimate=pl.CostEstimate(
            flops=4 * length * length * pairs * PAIR, bytes_accessed=8 * length * pairs * PAIR,
            transcendentals=length * length * pairs,
        ),
        name="attend_forward",
    )(seg_row, seg_col, projected, projected, projected)


def attend_backward(seg_row, seg_col, projected, logs_all, grad_mixture):
    length = projected.shape[0]
    pairs = projected.shape[1] // (3 * PAIR)
    whole, columns, logs = attend_specs(length, pairs)
    return pl.pallas_call(
        attend_backward_kernel,
        grid=(pairs,),
        in_specs=[
            whole((1, length)),
            whole((length, 1)),
            columns(0),
            columns(pairs),
            columns(2 * pairs),
            logs,
            columns(0),
        ],
        out_specs=[columns(0)] * 3,
        out_shape=[jax.ShapeDtypeStruct((length, pairs * PAIR), low)] * 3,
        scratch_shapes=[
            pltpu.VMEM((tile_total, 256), jnp.float32),
            pltpu.VMEM((length, PAIR), jnp.float32),
            pltpu.VMEM((length, PAIR), jnp.float32),
        ],
        compiler_params=pltpu.CompilerParams(vmem_limit_bytes=vmem_bytes),
        cost_estimate=pl.CostEstimate(
            flops=10 * length * length * pairs * PAIR, bytes_accessed=14 * length * pairs * PAIR,
            transcendentals=length * length * pairs,
        ),
        name="attend_backward",
    )(seg_row, seg_col, projected, projected, projected, logs_all, grad_mixture)


def feed_kernel(part_counts, *refs):
    refs = list(refs)
    take = lambda count: [refs.pop(0) for _ in range(count)]
    normed = [ref[...] for ref in take(2)]
    tops = [ref[...] for ref in take(2)]
    blocks = [take(count) for count in part_counts]
    bias_ref = take(1)[0]
    reduced, reduced_out, back, back_out = take(4)
    own_first, own_second, x_second, y_first, x_sent, y_sent = take(6)
    dbu_ref = take(1)[0]
    turned, weights, grads, reduced_sum, back_sum, in_sems, out_sems = refs
    owners, depth, units = weights.shape[2:]
    side_rows = units // (2 * owners)
    split = depth - 2 * side_rows
    arrivals = [
        [
            pltpu.make_async_copy(
                parts[part] if len(parts) == 2 else parts[0].at[pl.ds(part * owners, owners)],
                weights.at[index, part],
                in_sems.at[index, part],
            )
            for part in range(2)
        ]
        for index, parts in enumerate(blocks)
    ]
    for copies in arrivals:
        for copy in copies:
            copy.start()
    rows = normed[0].shape[0]
    reduced_sums = (reduced, reduced_sum)
    back_sums = (back, back_sum)
    for side in range(2):
        turned[:, side * rows : (side + 1) * rows] = normed[side].T
    departures = []
    targets = (
        (own_first, own_second),
        (x_sent.at[pl.ds(0, owners)], x_second),
        (y_first, y_sent.at[pl.ds(0, owners)]),
        (x_sent.at[pl.ds(owners, owners)], y_sent.at[pl.ds(owners, owners)]),
    )
    for index, grad_refs in enumerate(targets):
        for copy in arrivals[index]:
            copy.wait()
        places = [(part, owner) for part in range(2) for owner in range(owners)]
        expand = jnp.concatenate([weights[index, part, owner, :split] for part, owner in places], axis=0)
        reduce = jnp.concatenate(
            [
                jnp.concatenate(
                    [
                        weights[index, part, owner, split : split + side_rows],
                        weights[index, part, owner, split + side_rows :],
                    ],
                    axis=1,
                )
                for part, owner in places
            ],
            axis=0,
        )
        bias_rows = range(2 * owners * index, 2 * owners * (index + 1))
        bias = jnp.concatenate([bias_ref[row : row + 1, :] for row in bias_rows], axis=1)
        hiddens, slopes = [], []
        for side in range(2):
            expanded = dot_nn(normed[side], expand) + bias
            phi = 0.5 + 0.5 * lax.erf(expanded * (0.5**0.5))
            density = jnp.exp(-0.5 * expanded * expanded) * 0.3989422804014327
            hiddens.append((expanded * phi).astype(low))
            grad_hidden = dot_nt(tops[side], reduce)
            slopes.append((grad_hidden * (phi + expanded * density)).astype(low))
        for side in range(2):
            down = dot_nn(hiddens[side], reduce)
            up = dot_nt(slopes[side], expand)
            if index:
                reduced_sums[side][...] += down
                back_sums[side][...] += up
            else:
                reduced_sums[side][...] = down
                back_sums[side][...] = up
        grad_both = jnp.concatenate(slopes, axis=0)
        grad_reduce = sum(dot_tn(hiddens[side], tops[side]) for side in range(2)).astype(low)
        for place, (part, owner) in enumerate(places):
            grads[index, part, owner, :split] = dot_nn(
                turned[place * split : (place + 1) * split, :], grad_both
            ).astype(low)
            rows_down = grad_reduce[place * side_rows : (place + 1) * side_rows]
            grads[index, part, owner, split : split + side_rows] = rows_down[:, :units]
            grads[index, part, owner, split + side_rows :] = rows_down[:, units:]
        bias_grad = jnp.sum(grad_both.astype(jnp.float32), axis=0, keepdims=True)
        for place, row in enumerate(bias_rows):
            dbu_ref[row : row + 1, :] = bias_grad[:, place * side_rows : (place + 1) * side_rows]
        for part in range(2):
            departures.append(
                pltpu.make_async_copy(
                    grads.at[index, part], grad_refs[part], out_sems.at[index, part]
                )
            )
            departures[-1].start()
    reduced_out[...] = reduced_sum[...].astype(low)
    back_out[...] = back_sum[...].astype(low)
    for copy in departures:
        copy.wait()


def feed_blocks(normed, tops, blocks, biases):
    rows, features = normed[0].shape
    count = len(blocks)
    units = biases.shape[0] * biases.shape[1] // count
    operands = [*normed, *tops]
    in_vmem = pl.BlockSpec(memory_space=pltpu.VMEM)
    anywhere = pl.BlockSpec(memory_space=pl.ANY)
    sum_shape = jax.ShapeDtypeStruct((rows, features), jnp.float32)
    sent_shape = jax.ShapeDtypeStruct((rows, features), low)
    shapes = [sum_shape, sent_shape, sum_shape, sent_shape]
    part_shape = blocks[-1][0].shape
    for parts in blocks:
        operands += parts
    sent_block = (2 * part_shape[0],) + part_shape[1:]
    shapes += [jax.ShapeDtypeStruct(part_shape, low)] * 4
    shapes += [jax.ShapeDtypeStruct(sent_block, low)] * 2
    operands += [biases]
    shapes += [jax.ShapeDtypeStruct(biases.shape, jnp.float32)]
    part_counts = [len(parts) for parts in blocks]
    results = pl.pallas_call(
        partial(feed_kernel, part_counts),
        in_specs=[in_vmem] * 4 + [anywhere] * sum(part_counts) + [in_vmem],
        out_specs=[in_vmem] * 4 + [anywhere] * 6 + [in_vmem],
        out_shape=shapes,
        scratch_shapes=[
            pltpu.VMEM((features, 2 * rows), low),
            pltpu.VMEM((count, 2) + part_shape, low),
            pltpu.VMEM((count, 2) + part_shape, low),
            pltpu.VMEM((rows, features), jnp.float32),
            pltpu.VMEM((rows, features), jnp.float32),
            pltpu.SemaphoreType.DMA((count, 2)),
            pltpu.SemaphoreType.DMA((count, 2)),
        ],
        compiler_params=pltpu.CompilerParams(vmem_limit_bytes=vmem_bytes),
        cost_estimate=pl.CostEstimate(
            flops=24 * rows * features * units * count,
            bytes_accessed=8 * features * units * count,
            transcendentals=4 * rows * units * count,
        ),
        name="feed_blocks",
    )(*operands)
    return results[:4], results[4:10], results[10]


def renew_into(sources, targets, gradient, step_rate, place=Ellipsis):
    weight, moment, second = (ref[place] for ref in sources)
    results = adamw_step(weight, moment, second, gradient, step_rate, decay_rate)
    for ref, result in zip(targets, results):
        ref[place] = result


def renew_feed_kernel(place_ref, mine, other, *refs):
    expand_in, reduce_in, expand_out, reduce_out = (refs[3 * i : 3 * i + 3] for i in range(4))
    pieces, expand_grad = refs[12:]
    step = pl.program_id(0)
    groups, depth, units = mine.shape
    owners, owned, features = expand_grad.shape
    units_piece = units // owners

    @pl.when(step == 0)
    def _():
        group, core = place_ref[0], place_ref[1]
        for offset in range(groups):
            slot = 2 * (group ^ offset)
            pieces[slot + core] = mine[offset]
            pieces[slot + 1 - core] = other[offset]
        for owner in range(owners):
            expand_grad[owner] = jnp.concatenate(
                [
                    pieces[slot, :owned, owner * units_piece : (owner + 1) * units_piece].astype(
                        jnp.float32
                    )
                    for slot in range(2 * groups)
                ],
                axis=1,
            )

    renew_into(expand_in, expand_out, expand_grad[step], 0.03)
    slots = 2 * groups // owners
    for index in range(slots):
        slot = slots * step + index
        gradient = jnp.concatenate(
            [pieces[slot, owned : owned + units_piece], pieces[slot, owned + units_piece :]],
            axis=1,
        )
        rows = slice(index * units_piece, (index + 1) * units_piece)
        renew_into(reduce_in, reduce_out, gradient.astype(jnp.float32), 0.02, (rows, slice(None)))


def renew_feed(place, mine, other, expand_state, reduce_state):
    groups, depth, units = mine.shape
    owned, hidden_count = expand_state[0].shape
    owned_units, features = reduce_state[0].shape
    owners = hidden_count // owned_units
    whole = pl.BlockSpec(mine.shape, lambda j, _: (0, 0, 0))
    across = pl.BlockSpec((owned, owned_units), lambda j, _: (0, j))
    down = pl.BlockSpec((owned_units // owners, features), lambda j, _: (j, 0))
    shapes = [jax.ShapeDtypeStruct(array.shape, jnp.float32) for array in expand_state]
    shapes += [jax.ShapeDtypeStruct(array.shape, jnp.float32) for array in reduce_state]
    results = pl.pallas_call(
        renew_feed_kernel,
        grid_spec=pltpu.PrefetchScalarGridSpec(
            num_scalar_prefetch=1,
            grid=(owners,),
            in_specs=[whole] * 2 + [across] * 3 + [down] * 3,
            out_specs=[across] * 3 + [down] * 3,
            scratch_shapes=[
                pltpu.VMEM((2 * groups, depth, units), low),
                pltpu.VMEM((owners, owned, owned_units), jnp.float32),
            ],
        ),
        out_shape=shapes,
        compiler_params=pltpu.CompilerParams(vmem_limit_bytes=vmem_bytes),
        cost_estimate=pl.CostEstimate(
            flops=40 * owned * hidden_count, bytes_accessed=48 * owned * hidden_count,
            transcendentals=4 * owned * hidden_count,
        ),
        name="renew_feed",
    )(place, mine, other, *expand_state, *reduce_state)
    return results[:3], results[3:]


def renew_first_kernel(place_ref, mine, other, *refs):
    inputs_in, output_in, inputs_out, output_out = (refs[3 * i : 3 * i + 3] for i in range(4))
    (pieces,) = refs[12:]
    step = pl.program_id(0)
    groups = mine.shape[0]
    group, core = place_ref[0], place_ref[1]
    for offset in range(groups):
        pieces[core, group ^ offset] = mine[offset]
        pieces[1 - core, group ^ offset] = other[offset]
    rows, half = pieces.shape[2:]
    gradient = jnp.concatenate(
        [pieces[side].reshape(groups * rows, half) for side in range(2)], axis=1
    ).astype(jnp.float32)

    @pl.when(step < 3)
    def _():
        renew_into(inputs_in, inputs_out, gradient, 0.03)

    @pl.when(step == 3)
    def _():
        renew_into(output_in, output_out, gradient, 0.3)


def renew_first(place, mine, other, inputs_state, output_state):
    groups, rows, _ = mine.shape
    owned, features = output_state[0].shape
    half = features // 2
    piece = pl.BlockSpec((groups, rows, half), lambda j, _: (0, 0, j))
    across = pl.BlockSpec((owned, features), lambda j, _: (0, jnp.minimum(j, 2)))
    whole = pl.BlockSpec((owned, features), lambda j, _: (0, 0))
    shapes = [jax.ShapeDtypeStruct(array.shape, jnp.float32) for array in inputs_state]
    shapes += [jax.ShapeDtypeStruct(array.shape, jnp.float32) for array in output_state]
    results = pl.pallas_call(
        renew_first_kernel,
        grid_spec=pltpu.PrefetchScalarGridSpec(
            num_scalar_prefetch=1,
            grid=(4,),
            in_specs=[piece] * 2 + [across] * 3 + [whole] * 3,
            out_specs=[across] * 3 + [whole] * 3,
            scratch_shapes=[pltpu.VMEM((2, groups, rows, half), low)],
        ),
        out_shape=shapes,
        compiler_params=pltpu.CompilerParams(vmem_limit_bytes=vmem_bytes),
        cost_estimate=pl.CostEstimate(
            flops=80 * owned * features, bytes_accessed=96 * owned * features,
            transcendentals=8 * owned * features,
        ),
        name="renew_first",
    )(place, mine, other, *inputs_state, *output_state)
    return results[:3], results[3:]


def chip_routes(dp_count, seq_count):
    straight, crossed = [], []
    for place in range(dp_count):
        group, core = place - place % 2, place % 2
        for quarter in range(seq_count):
            source = place * seq_count + quarter
            holder = (group + quarter // 2) * seq_count
            straight.append((source, holder + 2 * core + quarter % 2))
            crossed.append((source, holder + 2 * core + 1 - quarter % 2))
    return straight, crossed


def on_device(
    dp_count,
    seq_count,
    activations,
    cotangent,
    segment_ids,
    inputs_weight,
    inputs_moment,
    inputs_second,
    output_weight,
    output_moment,
    output_second,
    expand_weight,
    expand_moment,
    expand_second,
    reduce_weight,
    reduce_moment,
    reduce_second,
    vector_params,
    vector_moment,
    vector_second,
):
    axes = ("dp", "seq")
    dp_index = lax.axis_index("dp")
    seq_index = lax.axis_index("seq")
    core = dp_index % 2
    group = dp_index // 2
    groups = dp_count // 2
    four_chips = groups == 4
    odd = seq_index % 2
    features = activations.shape[2]
    quarter = activations.shape[1]
    half = features // 2
    owned = inputs_weight.shape[0]
    owned_units = reduce_weight.shape[0]
    rows_piece = owned // groups
    units_piece = owned_units // dp_count
    vector_rows = vector_params.shape[0]
    straight, crossed = chip_routes(dp_count, seq_count)
    core_pairs = [(place, place ^ 1) for place in range(dp_count)]
    x_pairs = [(place, place ^ 2) for place in range(dp_count)]
    y_pairs = [(place, place ^ 4) for place in range(dp_count)]
    far_pairs = [(place, place ^ 6) for place in range(dp_count)]
    same_core = [list(range(first, dp_count, 2)) for first in range(2)]

    def to_chip(values):
        near = lax.dynamic_index_in_dim(values, odd, 0, keepdims=False)
        far = lax.dynamic_index_in_dim(values, 1 - odd, 0, keepdims=False)
        near = lax.ppermute(near, axes, straight)
        far = lax.ppermute(far, axes, crossed)
        return jnp.concatenate(
            [jnp.where(odd == 0, near, far), jnp.where(odd == 0, far, near)], axis=0
        )

    def from_chip_begin(values):
        near = lax.dynamic_slice_in_dim(values, odd * quarter, quarter, 0)
        far = lax.dynamic_slice_in_dim(values, (1 - odd) * quarter, quarter, 0)
        near = lax.ppermute(near, axes, [(there, here) for here, there in straight])
        far = lax.ppermute(far, axes, [(there, here) for here, there in crossed])
        return near, far

    def from_chip_end(near, far):
        return jnp.stack([jnp.where(odd == 0, near, far), jnp.where(odd == 0, far, near)])

    def from_chip(values):
        return from_chip_end(*from_chip_begin(values))

    def swap_cores(values):
        return lax.ppermute(values, "dp", core_pairs)

    def via_x(values):
        return lax.ppermute(values, "dp", x_pairs)

    def via_y(values):
        return lax.ppermute(values, "dp", y_pairs)

    def by_core(mine, theirs, axis):
        return jnp.where(
            core == 0,
            jnp.concatenate([mine, theirs], axis=axis),
            jnp.concatenate([theirs, mine], axis=axis),
        )

    def add_low(*terms):
        return sum(term.astype(jnp.float32) for term in terms).astype(low)

    def after(values, *gates):
        return lax.optimization_barrier((values, gates))[0]

    def gather_z(piece):
        parts = [piece]
        for shift in range(1, seq_count):
            ring = [(place, (place + shift) % seq_count) for place in range(seq_count)]
            parts.append(lax.ppermute(piece, "seq", ring))
        placed = [
            lax.select_n((seq_index - owner) % seq_count, *parts) for owner in range(seq_count)
        ]
        middle = seq_count // 2
        return jnp.stack(placed[:middle]), jnp.stack(placed[middle:])

    def in_order(own, from_x, from_y, from_far, axis):
        x_set = group % 2 == 1
        y_set = group // 2 == 1
        near_low = jnp.where(x_set, from_x, own)
        near_high = jnp.where(x_set, own, from_x)
        far_low = jnp.where(x_set, from_far, from_y)
        far_high = jnp.where(x_set, from_y, from_far)
        return jnp.stack(
            [
                jnp.where(y_set, far_low, near_low),
                jnp.where(y_set, far_high, near_high),
                jnp.where(y_set, near_low, far_low),
                jnp.where(y_set, near_high, far_high),
            ],
            axis=axis,
        )

    def scatter_begin(own_first, own_second, x_second, y_first, x_sent, y_sent):
        return own_first, own_second, x_second, y_first, via_x(x_sent), via_y(y_sent)

    def scatter_middle(state, *gates):
        own_first, own_second, x_second, y_first, from_x, from_y = state
        from_x, from_y = after((from_x, from_y), *gates)
        near = from_x.shape[0] // 2
        y_first = add_low(y_first, from_x[near:])
        x_second = add_low(x_second, from_y[near:])
        state = (own_first, own_second, from_x[:near], from_y[:near])
        return state + (via_y(y_first), via_x(x_second)), (y_first, x_second)

    def scatter_end(state):
        own_first, own_second, x_first, y_second, y_first, x_second = state
        first = add_low(own_first, x_first, y_first)
        second = add_low(own_second, x_second, y_second)
        return first, second

    def scatter_z_begin(blocks):
        parts = [lax.dynamic_index_in_dim(blocks, seq_index, 0, keepdims=False)]
        for shift in range(1, seq_count):
            target = (seq_index + shift) % seq_count
            sent = lax.dynamic_index_in_dim(blocks, target, 0, keepdims=False)
            ring = [(place, (place + shift) % seq_count) for place in range(seq_count)]
            parts.append(lax.ppermute(sent, "seq", ring))
        return parts

    def scatter_z(blocks):
        return add_low(*scatter_z_begin(blocks))

    def regather_begin(piece):
        return piece, via_x(piece), via_y(piece), lax.ppermute(piece, "dp", far_pairs)

    def regather_end(state):
        mine = in_order(*state, 0)
        return by_core(mine[:, None], swap_cores(mine)[:, None], 1)

    def regather(piece):
        every = lax.all_gather(piece, "dp", axis=0, tiled=False)
        return every.reshape((groups, 2) + piece.shape)

    def corner(weight, column):
        return lax.dynamic_slice(
            weight, (group * rows_piece, column + core * half), (rows_piece, half)
        ).astype(low)

    vector_piece = lax.dynamic_slice_in_dim(vector_params, group * rows_piece, rows_piece, 1)
    first_piece = jnp.concatenate(
        [
            corner(inputs_weight, 0),
            corner(inputs_weight, features),
            corner(inputs_weight, 2 * features),
            corner(output_weight, 0),
            jnp.pad(vector_piece.T.astype(low), ((0, 0), (0, LANES - vector_rows))),
        ],
        axis=1,
    )
    expand_piece = jnp.concatenate(
        [
            lax.dynamic_slice_in_dim(
                expand_weight, owner * owned_units + dp_index * units_piece, units_piece, 1
            ).astype(low)
            for owner in range(seq_count)
        ],
        axis=1,
    )
    reduce_piece = lax.dynamic_slice_in_dim(
        reduce_weight, dp_index * units_piece, units_piece, 0
    ).astype(low)

    def pack(expand, reduce):
        return jnp.concatenate([expand, reduce[..., :half], reduce[..., half:]], axis=-2)

    residual_low = to_chip(activations)
    first_block = gather_z(first_piece)
    if four_chips:
        feed_block = lax.all_gather(
            pack(expand_piece, reduce_piece), "seq", axis=0, tiled=False
        )
        cotangent = after(cotangent, feed_block)
    grad_top = to_chip(cotangent)
    rows_here = residual_low.shape[0]
    residual_other = swap_cores(residual_low)
    grad_top_other = swap_cores(grad_top)
    other_segments = swap_cores(segment_ids)
    segment_pair = jnp.where(seq_index // 2 == core, segment_ids, other_segments)
    segments = lax.dynamic_index_in_dim(segment_pair, odd, 0, keepdims=False)
    seg_row, seg_col = segments[None, :], segments[:, None]

    if four_chips:
        first_all = jnp.concatenate(first_block, axis=0)
        first_x, first_y = via_x(first_all), via_y(first_all)
        middle_owner = seq_count // 2
        first_far = jnp.concatenate(
            [via_y(first_x[:middle_owner]), via_x(first_y[middle_owner:])], axis=0
        )
        first_low = in_order(first_all, first_x, first_y, first_far, 1)
    else:
        first_low = lax.all_gather(
            jnp.concatenate(first_block, axis=0),
            "dp",
            axis=1,
            tiled=False,
            axis_index_groups=same_core,
        )
    first_low = first_low.reshape(features, first_low.shape[-1])
    wide = 3 * half
    inputs_low = first_low[:, :wide]
    output_half = first_low[:, wide : wide + half]
    output_all = by_core(output_half, swap_cores(output_half), 1)
    vectors = first_low[:, wide + half : wide + half + vector_rows].T.astype(jnp.float32)

    expand_bias = vectors[8:].reshape(seq_count, dp_count, units_piece)
    block_units = seq_count * owned_units // 8
    if four_chips:
        feed_x, feed_y = via_x(feed_block), via_y(feed_block)
        middle_owner = seq_count // 2
        feed_far = (via_y(feed_x[:middle_owner]), via_x(feed_y[middle_owner:]))
        blocks = [(feed_block,), (feed_x,), (feed_y,), feed_far]
        biases = jnp.concatenate(
            [
                lax.dynamic_index_in_dim(expand_bias, dp_index ^ (2 * offset), 1, keepdims=False)
                for offset in range(4)
            ],
            axis=0,
        )
    else:
        expand_all = lax.all_gather(
            jnp.concatenate(gather_z(expand_piece), axis=0).reshape(features, -1),
            "dp",
            axis=1,
            axis_index_groups=same_core,
        ).reshape(seq_count, owned, 4, block_units)
        reduce_all = lax.all_gather(
            jnp.concatenate(gather_z(reduce_piece), axis=0).reshape(-1, features),
            "dp",
            axis=0,
            axis_index_groups=same_core,
        ).reshape(4, seq_count, -1, features)
        picked = lax.dynamic_index_in_dim(
            expand_bias.reshape(seq_count, groups, 2, units_piece), core, 2, keepdims=False
        )
        biases = picked.transpose(1, 0, 2).reshape(4 * seq_count, block_units // seq_count)
        blocks = []
        for index in range(4):
            packed = pack(expand_all[:, :, index], reduce_all[index])
            blocks.append((packed[: seq_count // 2], packed[seq_count // 2 :]))

    def tokens_of(values, which):
        return lax.dynamic_slice_in_dim(values, which * rows_here, rows_here, 0)

    def heads_part(vector):
        return lax.dynamic_slice_in_dim(vector, core * half, half, 0)

    unit_all, _ = normalize(by_core(residual_low, residual_other, 0).astype(jnp.float32))
    normed_one = (unit_all * vectors[0] + vectors[1]).astype(low)
    input_bias = jnp.concatenate(
        [heads_part(vectors[4]), jnp.zeros((half,), jnp.float32), heads_part(vectors[5])]
    )
    projected = (dot_nn(normed_one, inputs_low) + input_bias).astype(low)
    if four_chips:
        projected = after(projected, feed_block)
    mixture_heads, logs_all = attend_forward(seg_row, seg_col, projected)
    if four_chips:
        mixture_heads = after(mixture_heads, grad_top, feed_x, feed_y)
    mixture_theirs = swap_cores(tokens_of(mixture_heads, 1 - core))
    mixture = by_core(tokens_of(mixture_heads, core), mixture_theirs, 1)

    residual = residual_low.astype(jnp.float32)
    middle = residual + (dot_nn(mixture, output_all) + vectors[6])
    unit_two, inverse_two = normalize(middle)
    normed_two = (unit_two * vectors[2] + vectors[3]).astype(low)
    if four_chips:
        normed_two = after(normed_two, feed_far)
    normed_pair = (normed_two, swap_cores(normed_two))
    top_pair = (grad_top, grad_top_other)
    sums, grads, bias_grads = feed_blocks(normed_pair, top_pair, blocks, biases)
    grad_normed_two = sums[2] + swap_cores(sums[3]).astype(jnp.float32)
    reduced = sums[0] + swap_cores(sums[1]).astype(jnp.float32)
    output_low = (middle + (reduced + vectors[7])).astype(low)

    if four_chips:
        feed_state = scatter_begin(*grads)
        place = jnp.arange(dp_count)[None, :, None]
        bias_sums = sum(
            jnp.where(
                place == (dp_index ^ (2 * offset)),
                bias_grads[seq_count * offset : seq_count * (offset + 1), None, :],
                0.0,
            )
            for offset in range(4)
        )
    else:
        middle_owner = seq_count // 2
        x_near, x_far = grads[4][:middle_owner], grads[4][middle_owner:]
        y_near, y_far = grads[5][:middle_owner], grads[5][middle_owner:]
        pairs = ((grads[0], grads[1]), (x_near, grads[2]), (grads[3], y_near), (x_far, y_far))
        packed = [jnp.concatenate(pair, axis=0) for pair in pairs]
        expand_sum = jnp.stack([part[:, :owned] for part in packed], axis=2)
        expand_sum = expand_sum.reshape(features, groups, -1).transpose(1, 0, 2)
        expand_sum = lax.psum_scatter(expand_sum, "dp", axis_index_groups=same_core)
        reduce_sum = [part[:, owned:].reshape(seq_count, 2, -1, half) for part in packed]
        reduce_sum = jnp.stack([part.transpose(0, 2, 1, 3) for part in reduce_sum])
        reduce_sum = reduce_sum.reshape(groups, -1, features)
        reduce_sum = lax.psum_scatter(reduce_sum, "dp", axis_index_groups=same_core)
        bias_sums = bias_grads.reshape(groups, seq_count, units_piece).transpose(1, 0, 2)
        is_core = jnp.arange(2)[None, None, :, None] == core
        bias_sums = jnp.where(is_core, bias_sums[:, :, None, :], 0.0)

    grad_middle = grad_top.astype(jnp.float32) + norm_back(
        grad_normed_two, vectors[2], unit_two, inverse_two
    )
    grad_attended = grad_middle.astype(low)
    grad_output = dot_tn(mixture, grad_attended).astype(low)
    grad_mixture = dot_nt(grad_attended, output_all).astype(low)

    def columns_of(values, which):
        return lax.dynamic_slice_in_dim(values, which * half, half, 1)

    grad_theirs = swap_cores(columns_of(grad_mixture, 1 - core))
    grad_joined = by_core(columns_of(grad_mixture, core), grad_theirs, 0)
    if four_chips:
        feed_state, gates = scatter_middle(feed_state, grad_mixture)
        grad_joined = after(grad_joined, *gates)
    grad_heads = attend_backward(seg_row, seg_col, projected, logs_all, grad_joined)
    output_sum = add_low(
        columns_of(grad_output, core), swap_cores(columns_of(grad_output, 1 - core))
    )
    grad_projected = jnp.concatenate(grad_heads, axis=1)
    if four_chips:
        feed_sum = scatter_end(after(feed_state, grad_projected))
        feed_parts = scatter_z_begin(jnp.concatenate(feed_sum, axis=0))
        grad_projected = after(grad_projected, *feed_sum)
    grad_inputs = dot_tn(normed_one, grad_projected).astype(low)
    grad_normed_all = dot_nt(grad_projected, inputs_low)
    grad_normed_one = tokens_of(grad_normed_all, core) + swap_cores(
        tokens_of(grad_normed_all, 1 - core).astype(low)
    ).astype(jnp.float32)
    unit_one, inverse_one = normalize(residual)
    grad_residual = norm_back(grad_normed_one, vectors[0], unit_one, inverse_one)
    input_grad = (grad_middle + grad_residual).astype(low)

    def heads_sum(values):
        return lax.dynamic_update_slice_in_dim(
            jnp.zeros((features,), jnp.float32), column_sum(values), core * half, 0
        )

    head_rows = jnp.stack(
        [
            column_sum(grad_normed_one * unit_one),
            column_sum(grad_normed_one),
            column_sum(grad_normed_two * unit_two),
            column_sum(grad_normed_two),
            heads_sum(grad_heads[0]),
            heads_sum(grad_heads[2]),
            column_sum(grad_attended),
            column_sum(grad_top),
        ]
    )
    grad_vectors = jnp.concatenate([head_rows, bias_sums.reshape(-1, features)], axis=0)
    vector_columns = jnp.pad(grad_vectors.T.astype(low), ((0, 0), (0, LANES - vector_rows)))
    first_grad = jnp.concatenate([grad_inputs, output_sum, vector_columns], axis=1)
    first_grad = first_grad.reshape(seq_count, groups, rows_piece, -1)
    if four_chips:
        middle_owner = seq_count // 2
        split = []
        for offset in range(4):
            split.append(
                [
                    lax.dynamic_index_in_dim(part, group ^ offset, 1, keepdims=False)
                    for part in (first_grad[:middle_owner], first_grad[middle_owner:])
                ]
            )
        feed_piece = add_low(*after(feed_parts, grad_inputs))
        output_parts = from_chip_begin(after(output_low, feed_piece))
        own, to_x, to_y, to_far = after(split, feed_piece)
        first_state = scatter_begin(
            own[0],
            own[1],
            to_x[1],
            to_y[0],
            jnp.concatenate([to_x[0], to_far[0]], axis=0),
            jnp.concatenate([to_y[1], to_far[1]], axis=0),
        )
        first_state, output_parts = after((first_state, output_parts))
        first_state, gates = scatter_middle(first_state)
        first_parts = scatter_z_begin(jnp.concatenate(scatter_end(first_state), axis=0))
        feed_mine = lax.all_gather(
            feed_piece, "dp", axis=0, tiled=False, axis_index_groups=same_core
        )
        feed_mine = after(feed_mine, *gates)
        feed_other = swap_cores(feed_mine)
        place = jnp.stack([group, core]).astype(jnp.int32)
        new_expand, new_reduce = renew_feed(
            jnp.stack([jnp.zeros_like(group), core]).astype(jnp.int32),
            feed_mine,
            feed_other,
            (expand_weight, expand_moment, expand_second),
            (reduce_weight, reduce_moment, reduce_second),
        )
        first_piece_sum = add_low(*first_parts)
        grad_parts = from_chip_begin(after(input_grad, first_piece_sum))
        first_pieces = after(regather_begin(first_piece_sum), new_expand)
        first_mine = jnp.stack(first_pieces)
        first_other, grad_parts = after((swap_cores(first_mine), grad_parts))
        layer_output = from_chip_end(*output_parts)
        new_inputs, new_output = renew_first(
            place,
            first_mine,
            first_other,
            (inputs_weight, inputs_moment, inputs_second),
            (output_weight, output_moment, output_second),
        )
        input_grad = from_chip_end(*grad_parts)
        vector_slice = slice(wide + half, wide + half + vector_rows)
        vector_parts = first_mine[..., vector_slice].astype(jnp.float32) + first_other[
            ..., vector_slice
        ].astype(jnp.float32)
        sum_vectors = in_order(*[vector_parts[offset] for offset in range(4)], 0)
        sum_vectors = sum_vectors.reshape(owned, vector_rows).T
    else:
        first_sum = lax.psum_scatter(
            first_grad, "dp", scatter_dimension=1, axis_index_groups=same_core
        )
        layer_output, input_grad = from_chip(output_low), from_chip(input_grad)
        every_first = regather(scatter_z(first_sum))
        sum_expand = regather(scatter_z(expand_sum.reshape(seq_count, owned, -1)))
        sum_reduce = regather(scatter_z(reduce_sum.reshape(seq_count, units_piece, features)))
    def renew(weight, moment, second, gradient, step_rate, weight_decay):
        return adamw_step(
            weight, moment, second, gradient.astype(jnp.float32), step_rate, weight_decay
        )

    if not four_chips:
        sum_expand = sum_expand.reshape(dp_count, owned, seq_count, units_piece)
        sum_expand = sum_expand.transpose(1, 2, 0, 3).reshape(expand_weight.shape)
        sum_reduce = sum_reduce.reshape(reduce_weight.shape)
        sum_first = every_first.transpose(0, 2, 1, 3)
        sum_inputs = sum_first[..., :wide].reshape(groups, rows_piece, 2, 3, half)
        sum_inputs = sum_inputs.transpose(0, 1, 3, 2, 4).reshape(inputs_weight.shape)
        sum_output = sum_first[..., wide : wide + half].reshape(output_weight.shape)
        sum_vectors = sum_first[..., wide + half : wide + half + vector_rows].astype(jnp.float32)
        sum_vectors = jnp.sum(sum_vectors, axis=2).reshape(owned, vector_rows).T
        new_inputs = renew(inputs_weight, inputs_moment, inputs_second, sum_inputs, 0.03, decay_rate)
        new_output = renew(output_weight, output_moment, output_second, sum_output, 0.3, decay_rate)
        new_expand = renew(expand_weight, expand_moment, expand_second, sum_expand, 0.03, decay_rate)
        new_reduce = renew(reduce_weight, reduce_moment, reduce_second, sum_reduce, 0.02, decay_rate)
    new_vectors = renew(vector_params, vector_moment, vector_second, sum_vectors, 0.5, 0.0)
    return (
        layer_output,
        input_grad,
        *new_inputs,
        *new_output,
        *new_expand,
        *new_reduce,
        *new_vectors,
    )


def solution(mesh):
    tokens = P("dp", "seq", None)
    rows = P("seq", None)
    columns = P(None, "seq")
    in_specs = (tokens, tokens, P("dp", None)) + (rows,) * 12 + (columns,) * 3
    out_specs = (tokens, tokens) + (rows,) * 12 + (columns,) * 3
    return jax.shard_map(
        partial(on_device, mesh.shape["dp"], mesh.shape["seq"]),
        mesh=mesh,
        in_specs=in_specs,
        out_specs=out_specs,
        check_vma=False,
    )
```

```python
from functools import partial

import jax
import jax.numpy as jnp
from jax import lax
from jax.experimental import pallas as pl
from jax.experimental.pallas import tpu as pltpu
from jax.sharding import PartitionSpec as P

HEADS = 12
HD = 64
STEP = 10
PAIR = 2 * HD
LANES = 128

eps_norm = 1e-05
eps_adam = 1e-08
beta_one = 0.9
beta_two = 0.95
decay_rate = 0.1
mask_fill = -1e30
vmem_bytes = 56 * 1024 * 1024

VISIBLE = (
    (0, 256, 0, 256),
    (256, 256, 128, 512),
    (512, 256, 128, 768),
    (768, 128, 128, 896),
    (896, 128, 768, 1024),
)
TILE_STARTS = []
tile_total = 0
for _first, _rows, _low, _high in VISIBLE:
    TILE_STARTS.append(tile_total)
    tile_total += _high - _low

low = jnp.bfloat16


def dot_nn(left_side, right_side):
    return lax.dot_general(
        left_side, right_side, (((1,), (0,)), ((), ())), preferred_element_type=jnp.float32
    )


def dot_tn(left_side, right_side):
    return lax.dot_general(
        left_side, right_side, (((0,), (0,)), ((), ())), preferred_element_type=jnp.float32
    )


def dot_nt(left_side, right_side):
    return lax.dot_general(
        left_side, right_side, (((1,), (1,)), ((), ())), preferred_element_type=jnp.float32
    )


def normalize(values):
    center = jnp.mean(values, axis=-1, keepdims=True)
    offsets = values - center
    spread = jnp.mean(offsets * offsets, axis=-1, keepdims=True)
    inverse = lax.rsqrt(spread + eps_norm)
    return offsets * inverse, inverse


def norm_back(grad_normed, gain, unit, inverse):
    scaled = grad_normed * gain
    mean_scaled = jnp.mean(scaled, axis=-1, keepdims=True)
    mean_cross = jnp.mean(scaled * unit, axis=-1, keepdims=True)
    return inverse * (scaled - mean_scaled - unit * mean_cross)


def adamw_step(weight, moment, second, gradient, step_rate, weight_decay):
    moment_new = beta_one * moment + (1.0 - beta_one) * gradient
    second_new = beta_two * second + (1.0 - beta_two) * gradient * gradient
    fix_one = 1.0 - beta_one**STEP
    fix_two = 1.0 - beta_two**STEP
    update = moment_new / fix_one / (jnp.sqrt(second_new / fix_two) + eps_adam)
    return (weight - step_rate * (update + weight_decay * weight), moment_new, second_new)


def column_sum(values):
    return jnp.sum(values.astype(jnp.float32), axis=0)


def fill_bias(seg_row, seg_col, bias):
    for (first, rows, key_low, key_high), start in zip(VISIBLE, TILE_STARTS):
        keys = key_high - key_low
        key_places = key_low + lax.broadcasted_iota(jnp.int32, (keys, rows), 0)
        query_places = first + lax.broadcasted_iota(jnp.int32, (keys, rows), 1)
        same = seg_col[key_low:key_high, :] == seg_row[:, first : first + rows]
        allowed = same & (key_places <= query_places)
        bias[start : start + keys, 0:rows] = jnp.where(allowed, 0.0, mask_fill)


def lane_masks(shape):
    lane = lax.broadcasted_iota(jnp.int32, shape, 1)
    return (lane < HD, lane >= HD)


def masked_to(values, mask):
    return jnp.where(mask, values, jnp.zeros_like(values))


def attend_forward_kernel(seg_row, seg_col, q_ref, k_ref, v_ref, out_ref, log_ref, bias):
    @pl.when(pl.program_id(0) == 0)
    def _():
        fill_bias(seg_row, seg_col, bias)

    masks = lane_masks((k_ref.shape[0], PAIR))
    keys_masked = [masked_to(k_ref[...], mask) for mask in masks]
    for (first, rows, key_low, key_high), start in zip(VISIBLE, TILE_STARTS):
        queries = q_ref[first : first + rows, :] * jnp.asarray(HD**-0.5, low)
        values = v_ref[key_low:key_high, :]
        mixed = []
        for head in range(2):
            scores = dot_nt(keys_masked[head][key_low:key_high], queries)
            scores = scores + bias[start : start + key_high - key_low, 0:rows]
            highest = jnp.max(scores, axis=0, keepdims=True)
            exponent = jnp.exp(scores - highest)
            totals = jnp.sum(exponent, axis=0, keepdims=True)
            soft = (exponent * (1.0 / totals)).astype(low)
            mixed.append(dot_tn(soft, values))
            log_ref[0, head : head + 1, first : first + rows] = highest + jnp.log(totals)
        half = lane_masks((rows, PAIR))[0]
        out_ref[first : first + rows, :] = jnp.where(half, mixed[0], mixed[1]).astype(low)


def attend_backward_kernel(
    seg_row, seg_col, q_ref, k_ref, v_ref, log_ref, do_ref, dq_ref, dk_ref, dv_ref, bias, dk_acc, dv_acc
):
    @pl.when(pl.program_id(0) == 0)
    def _():
        fill_bias(seg_row, seg_col, bias)

    masks = lane_masks((k_ref.shape[0], PAIR))
    keys_masked = [masked_to(k_ref[...], mask) for mask in masks]
    values_masked = [masked_to(v_ref[...], mask) for mask in masks]
    dk_acc[...] = jnp.zeros_like(dk_acc)
    dv_acc[...] = jnp.zeros_like(dv_acc)
    for (first, rows, key_low, key_high), start in zip(VISIBLE, TILE_STARTS):
        queries = q_ref[first : first + rows, :] * jnp.asarray(HD**-0.5, low)
        grads = do_ref[first : first + rows, :]
        grad_query = jnp.zeros((rows, PAIR), jnp.float32)
        row_masks = lane_masks((rows, PAIR))
        for head in range(2):
            keys = keys_masked[head][key_low:key_high]
            scores = dot_nt(keys, queries)
            scores = scores + bias[start : start + key_high - key_low, 0:rows]
            soft = jnp.exp(scores - log_ref[0, head : head + 1, first : first + rows])
            grad_soft = dot_nt(values_masked[head][key_low:key_high], grads)
            inner = jnp.sum(soft * grad_soft, axis=0, keepdims=True)
            grad_scores = (soft * (grad_soft - inner)).astype(low)
            dv_acc[key_low:key_high, :] += dot_nn(
                soft.astype(low), masked_to(grads, row_masks[head])
            )
            dk_acc[key_low:key_high, :] += dot_nn(
                grad_scores, masked_to(queries, row_masks[head])
            )
            grad_query = grad_query + dot_tn(grad_scores, keys)
        dq_ref[first : first + rows, :] = (grad_query * HD**-0.5).astype(low)
    dk_ref[...] = dk_acc[...].astype(low)
    dv_ref[...] = dv_acc[...].astype(low)


def attend_specs(length, pairs):
    whole = lambda shape: pl.BlockSpec(shape, lambda j: (0,) * len(shape))
    columns = lambda offset: pl.BlockSpec((length, PAIR), lambda j, offset=offset: (0, offset + j))
    logs = pl.BlockSpec((1, 8, length), lambda j: (j, 0, 0))
    return whole, columns, logs


def attend_forward(seg_row, seg_col, projected):
    length = projected.shape[0]
    pairs = projected.shape[1] // (3 * PAIR)
    whole, columns, logs = attend_specs(length, pairs)
    return pl.pallas_call(
        attend_forward_kernel,
        grid=(pairs,),
        in_specs=[
            whole((1, length)),
            whole((length, 1)),
            columns(0),
            columns(pairs),
            columns(2 * pairs),
        ],
        out_specs=[columns(0), logs],
        out_shape=[
            jax.ShapeDtypeStruct((length, pairs * PAIR), low),
            jax.ShapeDtypeStruct((pairs, 8, length), jnp.float32),
        ],
        scratch_shapes=[pltpu.VMEM((tile_total, 256), jnp.float32)],
        compiler_params=pltpu.CompilerParams(vmem_limit_bytes=vmem_bytes),
        cost_estimate=pl.CostEstimate(
            flops=4 * length * length * pairs * PAIR, bytes_accessed=8 * length * pairs * PAIR,
            transcendentals=length * length * pairs,
        ),
        name="attend_forward",
    )(seg_row, seg_col, projected, projected, projected)


def attend_backward(seg_row, seg_col, projected, logs_all, grad_mixture):
    length = projected.shape[0]
    pairs = projected.shape[1] // (3 * PAIR)
    whole, columns, logs = attend_specs(length, pairs)
    return pl.pallas_call(
        attend_backward_kernel,
        grid=(pairs,),
        in_specs=[
            whole((1, length)),
            whole((length, 1)),
            columns(0),
            columns(pairs),
            columns(2 * pairs),
            logs,
            columns(0),
        ],
        out_specs=[columns(0)] * 3,
        out_shape=[jax.ShapeDtypeStruct((length, pairs * PAIR), low)] * 3,
        scratch_shapes=[
            pltpu.VMEM((tile_total, 256), jnp.float32),
            pltpu.VMEM((length, PAIR), jnp.float32),
            pltpu.VMEM((length, PAIR), jnp.float32),
        ],
        compiler_params=pltpu.CompilerParams(vmem_limit_bytes=vmem_bytes),
        cost_estimate=pl.CostEstimate(
            flops=10 * length * length * pairs * PAIR, bytes_accessed=14 * length * pairs * PAIR,
            transcendentals=length * length * pairs,
        ),
        name="attend_backward",
    )(seg_row, seg_col, projected, projected, projected, logs_all, grad_mixture)


def feed_kernel(part_counts, *refs):
    refs = list(refs)
    take = lambda count: [refs.pop(0) for _ in range(count)]
    normed = [ref[...] for ref in take(2)]
    tops = [ref[...] for ref in take(2)]
    blocks = [take(count) for count in part_counts]
    bias_ref = take(1)[0]
    reduced, reduced_out, back, back_out = take(4)
    outs = [take(2) for _ in part_counts]
    dbu_ref = take(1)[0]
    turned, weights, grads, reduced_sum, back_sum, in_sems, out_sems = refs
    owners, depth, units = weights.shape[2:]
    side_rows = units // (2 * owners)
    split = depth - 2 * side_rows
    arrivals = [
        [
            pltpu.make_async_copy(
                parts[part] if len(parts) == 2 else parts[0].at[pl.ds(part * owners, owners)],
                weights.at[index, part],
                in_sems.at[index, part],
            )
            for part in range(2)
        ]
        for index, parts in enumerate(blocks)
    ]
    for copies in arrivals:
        for copy in copies:
            copy.start()
    rows = normed[0].shape[0]
    reduced_sums = (reduced, reduced_sum)
    back_sums = (back, back_sum)
    for side in range(2):
        turned[:, side * rows : (side + 1) * rows] = normed[side].T
    departures = []
    for index, grad_refs in enumerate(outs):
        for copy in arrivals[index]:
            copy.wait()
        places = [(part, owner) for part in range(2) for owner in range(owners)]
        expand = jnp.concatenate([weights[index, part, owner, :split] for part, owner in places], axis=0)
        reduce = jnp.concatenate(
            [
                jnp.concatenate(
                    [
                        weights[index, part, owner, split : split + side_rows],
                        weights[index, part, owner, split + side_rows :],
                    ],
                    axis=1,
                )
                for part, owner in places
            ],
            axis=0,
        )
        bias_rows = range(2 * owners * index, 2 * owners * (index + 1))
        bias = jnp.concatenate([bias_ref[row : row + 1, :] for row in bias_rows], axis=1)
        hiddens, slopes = [], []
        for side in range(2):
            expanded = dot_nn(normed[side], expand) + bias
            phi = 0.5 + 0.5 * lax.erf(expanded * (0.5**0.5))
            density = jnp.exp(-0.5 * expanded * expanded) * 0.3989422804014327
            hiddens.append((expanded * phi).astype(low))
            grad_hidden = dot_nt(tops[side], reduce)
            slopes.append((grad_hidden * (phi + expanded * density)).astype(low))
        for side in range(2):
            down = dot_nn(hiddens[side], reduce)
            up = dot_nt(slopes[side], expand)
            if index:
                reduced_sums[side][...] += down
                back_sums[side][...] += up
            else:
                reduced_sums[side][...] = down
                back_sums[side][...] = up
        grad_both = jnp.concatenate(slopes, axis=0)
        grad_reduce = sum(dot_tn(hiddens[side], tops[side]) for side in range(2)).astype(low)
        for place, (part, owner) in enumerate(places):
            grads[index, part, owner, :split] = dot_nn(
                turned[place * split : (place + 1) * split, :], grad_both
            ).astype(low)
            rows_down = grad_reduce[place * side_rows : (place + 1) * side_rows]
            grads[index, part, owner, split : split + side_rows] = rows_down[:, :units]
            grads[index, part, owner, split + side_rows :] = rows_down[:, units:]
        bias_grad = jnp.sum(grad_both.astype(jnp.float32), axis=0, keepdims=True)
        for place, row in enumerate(bias_rows):
            dbu_ref[row : row + 1, :] = bias_grad[:, place * side_rows : (place + 1) * side_rows]
        for part in range(2):
            departures.append(
                pltpu.make_async_copy(
                    grads.at[index, part], grad_refs[part], out_sems.at[index, part]
                )
            )
            departures[-1].start()
    reduced_out[...] = reduced_sum[...].astype(low)
    back_out[...] = back_sum[...].astype(low)
    for copy in departures:
        copy.wait()


def feed_blocks(normed, tops, blocks, biases):
    rows, features = normed[0].shape
    count = len(blocks)
    units = biases.shape[0] * biases.shape[1] // count
    operands = [*normed, *tops]
    in_vmem = pl.BlockSpec(memory_space=pltpu.VMEM)
    anywhere = pl.BlockSpec(memory_space=pl.ANY)
    sum_shape = jax.ShapeDtypeStruct((rows, features), jnp.float32)
    sent_shape = jax.ShapeDtypeStruct((rows, features), low)
    shapes = [sum_shape, sent_shape, sum_shape, sent_shape]
    part_shape = blocks[-1][0].shape
    for parts in blocks:
        operands += parts
        shapes += [jax.ShapeDtypeStruct(part_shape, low)] * 2
    operands += [biases]
    shapes += [jax.ShapeDtypeStruct(biases.shape, jnp.float32)]
    part_counts = [len(parts) for parts in blocks]
    results = pl.pallas_call(
        partial(feed_kernel, part_counts),
        in_specs=[in_vmem] * 4 + [anywhere] * sum(part_counts) + [in_vmem],
        out_specs=[in_vmem] * 4 + [anywhere] * (2 * count) + [in_vmem],
        out_shape=shapes,
        scratch_shapes=[
            pltpu.VMEM((features, 2 * rows), low),
            pltpu.VMEM((count, 2) + part_shape, low),
            pltpu.VMEM((count, 2) + part_shape, low),
            pltpu.VMEM((rows, features), jnp.float32),
            pltpu.VMEM((rows, features), jnp.float32),
            pltpu.SemaphoreType.DMA((count, 2)),
            pltpu.SemaphoreType.DMA((count, 2)),
        ],
        compiler_params=pltpu.CompilerParams(vmem_limit_bytes=vmem_bytes),
        cost_estimate=pl.CostEstimate(
            flops=24 * rows * features * units * count,
            bytes_accessed=8 * features * units * count,
            transcendentals=4 * rows * units * count,
        ),
        name="feed_blocks",
    )(*operands)
    grads = [results[4 + 2 * index : 6 + 2 * index] for index in range(count)]
    return results[:4], grads, results[-1]


def renew_into(sources, targets, gradient, step_rate, place=Ellipsis):
    weight, moment, second = (ref[place] for ref in sources)
    results = adamw_step(weight, moment, second, gradient, step_rate, decay_rate)
    for ref, result in zip(targets, results):
        ref[place] = result


def renew_feed_kernel(place_ref, mine, other, *refs):
    expand_in, reduce_in, expand_out, reduce_out = (refs[3 * i : 3 * i + 3] for i in range(4))
    pieces, expand_grad = refs[12:]
    step = pl.program_id(0)
    groups, depth, units = mine.shape
    owners, owned, features = expand_grad.shape
    units_piece = units // owners

    @pl.when(step == 0)
    def _():
        group, core = place_ref[0], place_ref[1]
        for offset in range(groups):
            slot = 2 * (group ^ offset)
            pieces[slot + core] = mine[offset]
            pieces[slot + 1 - core] = other[offset]
        for owner in range(owners):
            expand_grad[owner] = jnp.concatenate(
                [
                    pieces[slot, :owned, owner * units_piece : (owner + 1) * units_piece].astype(
                        jnp.float32
                    )
                    for slot in range(2 * groups)
                ],
                axis=1,
            )

    renew_into(expand_in, expand_out, expand_grad[step], 0.03)
    slots = 2 * groups // owners
    for index in range(slots):
        slot = slots * step + index
        gradient = jnp.concatenate(
            [pieces[slot, owned : owned + units_piece], pieces[slot, owned + units_piece :]],
            axis=1,
        )
        rows = slice(index * units_piece, (index + 1) * units_piece)
        renew_into(reduce_in, reduce_out, gradient.astype(jnp.float32), 0.02, (rows, slice(None)))


def renew_feed(place, mine, other, expand_state, reduce_state):
    groups, depth, units = mine.shape
    owned, hidden_count = expand_state[0].shape
    owned_units, features = reduce_state[0].shape
    owners = hidden_count // owned_units
    whole = pl.BlockSpec(mine.shape, lambda j, _: (0, 0, 0))
    across = pl.BlockSpec((owned, owned_units), lambda j, _: (0, j))
    down = pl.BlockSpec((owned_units // owners, features), lambda j, _: (j, 0))
    shapes = [jax.ShapeDtypeStruct(array.shape, jnp.float32) for array in expand_state]
    shapes += [jax.ShapeDtypeStruct(array.shape, jnp.float32) for array in reduce_state]
    results = pl.pallas_call(
        renew_feed_kernel,
        grid_spec=pltpu.PrefetchScalarGridSpec(
            num_scalar_prefetch=1,
            grid=(owners,),
            in_specs=[whole] * 2 + [across] * 3 + [down] * 3,
            out_specs=[across] * 3 + [down] * 3,
            scratch_shapes=[
                pltpu.VMEM((2 * groups, depth, units), low),
                pltpu.VMEM((owners, owned, owned_units), jnp.float32),
            ],
        ),
        out_shape=shapes,
        compiler_params=pltpu.CompilerParams(vmem_limit_bytes=vmem_bytes),
        cost_estimate=pl.CostEstimate(
            flops=40 * owned * hidden_count, bytes_accessed=48 * owned * hidden_count,
            transcendentals=4 * owned * hidden_count,
        ),
        name="renew_feed",
    )(place, mine, other, *expand_state, *reduce_state)
    return results[:3], results[3:]


def renew_first_kernel(place_ref, mine, other, *refs):
    inputs_in, output_in, inputs_out, output_out = (refs[3 * i : 3 * i + 3] for i in range(4))
    (pieces,) = refs[12:]
    step = pl.program_id(0)
    groups = mine.shape[0]
    group, core = place_ref[0], place_ref[1]
    for offset in range(groups):
        pieces[core, group ^ offset] = mine[offset]
        pieces[1 - core, group ^ offset] = other[offset]
    rows, half = pieces.shape[2:]
    gradient = jnp.concatenate(
        [pieces[side].reshape(groups * rows, half) for side in range(2)], axis=1
    ).astype(jnp.float32)

    @pl.when(step < 3)
    def _():
        renew_into(inputs_in, inputs_out, gradient, 0.03)

    @pl.when(step == 3)
    def _():
        renew_into(output_in, output_out, gradient, 0.3)


def renew_first(place, mine, other, inputs_state, output_state):
    groups, rows, _ = mine.shape
    owned, features = output_state[0].shape
    half = features // 2
    piece = pl.BlockSpec((groups, rows, half), lambda j, _: (0, 0, j))
    across = pl.BlockSpec((owned, features), lambda j, _: (0, jnp.minimum(j, 2)))
    whole = pl.BlockSpec((owned, features), lambda j, _: (0, 0))
    shapes = [jax.ShapeDtypeStruct(array.shape, jnp.float32) for array in inputs_state]
    shapes += [jax.ShapeDtypeStruct(array.shape, jnp.float32) for array in output_state]
    results = pl.pallas_call(
        renew_first_kernel,
        grid_spec=pltpu.PrefetchScalarGridSpec(
            num_scalar_prefetch=1,
            grid=(4,),
            in_specs=[piece] * 2 + [across] * 3 + [whole] * 3,
            out_specs=[across] * 3 + [whole] * 3,
            scratch_shapes=[pltpu.VMEM((2, groups, rows, half), low)],
        ),
        out_shape=shapes,
        compiler_params=pltpu.CompilerParams(vmem_limit_bytes=vmem_bytes),
        cost_estimate=pl.CostEstimate(
            flops=80 * owned * features, bytes_accessed=96 * owned * features,
            transcendentals=8 * owned * features,
        ),
        name="renew_first",
    )(place, mine, other, *inputs_state, *output_state)
    return results[:3], results[3:]


def chip_routes(dp_count, seq_count):
    straight, crossed = [], []
    for place in range(dp_count):
        group, core = place - place % 2, place % 2
        for quarter in range(seq_count):
            source = place * seq_count + quarter
            holder = (group + quarter // 2) * seq_count
            straight.append((source, holder + 2 * core + quarter % 2))
            crossed.append((source, holder + 2 * core + 1 - quarter % 2))
    return straight, crossed


def on_device(
    dp_count,
    seq_count,
    activations,
    cotangent,
    segment_ids,
    inputs_weight,
    inputs_moment,
    inputs_second,
    output_weight,
    output_moment,
    output_second,
    expand_weight,
    expand_moment,
    expand_second,
    reduce_weight,
    reduce_moment,
    reduce_second,
    vector_params,
    vector_moment,
    vector_second,
):
    axes = ("dp", "seq")
    dp_index = lax.axis_index("dp")
    seq_index = lax.axis_index("seq")
    core = dp_index % 2
    group = dp_index // 2
    groups = dp_count // 2
    four_chips = groups == 4
    odd = seq_index % 2
    features = activations.shape[2]
    quarter = activations.shape[1]
    half = features // 2
    owned = inputs_weight.shape[0]
    owned_units = reduce_weight.shape[0]
    rows_piece = owned // groups
    units_piece = owned_units // dp_count
    vector_rows = vector_params.shape[0]
    straight, crossed = chip_routes(dp_count, seq_count)
    core_pairs = [(place, place ^ 1) for place in range(dp_count)]
    x_pairs = [(place, place ^ 2) for place in range(dp_count)]
    y_pairs = [(place, place ^ 4) for place in range(dp_count)]
    far_pairs = [(place, place ^ 6) for place in range(dp_count)]
    same_core = [list(range(first, dp_count, 2)) for first in range(2)]

    def to_chip(values):
        near = lax.dynamic_index_in_dim(values, odd, 0, keepdims=False)
        far = lax.dynamic_index_in_dim(values, 1 - odd, 0, keepdims=False)
        near = lax.ppermute(near, axes, straight)
        far = lax.ppermute(far, axes, crossed)
        return jnp.concatenate(
            [jnp.where(odd == 0, near, far), jnp.where(odd == 0, far, near)], axis=0
        )

    def from_chip_begin(values):
        near = lax.dynamic_slice_in_dim(values, odd * quarter, quarter, 0)
        far = lax.dynamic_slice_in_dim(values, (1 - odd) * quarter, quarter, 0)
        near = lax.ppermute(near, axes, [(there, here) for here, there in straight])
        far = lax.ppermute(far, axes, [(there, here) for here, there in crossed])
        return near, far

    def from_chip_end(near, far):
        return jnp.stack([jnp.where(odd == 0, near, far), jnp.where(odd == 0, far, near)])

    def from_chip(values):
        return from_chip_end(*from_chip_begin(values))

    def swap_cores(values):
        return lax.ppermute(values, "dp", core_pairs)

    def via_x(values):
        return lax.ppermute(values, "dp", x_pairs)

    def via_y(values):
        return lax.ppermute(values, "dp", y_pairs)

    def by_core(mine, theirs, axis):
        return jnp.where(
            core == 0,
            jnp.concatenate([mine, theirs], axis=axis),
            jnp.concatenate([theirs, mine], axis=axis),
        )

    def add_low(*terms):
        return sum(term.astype(jnp.float32) for term in terms).astype(low)

    def after(values, *gates):
        return lax.optimization_barrier((values, gates))[0]

    def gather_z_begin(piece):
        parts = [piece]
        for shift in range(1, seq_count):
            ring = [(place, (place + shift) % seq_count) for place in range(seq_count)]
            parts.append(lax.ppermute(piece, "seq", ring))
        return parts

    def gather_z_end(parts):
        return jnp.stack(
            [lax.select_n((seq_index - owner) % seq_count, *parts) for owner in range(seq_count)]
        )

    def gather_z(piece):
        return gather_z_end(gather_z_begin(piece))

    def in_order(own, from_x, from_y, from_far, axis):
        x_set = group % 2 == 1
        y_set = group // 2 == 1
        near_low = jnp.where(x_set, from_x, own)
        near_high = jnp.where(x_set, own, from_x)
        far_low = jnp.where(x_set, from_far, from_y)
        far_high = jnp.where(x_set, from_y, from_far)
        return jnp.stack(
            [
                jnp.where(y_set, far_low, near_low),
                jnp.where(y_set, far_high, near_high),
                jnp.where(y_set, near_low, far_low),
                jnp.where(y_set, near_high, far_high),
            ],
            axis=axis,
        )

    def scatter_begin(own, to_x, to_y, to_far):
        far_first, far_second = via_x(to_far[0]), via_y(to_far[1])
        return *own, to_x[1], to_y[0], far_first, far_second, via_x(to_x[0]), via_y(to_y[1])

    def scatter_begin_joined(own, to_x, to_y, to_far):
        from_x = via_x(jnp.concatenate([to_x[0], to_far[0]], axis=0))
        from_y = via_y(jnp.concatenate([to_y[1], to_far[1]], axis=0))
        near = to_x[0].shape[0]
        return *own, to_x[1], to_y[0], from_x[near:], from_y[near:], from_x[:near], from_y[:near]

    def scatter_middle(state, *gates):
        own_first, own_second, x_second, y_first, far_first, far_second = state[:6]
        far_first, far_second = after((far_first, far_second), *gates)
        y_first = add_low(y_first, far_first)
        x_second = add_low(x_second, far_second)
        return (own_first, own_second, *state[6:], via_y(y_first), via_x(x_second)), (
            y_first,
            x_second,
        )

    def scatter_end(state):
        own_first, own_second, x_first, y_second, y_first, x_second = state
        first = add_low(own_first, x_first, y_first)
        second = add_low(own_second, x_second, y_second)
        return first, second

    def scatter_z_begin(blocks):
        parts = [lax.dynamic_index_in_dim(blocks, seq_index, 0, keepdims=False)]
        for shift in range(1, seq_count):
            target = (seq_index + shift) % seq_count
            sent = lax.dynamic_index_in_dim(blocks, target, 0, keepdims=False)
            ring = [(place, (place + shift) % seq_count) for place in range(seq_count)]
            parts.append(lax.ppermute(sent, "seq", ring))
        return parts

    def scatter_z(blocks):
        return add_low(*scatter_z_begin(blocks))

    def regather_begin(piece):
        return piece, via_x(piece), via_y(piece), lax.ppermute(piece, "dp", far_pairs)

    def regather_end(state):
        mine = in_order(*state, 0)
        return by_core(mine[:, None], swap_cores(mine)[:, None], 1)

    def regather(piece):
        every = lax.all_gather(piece, "dp", axis=0, tiled=False)
        return every.reshape((groups, 2) + piece.shape)

    def corner(weight, column):
        return lax.dynamic_slice(
            weight, (group * rows_piece, column + core * half), (rows_piece, half)
        ).astype(low)

    vector_piece = lax.dynamic_slice_in_dim(vector_params, group * rows_piece, rows_piece, 1)
    first_piece = jnp.concatenate(
        [
            corner(inputs_weight, 0),
            corner(inputs_weight, features),
            corner(inputs_weight, 2 * features),
            corner(output_weight, 0),
            jnp.pad(vector_piece.T.astype(low), ((0, 0), (0, LANES - vector_rows))),
        ],
        axis=1,
    )
    expand_piece = jnp.concatenate(
        [
            lax.dynamic_slice_in_dim(
                expand_weight, owner * owned_units + dp_index * units_piece, units_piece, 1
            ).astype(low)
            for owner in range(seq_count)
        ],
        axis=1,
    )
    reduce_piece = lax.dynamic_slice_in_dim(
        reduce_weight, dp_index * units_piece, units_piece, 0
    ).astype(low)

    def pack(expand, reduce):
        return jnp.concatenate([expand, reduce[..., :half], reduce[..., half:]], axis=-2)

    residual_low = to_chip(activations)
    first_block = gather_z(first_piece)
    if four_chips:
        feed_arrivals = gather_z_begin(after(pack(expand_piece, reduce_piece), first_block))
    rows_here = residual_low.shape[0]
    residual_other = swap_cores(residual_low)
    other_segments = swap_cores(segment_ids)
    segment_pair = jnp.where(seq_index // 2 == core, segment_ids, other_segments)
    segments = lax.dynamic_index_in_dim(segment_pair, odd, 0, keepdims=False)
    seg_row, seg_col = segments[None, :], segments[:, None]

    if four_chips:
        first_x, first_y = via_x(first_block), via_y(first_block)
        middle_owner = seq_count // 2
        first_far = jnp.concatenate(
            [via_y(first_x[:middle_owner]), via_x(first_y[middle_owner:])], axis=0
        )
        first_low = in_order(first_block, first_x, first_y, first_far, 1)
        feed_block = gather_z_end(after(feed_arrivals, first_far))
    else:
        first_low = lax.all_gather(
            first_block,
            "dp",
            axis=1,
            tiled=False,
            axis_index_groups=same_core,
        )
    first_low = first_low.reshape(features, first_low.shape[-1])
    wide = 3 * half
    inputs_low = first_low[:, :wide]
    output_half = first_low[:, wide : wide + half]
    output_all = by_core(output_half, swap_cores(output_half), 1)
    vectors = first_low[:, wide + half : wide + half + vector_rows].T.astype(jnp.float32)

    expand_bias = vectors[8:].reshape(seq_count, dp_count, units_piece)
    block_units = seq_count * owned_units // 8
    if four_chips:
        feed_x, feed_y = via_x(feed_block), via_y(feed_block)
        middle_owner = seq_count // 2
        feed_far = (via_y(feed_x[:middle_owner]), via_x(feed_y[middle_owner:]))
        blocks = [(feed_block,), (feed_x,), (feed_y,), feed_far]
        biases = jnp.concatenate(
            [
                lax.dynamic_index_in_dim(expand_bias, dp_index ^ (2 * offset), 1, keepdims=False)
                for offset in range(4)
            ],
            axis=0,
        )
    else:
        expand_all = lax.all_gather(
            gather_z(expand_piece).reshape(features, -1),
            "dp",
            axis=1,
            axis_index_groups=same_core,
        ).reshape(seq_count, owned, 4, block_units)
        reduce_all = lax.all_gather(
            gather_z(reduce_piece).reshape(-1, features),
            "dp",
            axis=0,
            axis_index_groups=same_core,
        ).reshape(4, seq_count, -1, features)
        picked = lax.dynamic_index_in_dim(
            expand_bias.reshape(seq_count, groups, 2, units_piece), core, 2, keepdims=False
        )
        biases = picked.transpose(1, 0, 2).reshape(4 * seq_count, block_units // seq_count)
        blocks = []
        for index in range(4):
            packed = pack(expand_all[:, :, index], reduce_all[index])
            blocks.append((packed[: seq_count // 2], packed[seq_count // 2 :]))

    def tokens_of(values, which):
        return lax.dynamic_slice_in_dim(values, which * rows_here, rows_here, 0)

    def heads_part(vector):
        return lax.dynamic_slice_in_dim(vector, core * half, half, 0)

    unit_all, _ = normalize(by_core(residual_low, residual_other, 0).astype(jnp.float32))
    normed_one = (unit_all * vectors[0] + vectors[1]).astype(low)
    input_bias = jnp.concatenate(
        [heads_part(vectors[4]), jnp.zeros((half,), jnp.float32), heads_part(vectors[5])]
    )
    projected = (dot_nn(normed_one, inputs_low) + input_bias).astype(low)
    if four_chips:
        projected = after(projected, feed_block)
        cotangent = after(cotangent, projected)
    grad_top = to_chip(cotangent)
    grad_top_other = swap_cores(grad_top)
    mixture_heads, logs_all = attend_forward(seg_row, seg_col, projected)
    if four_chips:
        mixture_heads = after(mixture_heads, grad_top, feed_x, feed_y)
    mixture_theirs = swap_cores(tokens_of(mixture_heads, 1 - core))
    mixture = by_core(tokens_of(mixture_heads, core), mixture_theirs, 1)

    residual = residual_low.astype(jnp.float32)
    middle = residual + (dot_nn(mixture, output_all) + vectors[6])
    unit_two, inverse_two = normalize(middle)
    normed_two = (unit_two * vectors[2] + vectors[3]).astype(low)
    if four_chips:
        normed_two = after(normed_two, feed_far)
    normed_pair = (normed_two, swap_cores(normed_two))
    top_pair = (grad_top, grad_top_other)
    sums, grads, bias_grads = feed_blocks(normed_pair, top_pair, blocks, biases)
    grad_normed_two = sums[2] + swap_cores(sums[3]).astype(jnp.float32)
    reduced = sums[0] + swap_cores(sums[1]).astype(jnp.float32)
    output_low = (middle + (reduced + vectors[7])).astype(low)

    if four_chips:
        feed_state = scatter_begin(*grads)
        place = jnp.arange(dp_count)[None, :, None]
        bias_sums = sum(
            jnp.where(
                place == (dp_index ^ (2 * offset)),
                bias_grads[seq_count * offset : seq_count * (offset + 1), None, :],
                0.0,
            )
            for offset in range(4)
        )
    else:
        packed = [jnp.concatenate(grad, axis=0) for grad in grads]
        expand_sum = jnp.stack([part[:, :owned] for part in packed], axis=2)
        expand_sum = expand_sum.reshape(features, groups, -1).transpose(1, 0, 2)
        expand_sum = lax.psum_scatter(expand_sum, "dp", axis_index_groups=same_core)
        reduce_sum = [part[:, owned:].reshape(seq_count, 2, -1, half) for part in packed]
        reduce_sum = jnp.stack([part.transpose(0, 2, 1, 3) for part in reduce_sum])
        reduce_sum = reduce_sum.reshape(groups, -1, features)
        reduce_sum = lax.psum_scatter(reduce_sum, "dp", axis_index_groups=same_core)
        bias_sums = bias_grads.reshape(groups, seq_count, units_piece).transpose(1, 0, 2)
        is_core = jnp.arange(2)[None, None, :, None] == core
        bias_sums = jnp.where(is_core, bias_sums[:, :, None, :], 0.0)

    grad_middle = grad_top.astype(jnp.float32) + norm_back(
        grad_normed_two, vectors[2], unit_two, inverse_two
    )
    grad_attended = grad_middle.astype(low)
    grad_output = dot_tn(mixture, grad_attended).astype(low)
    grad_mixture = dot_nt(grad_attended, output_all).astype(low)

    def columns_of(values, which):
        return lax.dynamic_slice_in_dim(values, which * half, half, 1)

    grad_theirs = swap_cores(columns_of(grad_mixture, 1 - core))
    grad_joined = by_core(columns_of(grad_mixture, core), grad_theirs, 0)
    if four_chips:
        feed_state, gates = scatter_middle(feed_state, grad_mixture)
        grad_joined = after(grad_joined, *gates)
    grad_heads = attend_backward(seg_row, seg_col, projected, logs_all, grad_joined)
    output_sum = add_low(
        columns_of(grad_output, core), swap_cores(columns_of(grad_output, 1 - core))
    )
    grad_projected = jnp.concatenate(grad_heads, axis=1)
    if four_chips:
        feed_sum = scatter_end(after(feed_state, grad_projected))
        feed_parts = scatter_z_begin(jnp.concatenate(feed_sum, axis=0))
        grad_projected = after(grad_projected, *feed_sum)
    grad_inputs = dot_tn(normed_one, grad_projected).astype(low)
    grad_normed_all = dot_nt(grad_projected, inputs_low)
    grad_normed_one = tokens_of(grad_normed_all, core) + swap_cores(
        tokens_of(grad_normed_all, 1 - core).astype(low)
    ).astype(jnp.float32)
    unit_one, inverse_one = normalize(residual)
    grad_residual = norm_back(grad_normed_one, vectors[0], unit_one, inverse_one)
    input_grad = (grad_middle + grad_residual).astype(low)

    def heads_sum(values):
        return lax.dynamic_update_slice_in_dim(
            jnp.zeros((features,), jnp.float32), column_sum(values), core * half, 0
        )

    head_rows = jnp.stack(
        [
            column_sum(grad_normed_one * unit_one),
            column_sum(grad_normed_one),
            column_sum(grad_normed_two * unit_two),
            column_sum(grad_normed_two),
            heads_sum(grad_heads[0]),
            heads_sum(grad_heads[2]),
            column_sum(grad_attended),
            column_sum(grad_top),
        ]
    )
    grad_vectors = jnp.concatenate([head_rows, bias_sums.reshape(-1, features)], axis=0)
    vector_columns = jnp.pad(grad_vectors.T.astype(low), ((0, 0), (0, LANES - vector_rows)))
    first_grad = jnp.concatenate([grad_inputs, output_sum, vector_columns], axis=1)
    first_grad = first_grad.reshape(seq_count, groups, rows_piece, -1)
    if four_chips:
        middle_owner = seq_count // 2
        split = []
        for offset in range(4):
            split.append(
                [
                    lax.dynamic_index_in_dim(part, group ^ offset, 1, keepdims=False)
                    for part in (first_grad[:middle_owner], first_grad[middle_owner:])
                ]
            )
        feed_piece = add_low(*after(feed_parts, grad_inputs))
        feed_pieces = regather_begin(feed_piece)
        output_parts = from_chip_begin(after(output_low, feed_piece))
        split, feed_pieces, output_parts = after((split, feed_pieces, output_parts))
        first_state = scatter_begin_joined(*split)
        grad_parts = from_chip_begin(after(input_grad, split))
        first_state, grad_parts = after((first_state, grad_parts))
        first_state, _ = scatter_middle(first_state)
        first_parts = scatter_z_begin(jnp.concatenate(scatter_end(first_state), axis=0))
        feed_mine = jnp.stack(feed_pieces)
        feed_other = swap_cores(feed_mine)
        place = jnp.stack([group, core]).astype(jnp.int32)
        new_expand, new_reduce = renew_feed(
            place,
            feed_mine,
            feed_other,
            (expand_weight, expand_moment, expand_second),
            (reduce_weight, reduce_moment, reduce_second),
        )
        first_parts, new_expand = after((first_parts, new_expand))
        first_pieces = regather_begin(add_low(*first_parts))
        first_mine = jnp.stack(first_pieces)
        first_other = swap_cores(first_mine)
        layer_output = from_chip_end(*output_parts)
        new_inputs, new_output = renew_first(
            place,
            first_mine,
            first_other,
            (inputs_weight, inputs_moment, inputs_second),
            (output_weight, output_moment, output_second),
        )
        input_grad = from_chip_end(*grad_parts)
        vector_slice = slice(wide + half, wide + half + vector_rows)
        vector_parts = first_mine[..., vector_slice].astype(jnp.float32) + first_other[
            ..., vector_slice
        ].astype(jnp.float32)
        sum_vectors = in_order(*[vector_parts[offset] for offset in range(4)], 0)
        sum_vectors = sum_vectors.reshape(owned, vector_rows).T
    else:
        first_sum = lax.psum_scatter(
            first_grad, "dp", scatter_dimension=1, axis_index_groups=same_core
        )
        layer_output, input_grad = from_chip(output_low), from_chip(input_grad)
        every_first = regather(scatter_z(first_sum))
        sum_expand = regather(scatter_z(expand_sum.reshape(seq_count, owned, -1)))
        sum_reduce = regather(scatter_z(reduce_sum.reshape(seq_count, units_piece, features)))
    def renew(weight, moment, second, gradient, step_rate, weight_decay):
        return adamw_step(
            weight, moment, second, gradient.astype(jnp.float32), step_rate, weight_decay
        )

    if not four_chips:
        sum_expand = sum_expand.reshape(dp_count, owned, seq_count, units_piece)
        sum_expand = sum_expand.transpose(1, 2, 0, 3).reshape(expand_weight.shape)
        sum_reduce = sum_reduce.reshape(reduce_weight.shape)
        sum_first = every_first.transpose(0, 2, 1, 3)
        sum_inputs = sum_first[..., :wide].reshape(groups, rows_piece, 2, 3, half)
        sum_inputs = sum_inputs.transpose(0, 1, 3, 2, 4).reshape(inputs_weight.shape)
        sum_output = sum_first[..., wide : wide + half].reshape(output_weight.shape)
        sum_vectors = sum_first[..., wide + half : wide + half + vector_rows].astype(jnp.float32)
        sum_vectors = jnp.sum(sum_vectors, axis=2).reshape(owned, vector_rows).T
        new_inputs = renew(inputs_weight, inputs_moment, inputs_second, sum_inputs, 0.03, decay_rate)
        new_output = renew(output_weight, output_moment, output_second, sum_output, 0.3, decay_rate)
        new_expand = renew(expand_weight, expand_moment, expand_second, sum_expand, 0.03, decay_rate)
        new_reduce = renew(reduce_weight, reduce_moment, reduce_second, sum_reduce, 0.02, decay_rate)
    new_vectors = renew(vector_params, vector_moment, vector_second, sum_vectors, 0.5, 0.0)
    return (
        layer_output,
        input_grad,
        *new_inputs,
        *new_output,
        *new_expand,
        *new_reduce,
        *new_vectors,
    )


def solution(mesh):
    tokens = P("dp", "seq", None)
    rows = P("seq", None)
    columns = P(None, "seq")
    in_specs = (tokens, tokens, P("dp", None)) + (rows,) * 12 + (columns,) * 3
    out_specs = (tokens, tokens) + (rows,) * 12 + (columns,) * 3
    return jax.shard_map(
        partial(on_device, mesh.shape["dp"], mesh.shape["seq"]),
        mesh=mesh,
        in_specs=in_specs,
        out_specs=out_specs,
        check_vma=False,
    )
```

```python
from functools import partial

import jax
import jax.numpy as jnp
from jax import lax
from jax.experimental import pallas as pl
from jax.experimental.pallas import tpu as pltpu
from jax.sharding import PartitionSpec as P

HEADS = 12
HD = 64
STEP = 10
PAIR = 2 * HD
LANES = 128

eps_norm = 1e-05
eps_adam = 1e-08
beta_one = 0.9
beta_two = 0.95
decay_rate = 0.1
mask_fill = -1e30
vmem_bytes = 56 * 1024 * 1024

VISIBLE = (
    (0, 256, 0, 256),
    (256, 256, 128, 512),
    (512, 256, 128, 768),
    (768, 128, 128, 896),
    (896, 128, 768, 1024),
)
TILE_STARTS = []
tile_total = 0
for _first, _rows, _low, _high in VISIBLE:
    TILE_STARTS.append(tile_total)
    tile_total += _high - _low

low = jnp.bfloat16


def dot_nn(left_side, right_side):
    return lax.dot_general(
        left_side, right_side, (((1,), (0,)), ((), ())), preferred_element_type=jnp.float32
    )


def dot_tn(left_side, right_side):
    return lax.dot_general(
        left_side, right_side, (((0,), (0,)), ((), ())), preferred_element_type=jnp.float32
    )


def dot_nt(left_side, right_side):
    return lax.dot_general(
        left_side, right_side, (((1,), (1,)), ((), ())), preferred_element_type=jnp.float32
    )


def normalize(values):
    center = jnp.mean(values, axis=-1, keepdims=True)
    offsets = values - center
    spread = jnp.mean(offsets * offsets, axis=-1, keepdims=True)
    inverse = lax.rsqrt(spread + eps_norm)
    return offsets * inverse, inverse


def norm_back(grad_normed, gain, unit, inverse):
    scaled = grad_normed * gain
    mean_scaled = jnp.mean(scaled, axis=-1, keepdims=True)
    mean_cross = jnp.mean(scaled * unit, axis=-1, keepdims=True)
    return inverse * (scaled - mean_scaled - unit * mean_cross)


def adamw_step(weight, moment, second, gradient, step_rate, weight_decay):
    moment_new = beta_one * moment + (1.0 - beta_one) * gradient
    second_new = beta_two * second + (1.0 - beta_two) * gradient * gradient
    fix_one = 1.0 - beta_one**STEP
    fix_two = 1.0 - beta_two**STEP
    update = moment_new / fix_one / (jnp.sqrt(second_new / fix_two) + eps_adam)
    return (weight - step_rate * (update + weight_decay * weight), moment_new, second_new)


def column_sum(values):
    return jnp.sum(values.astype(jnp.float32), axis=0)


def fill_bias(seg_row, seg_col, bias):
    for (first, rows, key_low, key_high), start in zip(VISIBLE, TILE_STARTS):
        keys = key_high - key_low
        key_places = key_low + lax.broadcasted_iota(jnp.int32, (keys, rows), 0)
        query_places = first + lax.broadcasted_iota(jnp.int32, (keys, rows), 1)
        same = seg_col[key_low:key_high, :] == seg_row[:, first : first + rows]
        allowed = same & (key_places <= query_places)
        bias[start : start + keys, 0:rows] = jnp.where(allowed, 0.0, mask_fill)


def lane_masks(shape):
    lane = lax.broadcasted_iota(jnp.int32, shape, 1)
    return (lane < HD, lane >= HD)


def masked_to(values, mask):
    return jnp.where(mask, values, jnp.zeros_like(values))


def attend_forward_kernel(seg_row, seg_col, q_ref, k_ref, v_ref, out_ref, log_ref, bias):
    @pl.when(pl.program_id(0) == 0)
    def _():
        fill_bias(seg_row, seg_col, bias)

    masks = lane_masks((k_ref.shape[0], PAIR))
    keys_masked = [masked_to(k_ref[...], mask) for mask in masks]
    for (first, rows, key_low, key_high), start in zip(VISIBLE, TILE_STARTS):
        queries = q_ref[first : first + rows, :] * jnp.asarray(HD**-0.5, low)
        values = v_ref[key_low:key_high, :]
        mixed = []
        for head in range(2):
            scores = dot_nt(keys_masked[head][key_low:key_high], queries)
            scores = scores + bias[start : start + key_high - key_low, 0:rows]
            highest = jnp.max(scores, axis=0, keepdims=True)
            exponent = jnp.exp(scores - highest)
            totals = jnp.sum(exponent, axis=0, keepdims=True)
            soft = (exponent * (1.0 / totals)).astype(low)
            mixed.append(dot_tn(soft, values))
            log_ref[0, head : head + 1, first : first + rows] = highest + jnp.log(totals)
        half = lane_masks((rows, PAIR))[0]
        out_ref[first : first + rows, :] = jnp.where(half, mixed[0], mixed[1]).astype(low)


def attend_backward_kernel(
    seg_row, seg_col, q_ref, k_ref, v_ref, log_ref, do_ref, dq_ref, dk_ref, dv_ref, bias, dk_acc, dv_acc
):
    @pl.when(pl.program_id(0) == 0)
    def _():
        fill_bias(seg_row, seg_col, bias)

    masks = lane_masks((k_ref.shape[0], PAIR))
    keys_masked = [masked_to(k_ref[...], mask) for mask in masks]
    values_masked = [masked_to(v_ref[...], mask) for mask in masks]
    dk_acc[...] = jnp.zeros_like(dk_acc)
    dv_acc[...] = jnp.zeros_like(dv_acc)
    for (first, rows, key_low, key_high), start in zip(VISIBLE, TILE_STARTS):
        queries = q_ref[first : first + rows, :] * jnp.asarray(HD**-0.5, low)
        grads = do_ref[first : first + rows, :]
        grad_query = jnp.zeros((rows, PAIR), jnp.float32)
        row_masks = lane_masks((rows, PAIR))
        for head in range(2):
            keys = keys_masked[head][key_low:key_high]
            scores = dot_nt(keys, queries)
            scores = scores + bias[start : start + key_high - key_low, 0:rows]
            soft = jnp.exp(scores - log_ref[0, head : head + 1, first : first + rows])
            grad_soft = dot_nt(values_masked[head][key_low:key_high], grads)
            inner = jnp.sum(soft * grad_soft, axis=0, keepdims=True)
            grad_scores = (soft * (grad_soft - inner)).astype(low)
            dv_acc[key_low:key_high, :] += dot_nn(
                soft.astype(low), masked_to(grads, row_masks[head])
            )
            dk_acc[key_low:key_high, :] += dot_nn(
                grad_scores, masked_to(queries, row_masks[head])
            )
            grad_query = grad_query + dot_tn(grad_scores, keys)
        dq_ref[first : first + rows, :] = (grad_query * HD**-0.5).astype(low)
    dk_ref[...] = dk_acc[...].astype(low)
    dv_ref[...] = dv_acc[...].astype(low)


def attend_specs(length, pairs):
    whole = lambda shape: pl.BlockSpec(shape, lambda j: (0,) * len(shape))
    columns = lambda offset: pl.BlockSpec((length, PAIR), lambda j, offset=offset: (0, offset + j))
    logs = pl.BlockSpec((1, 8, length), lambda j: (j, 0, 0))
    return whole, columns, logs


def attend_forward(seg_row, seg_col, projected):
    length = projected.shape[0]
    pairs = projected.shape[1] // (3 * PAIR)
    whole, columns, logs = attend_specs(length, pairs)
    return pl.pallas_call(
        attend_forward_kernel,
        grid=(pairs,),
        in_specs=[
            whole((1, length)),
            whole((length, 1)),
            columns(0),
            columns(pairs),
            columns(2 * pairs),
        ],
        out_specs=[columns(0), logs],
        out_shape=[
            jax.ShapeDtypeStruct((length, pairs * PAIR), low),
            jax.ShapeDtypeStruct((pairs, 8, length), jnp.float32),
        ],
        scratch_shapes=[pltpu.VMEM((tile_total, 256), jnp.float32)],
        compiler_params=pltpu.CompilerParams(vmem_limit_bytes=vmem_bytes),
        cost_estimate=pl.CostEstimate(
            flops=4 * length * length * pairs * PAIR, bytes_accessed=8 * length * pairs * PAIR,
            transcendentals=length * length * pairs,
        ),
        name="attend_forward",
    )(seg_row, seg_col, projected, projected, projected)


def attend_backward(seg_row, seg_col, projected, logs_all, grad_mixture):
    length = projected.shape[0]
    pairs = projected.shape[1] // (3 * PAIR)
    whole, columns, logs = attend_specs(length, pairs)
    return pl.pallas_call(
        attend_backward_kernel,
        grid=(pairs,),
        in_specs=[
            whole((1, length)),
            whole((length, 1)),
            columns(0),
            columns(pairs),
            columns(2 * pairs),
            logs,
            columns(0),
        ],
        out_specs=[columns(0)] * 3,
        out_shape=[jax.ShapeDtypeStruct((length, pairs * PAIR), low)] * 3,
        scratch_shapes=[
            pltpu.VMEM((tile_total, 256), jnp.float32),
            pltpu.VMEM((length, PAIR), jnp.float32),
            pltpu.VMEM((length, PAIR), jnp.float32),
        ],
        compiler_params=pltpu.CompilerParams(vmem_limit_bytes=vmem_bytes),
        cost_estimate=pl.CostEstimate(
            flops=10 * length * length * pairs * PAIR, bytes_accessed=14 * length * pairs * PAIR,
            transcendentals=length * length * pairs,
        ),
        name="attend_backward",
    )(seg_row, seg_col, projected, projected, projected, logs_all, grad_mixture)


def feed_kernel(part_counts, *refs):
    refs = list(refs)
    take = lambda count: [refs.pop(0) for _ in range(count)]
    normed = [ref[...] for ref in take(2)]
    tops = [ref[...] for ref in take(2)]
    blocks = [take(count) for count in part_counts]
    bias_ref = take(1)[0]
    reduced, reduced_out, back, back_out = take(4)
    outs = [take(2) for _ in part_counts]
    dbu_ref = take(1)[0]
    turned, weights, grads, reduced_sum, back_sum, in_sems, out_sems = refs
    owners, depth, units = weights.shape[2:]
    side_rows = units // (2 * owners)
    split = depth - 2 * side_rows
    arrivals = [
        [
            pltpu.make_async_copy(
                parts[part] if len(parts) == 2 else parts[0].at[pl.ds(part * owners, owners)],
                weights.at[index, part],
                in_sems.at[index, part],
            )
            for part in range(2)
        ]
        for index, parts in enumerate(blocks)
    ]
    for copies in arrivals:
        for copy in copies:
            copy.start()
    rows = normed[0].shape[0]
    reduced_sums = (reduced, reduced_sum)
    back_sums = (back, back_sum)
    for side in range(2):
        turned[:, side * rows : (side + 1) * rows] = normed[side].T
    departures = []
    for index, grad_refs in enumerate(outs):
        for copy in arrivals[index]:
            copy.wait()
        places = [(part, owner) for part in range(2) for owner in range(owners)]
        expand = jnp.concatenate([weights[index, part, owner, :split] for part, owner in places], axis=0)
        reduce = jnp.concatenate(
            [
                jnp.concatenate(
                    [
                        weights[index, part, owner, split : split + side_rows],
                        weights[index, part, owner, split + side_rows :],
                    ],
                    axis=1,
                )
                for part, owner in places
            ],
            axis=0,
        )
        bias_rows = range(2 * owners * index, 2 * owners * (index + 1))
        bias = jnp.concatenate([bias_ref[row : row + 1, :] for row in bias_rows], axis=1)
        hiddens, slopes = [], []
        for side in range(2):
            expanded = dot_nn(normed[side], expand) + bias
            phi = 0.5 + 0.5 * lax.erf(expanded * (0.5**0.5))
            density = jnp.exp(-0.5 * expanded * expanded) * 0.3989422804014327
            hiddens.append((expanded * phi).astype(low))
            grad_hidden = dot_nt(tops[side], reduce)
            slopes.append((grad_hidden * (phi + expanded * density)).astype(low))
        for side in range(2):
            down = dot_nn(hiddens[side], reduce)
            up = dot_nt(slopes[side], expand)
            if index:
                reduced_sums[side][...] += down
                back_sums[side][...] += up
            else:
                reduced_sums[side][...] = down
                back_sums[side][...] = up
        grad_both = jnp.concatenate(slopes, axis=0)
        grad_reduce = sum(dot_tn(hiddens[side], tops[side]) for side in range(2)).astype(low)
        for place, (part, owner) in enumerate(places):
            grads[index, part, owner, :split] = dot_nn(
                turned[place * split : (place + 1) * split, :], grad_both
            ).astype(low)
            rows_down = grad_reduce[place * side_rows : (place + 1) * side_rows]
            grads[index, part, owner, split : split + side_rows] = rows_down[:, :units]
            grads[index, part, owner, split + side_rows :] = rows_down[:, units:]
        bias_grad = jnp.sum(grad_both.astype(jnp.float32), axis=0, keepdims=True)
        for place, row in enumerate(bias_rows):
            dbu_ref[row : row + 1, :] = bias_grad[:, place * side_rows : (place + 1) * side_rows]
        for part in range(2):
            departures.append(
                pltpu.make_async_copy(
                    grads.at[index, part], grad_refs[part], out_sems.at[index, part]
                )
            )
            departures[-1].start()
    reduced_out[...] = reduced_sum[...].astype(low)
    back_out[...] = back_sum[...].astype(low)
    for copy in departures:
        copy.wait()


def feed_blocks(normed, tops, blocks, biases):
    rows, features = normed[0].shape
    count = len(blocks)
    units = biases.shape[0] * biases.shape[1] // count
    operands = [*normed, *tops]
    in_vmem = pl.BlockSpec(memory_space=pltpu.VMEM)
    anywhere = pl.BlockSpec(memory_space=pl.ANY)
    sum_shape = jax.ShapeDtypeStruct((rows, features), jnp.float32)
    sent_shape = jax.ShapeDtypeStruct((rows, features), low)
    shapes = [sum_shape, sent_shape, sum_shape, sent_shape]
    part_shape = blocks[-1][0].shape
    for parts in blocks:
        operands += parts
        shapes += [jax.ShapeDtypeStruct(part_shape, low)] * 2
    operands += [biases]
    shapes += [jax.ShapeDtypeStruct(biases.shape, jnp.float32)]
    part_counts = [len(parts) for parts in blocks]
    results = pl.pallas_call(
        partial(feed_kernel, part_counts),
        in_specs=[in_vmem] * 4 + [anywhere] * sum(part_counts) + [in_vmem],
        out_specs=[in_vmem] * 4 + [anywhere] * (2 * count) + [in_vmem],
        out_shape=shapes,
        scratch_shapes=[
            pltpu.VMEM((features, 2 * rows), low),
            pltpu.VMEM((count, 2) + part_shape, low),
            pltpu.VMEM((count, 2) + part_shape, low),
            pltpu.VMEM((rows, features), jnp.float32),
            pltpu.VMEM((rows, features), jnp.float32),
            pltpu.SemaphoreType.DMA((count, 2)),
            pltpu.SemaphoreType.DMA((count, 2)),
        ],
        compiler_params=pltpu.CompilerParams(vmem_limit_bytes=vmem_bytes),
        cost_estimate=pl.CostEstimate(
            flops=24 * rows * features * units * count,
            bytes_accessed=8 * features * units * count,
            transcendentals=4 * rows * units * count,
        ),
        name="feed_blocks",
    )(*operands)
    grads = [results[4 + 2 * index : 6 + 2 * index] for index in range(count)]
    return results[:4], grads, results[-1]


def renew_into(sources, targets, gradient, step_rate, place=Ellipsis):
    weight, moment, second = (ref[place] for ref in sources)
    results = adamw_step(weight, moment, second, gradient, step_rate, decay_rate)
    for ref, result in zip(targets, results):
        ref[place] = result


def renew_feed_kernel(place_ref, mine, other, *refs):
    expand_in, reduce_in, expand_out, reduce_out = (refs[3 * i : 3 * i + 3] for i in range(4))
    pieces, expand_grad = refs[12:]
    step = pl.program_id(0)
    groups, depth, units = mine.shape
    owners, owned, features = expand_grad.shape
    units_piece = units // owners

    @pl.when(step == 0)
    def _():
        group, core = place_ref[0], place_ref[1]
        for offset in range(groups):
            slot = 2 * (group ^ offset)
            pieces[slot + core] = mine[offset]
            pieces[slot + 1 - core] = other[offset]
        for owner in range(owners):
            expand_grad[owner] = jnp.concatenate(
                [
                    pieces[slot, :owned, owner * units_piece : (owner + 1) * units_piece].astype(
                        jnp.float32
                    )
                    for slot in range(2 * groups)
                ],
                axis=1,
            )

    renew_into(expand_in, expand_out, expand_grad[step], 0.03)
    slots = 2 * groups // owners
    for index in range(slots):
        slot = slots * step + index
        gradient = jnp.concatenate(
            [pieces[slot, owned : owned + units_piece], pieces[slot, owned + units_piece :]],
            axis=1,
        )
        rows = slice(index * units_piece, (index + 1) * units_piece)
        renew_into(reduce_in, reduce_out, gradient.astype(jnp.float32), 0.02, (rows, slice(None)))


def renew_feed(place, mine, other, expand_state, reduce_state):
    groups, depth, units = mine.shape
    owned, hidden_count = expand_state[0].shape
    owned_units, features = reduce_state[0].shape
    owners = hidden_count // owned_units
    whole = pl.BlockSpec(mine.shape, lambda j, _: (0, 0, 0))
    across = pl.BlockSpec((owned, owned_units), lambda j, _: (0, j))
    down = pl.BlockSpec((owned_units // owners, features), lambda j, _: (j, 0))
    shapes = [jax.ShapeDtypeStruct(array.shape, jnp.float32) for array in expand_state]
    shapes += [jax.ShapeDtypeStruct(array.shape, jnp.float32) for array in reduce_state]
    results = pl.pallas_call(
        renew_feed_kernel,
        grid_spec=pltpu.PrefetchScalarGridSpec(
            num_scalar_prefetch=1,
            grid=(owners,),
            in_specs=[whole] * 2 + [across] * 3 + [down] * 3,
            out_specs=[across] * 3 + [down] * 3,
            scratch_shapes=[
                pltpu.VMEM((2 * groups, depth, units), low),
                pltpu.VMEM((owners, owned, owned_units), jnp.float32),
            ],
        ),
        out_shape=shapes,
        compiler_params=pltpu.CompilerParams(vmem_limit_bytes=vmem_bytes),
        cost_estimate=pl.CostEstimate(
            flops=40 * owned * hidden_count, bytes_accessed=48 * owned * hidden_count,
            transcendentals=4 * owned * hidden_count,
        ),
        name="renew_feed",
    )(place, mine, other, *expand_state, *reduce_state)
    return results[:3], results[3:]


def renew_first_kernel(place_ref, mine, other, *refs):
    inputs_in, output_in, inputs_out, output_out = (refs[3 * i : 3 * i + 3] for i in range(4))
    (pieces,) = refs[12:]
    step = pl.program_id(0)
    groups = mine.shape[0]
    group, core = place_ref[0], place_ref[1]
    for offset in range(groups):
        pieces[core, group ^ offset] = mine[offset]
        pieces[1 - core, group ^ offset] = other[offset]
    rows, half = pieces.shape[2:]
    gradient = jnp.concatenate(
        [pieces[side].reshape(groups * rows, half) for side in range(2)], axis=1
    ).astype(jnp.float32)

    @pl.when(step < 3)
    def _():
        renew_into(inputs_in, inputs_out, gradient, 0.03)

    @pl.when(step == 3)
    def _():
        renew_into(output_in, output_out, gradient, 0.3)


def renew_first(place, mine, other, inputs_state, output_state):
    groups, rows, _ = mine.shape
    owned, features = output_state[0].shape
    half = features // 2
    piece = pl.BlockSpec((groups, rows, half), lambda j, _: (0, 0, j))
    across = pl.BlockSpec((owned, features), lambda j, _: (0, jnp.minimum(j, 2)))
    whole = pl.BlockSpec((owned, features), lambda j, _: (0, 0))
    shapes = [jax.ShapeDtypeStruct(array.shape, jnp.float32) for array in inputs_state]
    shapes += [jax.ShapeDtypeStruct(array.shape, jnp.float32) for array in output_state]
    results = pl.pallas_call(
        renew_first_kernel,
        grid_spec=pltpu.PrefetchScalarGridSpec(
            num_scalar_prefetch=1,
            grid=(4,),
            in_specs=[piece] * 2 + [across] * 3 + [whole] * 3,
            out_specs=[across] * 3 + [whole] * 3,
            scratch_shapes=[pltpu.VMEM((2, groups, rows, half), low)],
        ),
        out_shape=shapes,
        compiler_params=pltpu.CompilerParams(vmem_limit_bytes=vmem_bytes),
        cost_estimate=pl.CostEstimate(
            flops=80 * owned * features, bytes_accessed=96 * owned * features,
            transcendentals=8 * owned * features,
        ),
        name="renew_first",
    )(place, mine, other, *inputs_state, *output_state)
    return results[:3], results[3:]


def chip_routes(dp_count, seq_count):
    straight, crossed = [], []
    for place in range(dp_count):
        group, core = place - place % 2, place % 2
        for quarter in range(seq_count):
            source = place * seq_count + quarter
            holder = (group + quarter // 2) * seq_count
            straight.append((source, holder + 2 * core + quarter % 2))
            crossed.append((source, holder + 2 * core + 1 - quarter % 2))
    return straight, crossed


def on_device(
    dp_count,
    seq_count,
    activations,
    cotangent,
    segment_ids,
    inputs_weight,
    inputs_moment,
    inputs_second,
    output_weight,
    output_moment,
    output_second,
    expand_weight,
    expand_moment,
    expand_second,
    reduce_weight,
    reduce_moment,
    reduce_second,
    vector_params,
    vector_moment,
    vector_second,
):
    axes = ("dp", "seq")
    dp_index = lax.axis_index("dp")
    seq_index = lax.axis_index("seq")
    core = dp_index % 2
    group = dp_index // 2
    groups = dp_count // 2
    four_chips = groups == 4
    odd = seq_index % 2
    features = activations.shape[2]
    quarter = activations.shape[1]
    half = features // 2
    owned = inputs_weight.shape[0]
    owned_units = reduce_weight.shape[0]
    rows_piece = owned // groups
    units_piece = owned_units // dp_count
    vector_rows = vector_params.shape[0]
    straight, crossed = chip_routes(dp_count, seq_count)
    core_pairs = [(place, place ^ 1) for place in range(dp_count)]
    x_pairs = [(place, place ^ 2) for place in range(dp_count)]
    y_pairs = [(place, place ^ 4) for place in range(dp_count)]
    far_pairs = [(place, place ^ 6) for place in range(dp_count)]
    same_core = [list(range(first, dp_count, 2)) for first in range(2)]

    def to_chip_begin(values):
        near = lax.dynamic_index_in_dim(values, odd, 0, keepdims=False)
        far = lax.dynamic_index_in_dim(values, 1 - odd, 0, keepdims=False)
        return lax.ppermute(near, axes, straight), lax.ppermute(far, axes, crossed)

    def to_chip_end(near, far):
        return jnp.concatenate(
            [jnp.where(odd == 0, near, far), jnp.where(odd == 0, far, near)], axis=0
        )

    def to_chip(values):
        return to_chip_end(*to_chip_begin(values))

    def from_chip_begin(values):
        near = lax.dynamic_slice_in_dim(values, odd * quarter, quarter, 0)
        far = lax.dynamic_slice_in_dim(values, (1 - odd) * quarter, quarter, 0)
        near = lax.ppermute(near, axes, [(there, here) for here, there in straight])
        far = lax.ppermute(far, axes, [(there, here) for here, there in crossed])
        return near, far

    def from_chip_end(near, far):
        return jnp.stack([jnp.where(odd == 0, near, far), jnp.where(odd == 0, far, near)])

    def from_chip(values):
        return from_chip_end(*from_chip_begin(values))

    def swap_cores(values):
        return lax.ppermute(values, "dp", core_pairs)

    def via_x(values):
        return lax.ppermute(values, "dp", x_pairs)

    def via_y(values):
        return lax.ppermute(values, "dp", y_pairs)

    def by_core(mine, theirs, axis):
        return jnp.where(
            core == 0,
            jnp.concatenate([mine, theirs], axis=axis),
            jnp.concatenate([theirs, mine], axis=axis),
        )

    def add_low(*terms):
        return sum(term.astype(jnp.float32) for term in terms).astype(low)

    def after(values, *gates):
        return lax.optimization_barrier((values, gates))[0]

    def gather_z_begin(piece):
        parts = [piece]
        for shift in range(1, seq_count):
            ring = [(place, (place + shift) % seq_count) for place in range(seq_count)]
            parts.append(lax.ppermute(piece, "seq", ring))
        return parts

    def gather_z_end(parts):
        return jnp.stack(
            [lax.select_n((seq_index - owner) % seq_count, *parts) for owner in range(seq_count)]
        )

    def gather_z(piece):
        return gather_z_end(gather_z_begin(piece))

    def in_order(own, from_x, from_y, from_far, axis):
        x_set = group % 2 == 1
        y_set = group // 2 == 1
        near_low = jnp.where(x_set, from_x, own)
        near_high = jnp.where(x_set, own, from_x)
        far_low = jnp.where(x_set, from_far, from_y)
        far_high = jnp.where(x_set, from_y, from_far)
        return jnp.stack(
            [
                jnp.where(y_set, far_low, near_low),
                jnp.where(y_set, far_high, near_high),
                jnp.where(y_set, near_low, far_low),
                jnp.where(y_set, near_high, far_high),
            ],
            axis=axis,
        )

    def scatter_begin(own, to_x, to_y, to_far):
        far_first, far_second = via_x(to_far[0]), via_y(to_far[1])
        return *own, to_x[1], to_y[0], far_first, far_second, via_x(to_x[0]), via_y(to_y[1])

    def scatter_begin_joined(own, to_x, to_y, to_far):
        from_x = via_x(jnp.concatenate([to_x[0], to_far[0]], axis=0))
        from_y = via_y(jnp.concatenate([to_y[1], to_far[1]], axis=0))
        near = to_x[0].shape[0]
        return *own, to_x[1], to_y[0], from_x[near:], from_y[near:], from_x[:near], from_y[:near]

    def scatter_middle(state, *gates):
        own_first, own_second, x_second, y_first, far_first, far_second = state[:6]
        far_first, far_second = after((far_first, far_second), *gates)
        y_first = add_low(y_first, far_first)
        x_second = add_low(x_second, far_second)
        return (own_first, own_second, *state[6:], via_y(y_first), via_x(x_second)), (
            y_first,
            x_second,
        )

    def scatter_end(state):
        own_first, own_second, x_first, y_second, y_first, x_second = state
        first = add_low(own_first, x_first, y_first)
        second = add_low(own_second, x_second, y_second)
        return first, second

    def scatter_z_begin(blocks):
        parts = [lax.dynamic_index_in_dim(blocks, seq_index, 0, keepdims=False)]
        for shift in range(1, seq_count):
            target = (seq_index + shift) % seq_count
            sent = lax.dynamic_index_in_dim(blocks, target, 0, keepdims=False)
            ring = [(place, (place + shift) % seq_count) for place in range(seq_count)]
            parts.append(lax.ppermute(sent, "seq", ring))
        return parts

    def scatter_z(blocks):
        return add_low(*scatter_z_begin(blocks))

    def regather_begin(piece):
        return piece, via_x(piece), via_y(piece), lax.ppermute(piece, "dp", far_pairs)

    def regather_end(state):
        mine = in_order(*state, 0)
        return by_core(mine[:, None], swap_cores(mine)[:, None], 1)

    def regather(piece):
        every = lax.all_gather(piece, "dp", axis=0, tiled=False)
        return every.reshape((groups, 2) + piece.shape)

    def corner(weight, column):
        return lax.dynamic_slice(
            weight, (group * rows_piece, column + core * half), (rows_piece, half)
        ).astype(low)

    vector_piece = lax.dynamic_slice_in_dim(vector_params, group * rows_piece, rows_piece, 1)
    first_piece = jnp.concatenate(
        [
            corner(inputs_weight, 0),
            corner(inputs_weight, features),
            corner(inputs_weight, 2 * features),
            corner(output_weight, 0),
            jnp.pad(vector_piece.T.astype(low), ((0, 0), (0, LANES - vector_rows))),
        ],
        axis=1,
    )
    expand_piece = jnp.concatenate(
        [
            lax.dynamic_slice_in_dim(
                expand_weight, owner * owned_units + dp_index * units_piece, units_piece, 1
            ).astype(low)
            for owner in range(seq_count)
        ],
        axis=1,
    )
    reduce_piece = lax.dynamic_slice_in_dim(
        reduce_weight, dp_index * units_piece, units_piece, 0
    ).astype(low)

    def pack(expand, reduce):
        return jnp.concatenate([expand, reduce[..., :half], reduce[..., half:]], axis=-2)

    residual_low = to_chip(activations)
    first_block = gather_z(first_piece)
    if four_chips:
        feed_arrivals = gather_z_begin(after(pack(expand_piece, reduce_piece), first_block))
    rows_here = residual_low.shape[0]
    residual_other = swap_cores(residual_low)
    other_segments = swap_cores(segment_ids)
    segment_pair = jnp.where(seq_index // 2 == core, segment_ids, other_segments)
    segments = lax.dynamic_index_in_dim(segment_pair, odd, 0, keepdims=False)
    seg_row, seg_col = segments[None, :], segments[:, None]

    if four_chips:
        first_x, first_y = via_x(first_block), via_y(first_block)
        middle_owner = seq_count // 2
        first_far = jnp.concatenate(
            [via_y(first_x[:middle_owner]), via_x(first_y[middle_owner:])], axis=0
        )
        first_low = in_order(first_block, first_x, first_y, first_far, 1)
        feed_block = gather_z_end(after(feed_arrivals, first_far))
    else:
        first_low = lax.all_gather(
            first_block,
            "dp",
            axis=1,
            tiled=False,
            axis_index_groups=same_core,
        )
    first_low = first_low.reshape(features, first_low.shape[-1])
    wide = 3 * half
    inputs_low = first_low[:, :wide]
    output_half = first_low[:, wide : wide + half]
    output_all = by_core(output_half, swap_cores(output_half), 1)
    vectors = first_low[:, wide + half : wide + half + vector_rows].T.astype(jnp.float32)

    expand_bias = vectors[8:].reshape(seq_count, dp_count, units_piece)
    block_units = seq_count * owned_units // 8
    if four_chips:
        feed_x, feed_y = via_x(feed_block), via_y(feed_block)
        middle_owner = seq_count // 2
        feed_far = (via_y(feed_x[:middle_owner]), via_x(feed_y[middle_owner:]))
        blocks = [(feed_block,), (feed_x,), (feed_y,), feed_far]
        biases = jnp.concatenate(
            [
                lax.dynamic_index_in_dim(expand_bias, dp_index ^ (2 * offset), 1, keepdims=False)
                for offset in range(4)
            ],
            axis=0,
        )
    else:
        expand_all = lax.all_gather(
            gather_z(expand_piece).reshape(features, -1),
            "dp",
            axis=1,
            axis_index_groups=same_core,
        ).reshape(seq_count, owned, 4, block_units)
        reduce_all = lax.all_gather(
            gather_z(reduce_piece).reshape(-1, features),
            "dp",
            axis=0,
            axis_index_groups=same_core,
        ).reshape(4, seq_count, -1, features)
        picked = lax.dynamic_index_in_dim(
            expand_bias.reshape(seq_count, groups, 2, units_piece), core, 2, keepdims=False
        )
        biases = picked.transpose(1, 0, 2).reshape(4 * seq_count, block_units // seq_count)
        blocks = []
        for index in range(4):
            packed = pack(expand_all[:, :, index], reduce_all[index])
            blocks.append((packed[: seq_count // 2], packed[seq_count // 2 :]))

    def tokens_of(values, which):
        return lax.dynamic_slice_in_dim(values, which * rows_here, rows_here, 0)

    def heads_part(vector):
        return lax.dynamic_slice_in_dim(vector, core * half, half, 0)

    unit_all, _ = normalize(by_core(residual_low, residual_other, 0).astype(jnp.float32))
    normed_one = (unit_all * vectors[0] + vectors[1]).astype(low)
    input_bias = jnp.concatenate(
        [heads_part(vectors[4]), jnp.zeros((half,), jnp.float32), heads_part(vectors[5])]
    )
    projected = (dot_nn(normed_one, inputs_low) + input_bias).astype(low)
    if four_chips:
        projected = after(projected, feed_block)
    mixture_heads, logs_all = attend_forward(seg_row, seg_col, projected)
    if four_chips:
        cotangent = after(cotangent, mixture_heads)
        mixture_heads = after(mixture_heads, feed_x, feed_y)
    top_parts = to_chip_begin(cotangent)
    if four_chips:
        top_parts = after(top_parts, feed_far)
    grad_top = to_chip_end(*top_parts)
    grad_top_other = swap_cores(grad_top)
    mixture_theirs = swap_cores(tokens_of(mixture_heads, 1 - core))
    mixture = by_core(tokens_of(mixture_heads, core), mixture_theirs, 1)

    residual = residual_low.astype(jnp.float32)
    middle = residual + (dot_nn(mixture, output_all) + vectors[6])
    unit_two, inverse_two = normalize(middle)
    normed_two = (unit_two * vectors[2] + vectors[3]).astype(low)
    if four_chips:
        normed_two = after(normed_two, feed_far)
    normed_pair = (normed_two, swap_cores(normed_two))
    top_pair = (grad_top, grad_top_other)
    sums, grads, bias_grads = feed_blocks(normed_pair, top_pair, blocks, biases)
    grad_normed_two = sums[2] + swap_cores(sums[3]).astype(jnp.float32)
    reduced = sums[0] + swap_cores(sums[1]).astype(jnp.float32)
    output_low = (middle + (reduced + vectors[7])).astype(low)

    if four_chips:
        feed_state = scatter_begin(*grads)
        place = jnp.arange(dp_count)[None, :, None]
        bias_sums = sum(
            jnp.where(
                place == (dp_index ^ (2 * offset)),
                bias_grads[seq_count * offset : seq_count * (offset + 1), None, :],
                0.0,
            )
            for offset in range(4)
        )
    else:
        packed = [jnp.concatenate(grad, axis=0) for grad in grads]
        expand_sum = jnp.stack([part[:, :owned] for part in packed], axis=2)
        expand_sum = expand_sum.reshape(features, groups, -1).transpose(1, 0, 2)
        expand_sum = lax.psum_scatter(expand_sum, "dp", axis_index_groups=same_core)
        reduce_sum = [part[:, owned:].reshape(seq_count, 2, -1, half) for part in packed]
        reduce_sum = jnp.stack([part.transpose(0, 2, 1, 3) for part in reduce_sum])
        reduce_sum = reduce_sum.reshape(groups, -1, features)
        reduce_sum = lax.psum_scatter(reduce_sum, "dp", axis_index_groups=same_core)
        bias_sums = bias_grads.reshape(groups, seq_count, units_piece).transpose(1, 0, 2)
        is_core = jnp.arange(2)[None, None, :, None] == core
        bias_sums = jnp.where(is_core, bias_sums[:, :, None, :], 0.0)

    grad_middle = grad_top.astype(jnp.float32) + norm_back(
        grad_normed_two, vectors[2], unit_two, inverse_two
    )
    grad_attended = grad_middle.astype(low)
    grad_output = dot_tn(mixture, grad_attended).astype(low)
    grad_mixture = dot_nt(grad_attended, output_all).astype(low)

    def columns_of(values, which):
        return lax.dynamic_slice_in_dim(values, which * half, half, 1)

    grad_theirs = swap_cores(columns_of(grad_mixture, 1 - core))
    grad_joined = by_core(columns_of(grad_mixture, core), grad_theirs, 0)
    if four_chips:
        feed_state, gates = scatter_middle(feed_state, grad_mixture)
        grad_joined = after(grad_joined, *gates)
    grad_heads = attend_backward(seg_row, seg_col, projected, logs_all, grad_joined)
    output_sum = add_low(
        columns_of(grad_output, core), swap_cores(columns_of(grad_output, 1 - core))
    )
    grad_projected = jnp.concatenate(grad_heads, axis=1)
    if four_chips:
        feed_sum = scatter_end(after(feed_state, grad_projected))
        feed_parts = scatter_z_begin(jnp.concatenate(feed_sum, axis=0))
        grad_projected = after(grad_projected, *feed_sum)
    grad_inputs = dot_tn(normed_one, grad_projected).astype(low)
    grad_normed_all = dot_nt(grad_projected, inputs_low)
    grad_normed_one = tokens_of(grad_normed_all, core) + swap_cores(
        tokens_of(grad_normed_all, 1 - core).astype(low)
    ).astype(jnp.float32)
    unit_one, inverse_one = normalize(residual)
    grad_residual = norm_back(grad_normed_one, vectors[0], unit_one, inverse_one)
    input_grad = (grad_middle + grad_residual).astype(low)

    def heads_sum(values):
        return lax.dynamic_update_slice_in_dim(
            jnp.zeros((features,), jnp.float32), column_sum(values), core * half, 0
        )

    head_rows = jnp.stack(
        [
            column_sum(grad_normed_one * unit_one),
            column_sum(grad_normed_one),
            column_sum(grad_normed_two * unit_two),
            column_sum(grad_normed_two),
            heads_sum(grad_heads[0]),
            heads_sum(grad_heads[2]),
            column_sum(grad_attended),
            column_sum(grad_top),
        ]
    )
    grad_vectors = jnp.concatenate([head_rows, bias_sums.reshape(-1, features)], axis=0)
    vector_columns = jnp.pad(grad_vectors.T.astype(low), ((0, 0), (0, LANES - vector_rows)))
    first_grad = jnp.concatenate([grad_inputs, output_sum, vector_columns], axis=1)
    first_grad = first_grad.reshape(seq_count, groups, rows_piece, -1)
    if four_chips:
        middle_owner = seq_count // 2
        split = []
        for offset in range(4):
            split.append(
                [
                    lax.dynamic_index_in_dim(part, group ^ offset, 1, keepdims=False)
                    for part in (first_grad[:middle_owner], first_grad[middle_owner:])
                ]
            )
        feed_piece = add_low(*after(feed_parts, grad_inputs))
        feed_pieces = regather_begin(feed_piece)
        output_parts = from_chip_begin(after(output_low, feed_piece))
        split, feed_pieces = after((split, feed_pieces))
        first_state = scatter_begin_joined(*split)
        first_state, output_parts = after((first_state, output_parts))
        first_state, gates = scatter_middle(first_state)
        grad_parts = from_chip_begin(after(input_grad, *gates))
        first_parts = scatter_z_begin(jnp.concatenate(scatter_end(first_state), axis=0))
        feed_mine = jnp.stack(feed_pieces)
        feed_other = swap_cores(feed_mine)
        place = jnp.stack([group, core]).astype(jnp.int32)
        new_expand, new_reduce = renew_feed(
            place,
            feed_mine,
            feed_other,
            (expand_weight, expand_moment, expand_second),
            (reduce_weight, reduce_moment, reduce_second),
        )
        first_parts, new_expand, grad_parts = after((first_parts, new_expand, grad_parts))
        first_pieces = regather_begin(add_low(*first_parts))
        first_mine = jnp.stack(first_pieces)
        first_other = swap_cores(first_mine)
        layer_output = from_chip_end(*output_parts)
        new_inputs, new_output = renew_first(
            place,
            first_mine,
            first_other,
            (inputs_weight, inputs_moment, inputs_second),
            (output_weight, output_moment, output_second),
        )
        input_grad = from_chip_end(*grad_parts)
        vector_slice = slice(wide + half, wide + half + vector_rows)
        vector_parts = first_mine[..., vector_slice].astype(jnp.float32) + first_other[
            ..., vector_slice
        ].astype(jnp.float32)
        sum_vectors = in_order(*[vector_parts[offset] for offset in range(4)], 0)
        sum_vectors = sum_vectors.reshape(owned, vector_rows).T
    else:
        first_sum = lax.psum_scatter(
            first_grad, "dp", scatter_dimension=1, axis_index_groups=same_core
        )
        layer_output, input_grad = from_chip(output_low), from_chip(input_grad)
        every_first = regather(scatter_z(first_sum))
        sum_expand = regather(scatter_z(expand_sum.reshape(seq_count, owned, -1)))
        sum_reduce = regather(scatter_z(reduce_sum.reshape(seq_count, units_piece, features)))
    def renew(weight, moment, second, gradient, step_rate, weight_decay):
        return adamw_step(
            weight, moment, second, gradient.astype(jnp.float32), step_rate, weight_decay
        )

    if not four_chips:
        sum_expand = sum_expand.reshape(dp_count, owned, seq_count, units_piece)
        sum_expand = sum_expand.transpose(1, 2, 0, 3).reshape(expand_weight.shape)
        sum_reduce = sum_reduce.reshape(reduce_weight.shape)
        sum_first = every_first.transpose(0, 2, 1, 3)
        sum_inputs = sum_first[..., :wide].reshape(groups, rows_piece, 2, 3, half)
        sum_inputs = sum_inputs.transpose(0, 1, 3, 2, 4).reshape(inputs_weight.shape)
        sum_output = sum_first[..., wide : wide + half].reshape(output_weight.shape)
        sum_vectors = sum_first[..., wide + half : wide + half + vector_rows].astype(jnp.float32)
        sum_vectors = jnp.sum(sum_vectors, axis=2).reshape(owned, vector_rows).T
        new_inputs = renew(inputs_weight, inputs_moment, inputs_second, sum_inputs, 0.03, decay_rate)
        new_output = renew(output_weight, output_moment, output_second, sum_output, 0.3, decay_rate)
        new_expand = renew(expand_weight, expand_moment, expand_second, sum_expand, 0.03, decay_rate)
        new_reduce = renew(reduce_weight, reduce_moment, reduce_second, sum_reduce, 0.02, decay_rate)
    new_vectors = renew(vector_params, vector_moment, vector_second, sum_vectors, 0.5, 0.0)
    return (
        layer_output,
        input_grad,
        *new_inputs,
        *new_output,
        *new_expand,
        *new_reduce,
        *new_vectors,
    )


def solution(mesh):
    tokens = P("dp", "seq", None)
    rows = P("seq", None)
    columns = P(None, "seq")
    in_specs = (tokens, tokens, P("dp", None)) + (rows,) * 12 + (columns,) * 3
    out_specs = (tokens, tokens) + (rows,) * 12 + (columns,) * 3
    return jax.shard_map(
        partial(on_device, mesh.shape["dp"], mesh.shape["seq"]),
        mesh=mesh,
        in_specs=in_specs,
        out_specs=out_specs,
        check_vma=False,
    )
```

```python
from functools import partial

import jax
import jax.numpy as jnp
from jax import lax
from jax.experimental import pallas as pl
from jax.experimental.pallas import tpu as pltpu
from jax.sharding import PartitionSpec as P

HEADS = 12
HD = 64
STEP = 10
PAIR = 2 * HD
LANES = 128

eps_norm = 1e-05
eps_adam = 1e-08
beta_one = 0.9
beta_two = 0.95
decay_rate = 0.1
mask_fill = -1e30
vmem_bytes = 56 * 1024 * 1024

VISIBLE = (
    (0, 256, 0, 256),
    (256, 256, 128, 512),
    (512, 256, 128, 768),
    (768, 128, 128, 896),
    (896, 128, 768, 1024),
)
TILE_STARTS = []
tile_total = 0
for _first, _rows, _low, _high in VISIBLE:
    TILE_STARTS.append(tile_total)
    tile_total += _high - _low

low = jnp.bfloat16


def dot_nn(left_side, right_side):
    return lax.dot_general(
        left_side, right_side, (((1,), (0,)), ((), ())), preferred_element_type=jnp.float32
    )


def dot_tn(left_side, right_side):
    return lax.dot_general(
        left_side, right_side, (((0,), (0,)), ((), ())), preferred_element_type=jnp.float32
    )


def dot_nt(left_side, right_side):
    return lax.dot_general(
        left_side, right_side, (((1,), (1,)), ((), ())), preferred_element_type=jnp.float32
    )


def normalize(values):
    center = jnp.mean(values, axis=-1, keepdims=True)
    offsets = values - center
    spread = jnp.mean(offsets * offsets, axis=-1, keepdims=True)
    inverse = lax.rsqrt(spread + eps_norm)
    return offsets * inverse, inverse


def norm_back(grad_normed, gain, unit, inverse):
    scaled = grad_normed * gain
    mean_scaled = jnp.mean(scaled, axis=-1, keepdims=True)
    mean_cross = jnp.mean(scaled * unit, axis=-1, keepdims=True)
    return inverse * (scaled - mean_scaled - unit * mean_cross)


def adamw_step(weight, moment, second, gradient, step_rate, weight_decay):
    moment_new = beta_one * moment + (1.0 - beta_one) * gradient
    second_new = beta_two * second + (1.0 - beta_two) * gradient * gradient
    fix_one = 1.0 - beta_one**STEP
    fix_two = 1.0 - beta_two**STEP
    update = moment_new / fix_one / (jnp.sqrt(second_new / fix_two) + eps_adam)
    return (weight - step_rate * (update + weight_decay * weight), moment_new, second_new)


def column_sum(values):
    return jnp.sum(values.astype(jnp.float32), axis=0)


def fill_bias(seg_row, seg_col, bias):
    for (first, rows, key_low, key_high), start in zip(VISIBLE, TILE_STARTS):
        keys = key_high - key_low
        key_places = key_low + lax.broadcasted_iota(jnp.int32, (keys, rows), 0)
        query_places = first + lax.broadcasted_iota(jnp.int32, (keys, rows), 1)
        same = seg_col[key_low:key_high, :] == seg_row[:, first : first + rows]
        allowed = same & (key_places <= query_places)
        bias[start : start + keys, 0:rows] = jnp.where(allowed, 0.0, mask_fill)


def lane_masks(shape):
    lane = lax.broadcasted_iota(jnp.int32, shape, 1)
    return (lane < HD, lane >= HD)


def masked_to(values, mask):
    return jnp.where(mask, values, jnp.zeros_like(values))


def attend_forward_kernel(seg_row, seg_col, q_ref, k_ref, v_ref, out_ref, log_ref, bias):
    @pl.when(pl.program_id(0) == 0)
    def _():
        fill_bias(seg_row, seg_col, bias)

    masks = lane_masks((k_ref.shape[0], PAIR))
    keys_masked = [masked_to(k_ref[...], mask) for mask in masks]
    for (first, rows, key_low, key_high), start in zip(VISIBLE, TILE_STARTS):
        queries = q_ref[first : first + rows, :] * jnp.asarray(HD**-0.5, low)
        values = v_ref[key_low:key_high, :]
        mixed = []
        for head in range(2):
            scores = dot_nt(keys_masked[head][key_low:key_high], queries)
            scores = scores + bias[start : start + key_high - key_low, 0:rows]
            highest = jnp.max(scores, axis=0, keepdims=True)
            exponent = jnp.exp(scores - highest)
            totals = jnp.sum(exponent, axis=0, keepdims=True)
            soft = (exponent * (1.0 / totals)).astype(low)
            mixed.append(dot_tn(soft, values))
            log_ref[0, head : head + 1, first : first + rows] = highest + jnp.log(totals)
        half = lane_masks((rows, PAIR))[0]
        out_ref[first : first + rows, :] = jnp.where(half, mixed[0], mixed[1]).astype(low)


def attend_backward_kernel(
    seg_row, seg_col, q_ref, k_ref, v_ref, log_ref, do_ref, dq_ref, dk_ref, dv_ref, bias, dk_acc, dv_acc
):
    @pl.when(pl.program_id(0) == 0)
    def _():
        fill_bias(seg_row, seg_col, bias)

    masks = lane_masks((k_ref.shape[0], PAIR))
    keys_masked = [masked_to(k_ref[...], mask) for mask in masks]
    values_masked = [masked_to(v_ref[...], mask) for mask in masks]
    dk_acc[...] = jnp.zeros_like(dk_acc)
    dv_acc[...] = jnp.zeros_like(dv_acc)
    for (first, rows, key_low, key_high), start in zip(VISIBLE, TILE_STARTS):
        queries = q_ref[first : first + rows, :] * jnp.asarray(HD**-0.5, low)
        grads = do_ref[first : first + rows, :]
        grad_query = jnp.zeros((rows, PAIR), jnp.float32)
        row_masks = lane_masks((rows, PAIR))
        for head in range(2):
            keys = keys_masked[head][key_low:key_high]
            scores = dot_nt(keys, queries)
            scores = scores + bias[start : start + key_high - key_low, 0:rows]
            soft = jnp.exp(scores - log_ref[0, head : head + 1, first : first + rows])
            grad_soft = dot_nt(values_masked[head][key_low:key_high], grads)
            inner = jnp.sum(soft * grad_soft, axis=0, keepdims=True)
            grad_scores = (soft * (grad_soft - inner)).astype(low)
            dv_acc[key_low:key_high, :] += dot_nn(
                soft.astype(low), masked_to(grads, row_masks[head])
            )
            dk_acc[key_low:key_high, :] += dot_nn(
                grad_scores, masked_to(queries, row_masks[head])
            )
            grad_query = grad_query + dot_tn(grad_scores, keys)
        dq_ref[first : first + rows, :] = (grad_query * HD**-0.5).astype(low)
    dk_ref[...] = dk_acc[...].astype(low)
    dv_ref[...] = dv_acc[...].astype(low)


def attend_specs(length, pairs):
    whole = lambda shape: pl.BlockSpec(shape, lambda j: (0,) * len(shape))
    columns = lambda offset: pl.BlockSpec((length, PAIR), lambda j, offset=offset: (0, offset + j))
    logs = pl.BlockSpec((1, 8, length), lambda j: (j, 0, 0))
    return whole, columns, logs


def attend_forward(seg_row, seg_col, projected):
    length = projected.shape[0]
    pairs = projected.shape[1] // (3 * PAIR)
    whole, columns, logs = attend_specs(length, pairs)
    return pl.pallas_call(
        attend_forward_kernel,
        grid=(pairs,),
        in_specs=[
            whole((1, length)),
            whole((length, 1)),
            columns(0),
            columns(pairs),
            columns(2 * pairs),
        ],
        out_specs=[columns(0), logs],
        out_shape=[
            jax.ShapeDtypeStruct((length, pairs * PAIR), low),
            jax.ShapeDtypeStruct((pairs, 8, length), jnp.float32),
        ],
        scratch_shapes=[pltpu.VMEM((tile_total, 256), jnp.float32)],
        compiler_params=pltpu.CompilerParams(vmem_limit_bytes=vmem_bytes),
        cost_estimate=pl.CostEstimate(
            flops=4 * length * length * pairs * PAIR, bytes_accessed=8 * length * pairs * PAIR,
            transcendentals=length * length * pairs,
        ),
        name="attend_forward",
    )(seg_row, seg_col, projected, projected, projected)


def attend_backward(seg_row, seg_col, projected, logs_all, grad_mixture):
    length = projected.shape[0]
    pairs = projected.shape[1] // (3 * PAIR)
    whole, columns, logs = attend_specs(length, pairs)
    return pl.pallas_call(
        attend_backward_kernel,
        grid=(pairs,),
        in_specs=[
            whole((1, length)),
            whole((length, 1)),
            columns(0),
            columns(pairs),
            columns(2 * pairs),
            logs,
            columns(0),
        ],
        out_specs=[columns(0)] * 3,
        out_shape=[jax.ShapeDtypeStruct((length, pairs * PAIR), low)] * 3,
        scratch_shapes=[
            pltpu.VMEM((tile_total, 256), jnp.float32),
            pltpu.VMEM((length, PAIR), jnp.float32),
            pltpu.VMEM((length, PAIR), jnp.float32),
        ],
        compiler_params=pltpu.CompilerParams(vmem_limit_bytes=vmem_bytes),
        cost_estimate=pl.CostEstimate(
            flops=10 * length * length * pairs * PAIR, bytes_accessed=14 * length * pairs * PAIR,
            transcendentals=length * length * pairs,
        ),
        name="attend_backward",
    )(seg_row, seg_col, projected, projected, projected, logs_all, grad_mixture)


def feed_kernel(part_counts, *refs):
    refs = list(refs)
    take = lambda count: [refs.pop(0) for _ in range(count)]
    normed = [ref[...] for ref in take(2)]
    tops = [ref[...] for ref in take(2)]
    blocks = [take(count) for count in part_counts]
    bias_ref = take(1)[0]
    reduced, reduced_out, back, back_out = take(4)
    outs = [take(2) for _ in part_counts]
    dbu_ref = take(1)[0]
    turned, weights, grads, reduced_sum, back_sum, in_sems, out_sems = refs
    owners, depth, units = weights.shape[2:]
    side_rows = units // (2 * owners)
    split = depth - 2 * side_rows
    arrivals = [
        [
            pltpu.make_async_copy(
                parts[part] if len(parts) == 2 else parts[0].at[pl.ds(part * owners, owners)],
                weights.at[index, part],
                in_sems.at[index, part],
            )
            for part in range(2)
        ]
        for index, parts in enumerate(blocks)
    ]
    for copies in arrivals:
        for copy in copies:
            copy.start()
    rows = normed[0].shape[0]
    reduced_sums = (reduced, reduced_sum)
    back_sums = (back, back_sum)
    for side in range(2):
        turned[:, side * rows : (side + 1) * rows] = normed[side].T
    departures = []
    for index, grad_refs in enumerate(outs):
        for copy in arrivals[index]:
            copy.wait()
        places = [(part, owner) for part in range(2) for owner in range(owners)]
        expand = jnp.concatenate([weights[index, part, owner, :split] for part, owner in places], axis=0)
        reduce = jnp.concatenate(
            [
                jnp.concatenate(
                    [
                        weights[index, part, owner, split : split + side_rows],
                        weights[index, part, owner, split + side_rows :],
                    ],
                    axis=1,
                )
                for part, owner in places
            ],
            axis=0,
        )
        bias_rows = range(2 * owners * index, 2 * owners * (index + 1))
        bias = jnp.concatenate([bias_ref[row : row + 1, :] for row in bias_rows], axis=1)
        hiddens, slopes = [], []
        for side in range(2):
            expanded = dot_nn(normed[side], expand) + bias
            phi = 0.5 + 0.5 * lax.erf(expanded * (0.5**0.5))
            density = jnp.exp(-0.5 * expanded * expanded) * 0.3989422804014327
            hiddens.append((expanded * phi).astype(low))
            grad_hidden = dot_nt(tops[side], reduce)
            slopes.append((grad_hidden * (phi + expanded * density)).astype(low))
        for side in range(2):
            down = dot_nn(hiddens[side], reduce)
            up = dot_nt(slopes[side], expand)
            if index:
                reduced_sums[side][...] += down
                back_sums[side][...] += up
            else:
                reduced_sums[side][...] = down
                back_sums[side][...] = up
        grad_both = jnp.concatenate(slopes, axis=0)
        grad_reduce = sum(dot_tn(hiddens[side], tops[side]) for side in range(2)).astype(low)
        for place, (part, owner) in enumerate(places):
            grads[index, part, owner, :split] = dot_nn(
                turned[place * split : (place + 1) * split, :], grad_both
            ).astype(low)
            rows_down = grad_reduce[place * side_rows : (place + 1) * side_rows]
            grads[index, part, owner, split : split + side_rows] = rows_down[:, :units]
            grads[index, part, owner, split + side_rows :] = rows_down[:, units:]
        bias_grad = jnp.sum(grad_both.astype(jnp.float32), axis=0, keepdims=True)
        for place, row in enumerate(bias_rows):
            dbu_ref[row : row + 1, :] = bias_grad[:, place * side_rows : (place + 1) * side_rows]
        for part in range(2):
            departures.append(
                pltpu.make_async_copy(
                    grads.at[index, part], grad_refs[part], out_sems.at[index, part]
                )
            )
            departures[-1].start()
    reduced_out[...] = reduced_sum[...].astype(low)
    back_out[...] = back_sum[...].astype(low)
    for copy in departures:
        copy.wait()


def feed_blocks(normed, tops, blocks, biases):
    rows, features = normed[0].shape
    count = len(blocks)
    units = biases.shape[0] * biases.shape[1] // count
    operands = [*normed, *tops]
    in_vmem = pl.BlockSpec(memory_space=pltpu.VMEM)
    anywhere = pl.BlockSpec(memory_space=pl.ANY)
    sum_shape = jax.ShapeDtypeStruct((rows, features), jnp.float32)
    sent_shape = jax.ShapeDtypeStruct((rows, features), low)
    shapes = [sum_shape, sent_shape, sum_shape, sent_shape]
    part_shape = blocks[-1][0].shape
    for parts in blocks:
        operands += parts
        shapes += [jax.ShapeDtypeStruct(part_shape, low)] * 2
    operands += [biases]
    shapes += [jax.ShapeDtypeStruct(biases.shape, jnp.float32)]
    part_counts = [len(parts) for parts in blocks]
    results = pl.pallas_call(
        partial(feed_kernel, part_counts),
        in_specs=[in_vmem] * 4 + [anywhere] * sum(part_counts) + [in_vmem],
        out_specs=[in_vmem] * 4 + [anywhere] * (2 * count) + [in_vmem],
        out_shape=shapes,
        scratch_shapes=[
            pltpu.VMEM((features, 2 * rows), low),
            pltpu.VMEM((count, 2) + part_shape, low),
            pltpu.VMEM((count, 2) + part_shape, low),
            pltpu.VMEM((rows, features), jnp.float32),
            pltpu.VMEM((rows, features), jnp.float32),
            pltpu.SemaphoreType.DMA((count, 2)),
            pltpu.SemaphoreType.DMA((count, 2)),
        ],
        compiler_params=pltpu.CompilerParams(vmem_limit_bytes=vmem_bytes),
        cost_estimate=pl.CostEstimate(
            flops=24 * rows * features * units * count,
            bytes_accessed=8 * features * units * count,
            transcendentals=4 * rows * units * count,
        ),
        name="feed_blocks",
    )(*operands)
    grads = [results[4 + 2 * index : 6 + 2 * index] for index in range(count)]
    return results[:4], grads, results[-1]


def renew_into(sources, targets, gradient, step_rate, place=Ellipsis):
    weight, moment, second = (ref[place] for ref in sources)
    results = adamw_step(weight, moment, second, gradient, step_rate, decay_rate)
    for ref, result in zip(targets, results):
        ref[place] = result


def renew_feed_kernel(place_ref, mine, other, *refs):
    expand_in, reduce_in, expand_out, reduce_out = (refs[3 * i : 3 * i + 3] for i in range(4))
    pieces, expand_grad = refs[12:]
    step = pl.program_id(0)
    groups, depth, units = mine.shape
    owners, owned, features = expand_grad.shape
    units_piece = units // owners

    @pl.when(step == 0)
    def _():
        group, core = place_ref[0], place_ref[1]
        for offset in range(groups):
            slot = 2 * (group ^ offset)
            pieces[slot + core] = mine[offset]
            pieces[slot + 1 - core] = other[offset]
        for owner in range(owners):
            expand_grad[owner] = jnp.concatenate(
                [
                    pieces[slot, :owned, owner * units_piece : (owner + 1) * units_piece].astype(
                        jnp.float32
                    )
                    for slot in range(2 * groups)
                ],
                axis=1,
            )

    renew_into(expand_in, expand_out, expand_grad[step], 0.03)
    slots = 2 * groups // owners
    for index in range(slots):
        slot = slots * step + index
        gradient = jnp.concatenate(
            [pieces[slot, owned : owned + units_piece], pieces[slot, owned + units_piece :]],
            axis=1,
        )
        rows = slice(index * units_piece, (index + 1) * units_piece)
        renew_into(reduce_in, reduce_out, gradient.astype(jnp.float32), 0.02, (rows, slice(None)))


def renew_feed(place, mine, other, expand_state, reduce_state):
    groups, depth, units = mine.shape
    owned, hidden_count = expand_state[0].shape
    owned_units, features = reduce_state[0].shape
    owners = hidden_count // owned_units
    whole = pl.BlockSpec(mine.shape, lambda j, _: (0, 0, 0))
    across = pl.BlockSpec((owned, owned_units), lambda j, _: (0, j))
    down = pl.BlockSpec((owned_units // owners, features), lambda j, _: (j, 0))
    shapes = [jax.ShapeDtypeStruct(array.shape, jnp.float32) for array in expand_state]
    shapes += [jax.ShapeDtypeStruct(array.shape, jnp.float32) for array in reduce_state]
    results = pl.pallas_call(
        renew_feed_kernel,
        grid_spec=pltpu.PrefetchScalarGridSpec(
            num_scalar_prefetch=1,
            grid=(owners,),
            in_specs=[whole] * 2 + [across] * 3 + [down] * 3,
            out_specs=[across] * 3 + [down] * 3,
            scratch_shapes=[
                pltpu.VMEM((2 * groups, depth, units), low),
                pltpu.VMEM((owners, owned, owned_units), jnp.float32),
            ],
        ),
        out_shape=shapes,
        compiler_params=pltpu.CompilerParams(vmem_limit_bytes=vmem_bytes),
        cost_estimate=pl.CostEstimate(
            flops=40 * owned * hidden_count, bytes_accessed=48 * owned * hidden_count,
            transcendentals=4 * owned * hidden_count,
        ),
        name="renew_feed",
    )(place, mine, other, *expand_state, *reduce_state)
    return results[:3], results[3:]


def renew_first_kernel(place_ref, mine, other, *refs):
    inputs_in, output_in, inputs_out, output_out = (refs[3 * i : 3 * i + 3] for i in range(4))
    (pieces,) = refs[12:]
    step = pl.program_id(0)
    groups = mine.shape[0]
    group, core = place_ref[0], place_ref[1]
    for offset in range(groups):
        pieces[core, group ^ offset] = mine[offset]
        pieces[1 - core, group ^ offset] = other[offset]
    rows, half = pieces.shape[2:]
    gradient = jnp.concatenate(
        [pieces[side].reshape(groups * rows, half) for side in range(2)], axis=1
    ).astype(jnp.float32)

    @pl.when(step < 3)
    def _():
        renew_into(inputs_in, inputs_out, gradient, 0.03)

    @pl.when(step == 3)
    def _():
        renew_into(output_in, output_out, gradient, 0.3)


def renew_first(place, mine, other, inputs_state, output_state):
    groups, rows, _ = mine.shape
    owned, features = output_state[0].shape
    half = features // 2
    piece = pl.BlockSpec((groups, rows, half), lambda j, _: (0, 0, j))
    across = pl.BlockSpec((owned, features), lambda j, _: (0, jnp.minimum(j, 2)))
    whole = pl.BlockSpec((owned, features), lambda j, _: (0, 0))
    shapes = [jax.ShapeDtypeStruct(array.shape, jnp.float32) for array in inputs_state]
    shapes += [jax.ShapeDtypeStruct(array.shape, jnp.float32) for array in output_state]
    results = pl.pallas_call(
        renew_first_kernel,
        grid_spec=pltpu.PrefetchScalarGridSpec(
            num_scalar_prefetch=1,
            grid=(4,),
            in_specs=[piece] * 2 + [across] * 3 + [whole] * 3,
            out_specs=[across] * 3 + [whole] * 3,
            scratch_shapes=[pltpu.VMEM((2, groups, rows, half), low)],
        ),
        out_shape=shapes,
        compiler_params=pltpu.CompilerParams(vmem_limit_bytes=vmem_bytes),
        cost_estimate=pl.CostEstimate(
            flops=80 * owned * features, bytes_accessed=96 * owned * features,
            transcendentals=8 * owned * features,
        ),
        name="renew_first",
    )(place, mine, other, *inputs_state, *output_state)
    return results[:3], results[3:]


def chip_routes(dp_count, seq_count):
    straight, crossed = [], []
    for place in range(dp_count):
        group, core = place - place % 2, place % 2
        for quarter in range(seq_count):
            source = place * seq_count + quarter
            holder = (group + quarter // 2) * seq_count
            straight.append((source, holder + 2 * core + quarter % 2))
            crossed.append((source, holder + 2 * core + 1 - quarter % 2))
    return straight, crossed


def on_device(
    dp_count,
    seq_count,
    activations,
    cotangent,
    segment_ids,
    inputs_weight,
    inputs_moment,
    inputs_second,
    output_weight,
    output_moment,
    output_second,
    expand_weight,
    expand_moment,
    expand_second,
    reduce_weight,
    reduce_moment,
    reduce_second,
    vector_params,
    vector_moment,
    vector_second,
):
    axes = ("dp", "seq")
    dp_index = lax.axis_index("dp")
    seq_index = lax.axis_index("seq")
    core = dp_index % 2
    group = dp_index // 2
    groups = dp_count // 2
    four_chips = groups == 4
    odd = seq_index % 2
    features = activations.shape[2]
    quarter = activations.shape[1]
    half = features // 2
    owned = inputs_weight.shape[0]
    owned_units = reduce_weight.shape[0]
    rows_piece = owned // groups
    units_piece = owned_units // dp_count
    vector_rows = vector_params.shape[0]
    straight, crossed = chip_routes(dp_count, seq_count)
    core_pairs = [(place, place ^ 1) for place in range(dp_count)]
    x_pairs = [(place, place ^ 2) for place in range(dp_count)]
    y_pairs = [(place, place ^ 4) for place in range(dp_count)]
    far_pairs = [(place, place ^ 6) for place in range(dp_count)]
    same_core = [list(range(first, dp_count, 2)) for first in range(2)]

    def to_chip_begin(values):
        near = lax.dynamic_index_in_dim(values, odd, 0, keepdims=False)
        far = lax.dynamic_index_in_dim(values, 1 - odd, 0, keepdims=False)
        return lax.ppermute(near, axes, straight), lax.ppermute(far, axes, crossed)

    def to_chip_end(near, far):
        return jnp.concatenate(
            [jnp.where(odd == 0, near, far), jnp.where(odd == 0, far, near)], axis=0
        )

    def to_chip(values):
        return to_chip_end(*to_chip_begin(values))

    def from_chip_begin(values):
        near = lax.dynamic_slice_in_dim(values, odd * quarter, quarter, 0)
        far = lax.dynamic_slice_in_dim(values, (1 - odd) * quarter, quarter, 0)
        near = lax.ppermute(near, axes, [(there, here) for here, there in straight])
        far = lax.ppermute(far, axes, [(there, here) for here, there in crossed])
        return near, far

    def from_chip_end(near, far):
        return jnp.stack([jnp.where(odd == 0, near, far), jnp.where(odd == 0, far, near)])

    def from_chip(values):
        return from_chip_end(*from_chip_begin(values))

    def swap_cores(values):
        return lax.ppermute(values, "dp", core_pairs)

    def via_x(values):
        return lax.ppermute(values, "dp", x_pairs)

    def via_y(values):
        return lax.ppermute(values, "dp", y_pairs)

    def by_core(mine, theirs, axis):
        return jnp.where(
            core == 0,
            jnp.concatenate([mine, theirs], axis=axis),
            jnp.concatenate([theirs, mine], axis=axis),
        )

    def add_low(*terms):
        return sum(term.astype(jnp.float32) for term in terms).astype(low)

    def after(values, *gates):
        return lax.optimization_barrier((values, gates))[0]

    def gather_z_begin(piece):
        parts = [piece]
        for shift in range(1, seq_count):
            ring = [(place, (place + shift) % seq_count) for place in range(seq_count)]
            parts.append(lax.ppermute(piece, "seq", ring))
        return parts

    def gather_z_end(parts):
        return jnp.stack(
            [lax.select_n((seq_index - owner) % seq_count, *parts) for owner in range(seq_count)]
        )

    def gather_z(piece):
        return gather_z_end(gather_z_begin(piece))

    def in_order(own, from_x, from_y, from_far, axis):
        x_set = group % 2 == 1
        y_set = group // 2 == 1
        near_low = jnp.where(x_set, from_x, own)
        near_high = jnp.where(x_set, own, from_x)
        far_low = jnp.where(x_set, from_far, from_y)
        far_high = jnp.where(x_set, from_y, from_far)
        return jnp.stack(
            [
                jnp.where(y_set, far_low, near_low),
                jnp.where(y_set, far_high, near_high),
                jnp.where(y_set, near_low, far_low),
                jnp.where(y_set, near_high, far_high),
            ],
            axis=axis,
        )

    def scatter_begin(own, to_x, to_y, to_far):
        far_first, far_second = via_x(to_far[0]), via_y(to_far[1])
        return *own, to_x[1], to_y[0], far_first, far_second, via_x(to_x[0]), via_y(to_y[1])

    def scatter_begin_joined(own, to_x, to_y, to_far):
        from_x = via_x(jnp.concatenate([to_x[0], to_far[0]], axis=0))
        from_y = via_y(jnp.concatenate([to_y[1], to_far[1]], axis=0))
        near = to_x[0].shape[0]
        return *own, to_x[1], to_y[0], from_x[near:], from_y[near:], from_x[:near], from_y[:near]

    def scatter_middle(state, *gates):
        own_first, own_second, x_second, y_first, far_first, far_second = state[:6]
        far_first, far_second = after((far_first, far_second), *gates)
        y_first = add_low(y_first, far_first)
        x_second = add_low(x_second, far_second)
        return (own_first, own_second, *state[6:], via_y(y_first), via_x(x_second)), (
            y_first,
            x_second,
        )

    def scatter_end(state):
        own_first, own_second, x_first, y_second, y_first, x_second = state
        first = add_low(own_first, x_first, y_first)
        second = add_low(own_second, x_second, y_second)
        return first, second

    def scatter_z_begin(blocks):
        parts = [lax.dynamic_index_in_dim(blocks, seq_index, 0, keepdims=False)]
        for shift in range(1, seq_count):
            target = (seq_index + shift) % seq_count
            sent = lax.dynamic_index_in_dim(blocks, target, 0, keepdims=False)
            ring = [(place, (place + shift) % seq_count) for place in range(seq_count)]
            parts.append(lax.ppermute(sent, "seq", ring))
        return parts

    def scatter_z(blocks):
        return add_low(*scatter_z_begin(blocks))

    def regather_begin(piece):
        return piece, via_x(piece), via_y(piece), lax.ppermute(piece, "dp", far_pairs)

    def regather_end(state):
        mine = in_order(*state, 0)
        return by_core(mine[:, None], swap_cores(mine)[:, None], 1)

    def regather(piece):
        every = lax.all_gather(piece, "dp", axis=0, tiled=False)
        return every.reshape((groups, 2) + piece.shape)

    def corner(weight, column):
        return lax.dynamic_slice(
            weight, (group * rows_piece, column + core * half), (rows_piece, half)
        ).astype(low)

    vector_piece = lax.dynamic_slice_in_dim(vector_params, group * rows_piece, rows_piece, 1)
    first_piece = jnp.concatenate(
        [
            corner(inputs_weight, 0),
            corner(inputs_weight, features),
            corner(inputs_weight, 2 * features),
            corner(output_weight, 0),
            jnp.pad(vector_piece.T.astype(low), ((0, 0), (0, LANES - vector_rows))),
        ],
        axis=1,
    )
    expand_piece = jnp.concatenate(
        [
            lax.dynamic_slice_in_dim(
                expand_weight, owner * owned_units + dp_index * units_piece, units_piece, 1
            ).astype(low)
            for owner in range(seq_count)
        ],
        axis=1,
    )
    reduce_piece = lax.dynamic_slice_in_dim(
        reduce_weight, dp_index * units_piece, units_piece, 0
    ).astype(low)

    def pack(expand, reduce):
        return jnp.concatenate([expand, reduce[..., :half], reduce[..., half:]], axis=-2)

    residual_low = to_chip(activations)
    first_block = gather_z(first_piece)
    if four_chips:
        feed_arrivals = gather_z_begin(after(pack(expand_piece, reduce_piece), first_block))
    rows_here = residual_low.shape[0]
    residual_other = swap_cores(residual_low)
    other_segments = swap_cores(segment_ids)
    segment_pair = jnp.where(seq_index // 2 == core, segment_ids, other_segments)
    segments = lax.dynamic_index_in_dim(segment_pair, odd, 0, keepdims=False)
    seg_row, seg_col = segments[None, :], segments[:, None]

    if four_chips:
        first_x, first_y = via_x(first_block), via_y(first_block)
        middle_owner = seq_count // 2
        first_far = jnp.concatenate(
            [via_y(first_x[:middle_owner]), via_x(first_y[middle_owner:])], axis=0
        )
        first_low = in_order(first_block, first_x, first_y, first_far, 1)
        feed_block = gather_z_end(after(feed_arrivals, first_far))
    else:
        first_low = lax.all_gather(
            first_block,
            "dp",
            axis=1,
            tiled=False,
            axis_index_groups=same_core,
        )
    first_low = first_low.reshape(features, first_low.shape[-1])
    wide = 3 * half
    inputs_low = first_low[:, :wide]
    output_half = first_low[:, wide : wide + half]
    output_all = by_core(output_half, swap_cores(output_half), 1)
    vectors = first_low[:, wide + half : wide + half + vector_rows].T.astype(jnp.float32)

    expand_bias = vectors[8:].reshape(seq_count, dp_count, units_piece)
    block_units = seq_count * owned_units // 8
    if four_chips:
        feed_x, feed_y = via_x(feed_block), via_y(feed_block)
        middle_owner = seq_count // 2
        feed_far = (via_y(feed_x[:middle_owner]), via_x(feed_y[middle_owner:]))
        blocks = [(feed_block,), (feed_x,), (feed_y,), feed_far]
        biases = jnp.concatenate(
            [
                lax.dynamic_index_in_dim(expand_bias, dp_index ^ (2 * offset), 1, keepdims=False)
                for offset in range(4)
            ],
            axis=0,
        )
    else:
        expand_all = lax.all_gather(
            gather_z(expand_piece).reshape(features, -1),
            "dp",
            axis=1,
            axis_index_groups=same_core,
        ).reshape(seq_count, owned, 4, block_units)
        reduce_all = lax.all_gather(
            gather_z(reduce_piece).reshape(-1, features),
            "dp",
            axis=0,
            axis_index_groups=same_core,
        ).reshape(4, seq_count, -1, features)
        picked = lax.dynamic_index_in_dim(
            expand_bias.reshape(seq_count, groups, 2, units_piece), core, 2, keepdims=False
        )
        biases = picked.transpose(1, 0, 2).reshape(4 * seq_count, block_units // seq_count)
        blocks = []
        for index in range(4):
            packed = pack(expand_all[:, :, index], reduce_all[index])
            blocks.append((packed[: seq_count // 2], packed[seq_count // 2 :]))

    def tokens_of(values, which):
        return lax.dynamic_slice_in_dim(values, which * rows_here, rows_here, 0)

    def heads_part(vector):
        return lax.dynamic_slice_in_dim(vector, core * half, half, 0)

    unit_all, _ = normalize(by_core(residual_low, residual_other, 0).astype(jnp.float32))
    normed_one = (unit_all * vectors[0] + vectors[1]).astype(low)
    input_bias = jnp.concatenate(
        [heads_part(vectors[4]), jnp.zeros((half,), jnp.float32), heads_part(vectors[5])]
    )
    projected = (dot_nn(normed_one, inputs_low) + input_bias).astype(low)
    if four_chips:
        projected = after(projected, feed_block)
    mixture_heads, logs_all = attend_forward(seg_row, seg_col, projected)
    if four_chips:
        cotangent = after(cotangent, mixture_heads)
        mixture_heads = after(mixture_heads, feed_x, feed_y)
    top_parts = to_chip_begin(cotangent)
    if four_chips:
        top_parts = after(top_parts, feed_far)
    grad_top = to_chip_end(*top_parts)
    grad_top_other = swap_cores(grad_top)
    mixture_theirs = swap_cores(tokens_of(mixture_heads, 1 - core))
    mixture = by_core(tokens_of(mixture_heads, core), mixture_theirs, 1)

    residual = residual_low.astype(jnp.float32)
    middle = residual + (dot_nn(mixture, output_all) + vectors[6])
    unit_two, inverse_two = normalize(middle)
    normed_two = (unit_two * vectors[2] + vectors[3]).astype(low)
    if four_chips:
        normed_two = after(normed_two, feed_far)
    normed_pair = (normed_two, swap_cores(normed_two))
    top_pair = (grad_top, grad_top_other)
    sums, grads, bias_grads = feed_blocks(normed_pair, top_pair, blocks, biases)
    grad_normed_two = sums[2] + swap_cores(sums[3]).astype(jnp.float32)
    reduced = sums[0] + swap_cores(sums[1]).astype(jnp.float32)
    output_low = (middle + (reduced + vectors[7])).astype(low)

    if four_chips:
        feed_state = scatter_begin(*grads)
        place = jnp.arange(dp_count)[None, :, None]
        bias_sums = sum(
            jnp.where(
                place == (dp_index ^ (2 * offset)),
                bias_grads[seq_count * offset : seq_count * (offset + 1), None, :],
                0.0,
            )
            for offset in range(4)
        )
    else:
        packed = [jnp.concatenate(grad, axis=0) for grad in grads]
        expand_sum = jnp.stack([part[:, :owned] for part in packed], axis=2)
        expand_sum = expand_sum.reshape(features, groups, -1).transpose(1, 0, 2)
        expand_sum = lax.psum_scatter(expand_sum, "dp", axis_index_groups=same_core)
        reduce_sum = [part[:, owned:].reshape(seq_count, 2, -1, half) for part in packed]
        reduce_sum = jnp.stack([part.transpose(0, 2, 1, 3) for part in reduce_sum])
        reduce_sum = reduce_sum.reshape(groups, -1, features)
        reduce_sum = lax.psum_scatter(reduce_sum, "dp", axis_index_groups=same_core)
        bias_sums = bias_grads.reshape(groups, seq_count, units_piece).transpose(1, 0, 2)
        is_core = jnp.arange(2)[None, None, :, None] == core
        bias_sums = jnp.where(is_core, bias_sums[:, :, None, :], 0.0)

    grad_middle = grad_top.astype(jnp.float32) + norm_back(
        grad_normed_two, vectors[2], unit_two, inverse_two
    )
    grad_attended = grad_middle.astype(low)
    grad_output = dot_tn(mixture, grad_attended).astype(low)
    grad_mixture = dot_nt(grad_attended, output_all).astype(low)

    def columns_of(values, which):
        return lax.dynamic_slice_in_dim(values, which * half, half, 1)

    grad_theirs = swap_cores(columns_of(grad_mixture, 1 - core))
    grad_joined = by_core(columns_of(grad_mixture, core), grad_theirs, 0)
    if four_chips:
        feed_state, gates = scatter_middle(feed_state, grad_mixture)
        grad_joined = after(grad_joined, *gates)
    grad_heads = attend_backward(seg_row, seg_col, projected, logs_all, grad_joined)
    output_sum = add_low(
        columns_of(grad_output, core), swap_cores(columns_of(grad_output, 1 - core))
    )
    grad_projected = jnp.concatenate(grad_heads, axis=1)
    if four_chips:
        feed_sum = scatter_end(after(feed_state, grad_projected))
        feed_parts = scatter_z_begin(jnp.concatenate(feed_sum, axis=0))
        grad_projected = after(grad_projected, *feed_sum)
    grad_inputs = dot_tn(normed_one, grad_projected).astype(low)
    grad_normed_all = dot_nt(grad_projected, inputs_low)
    grad_normed_one = tokens_of(grad_normed_all, core) + swap_cores(
        tokens_of(grad_normed_all, 1 - core).astype(low)
    ).astype(jnp.float32)
    unit_one, inverse_one = normalize(residual)
    grad_residual = norm_back(grad_normed_one, vectors[0], unit_one, inverse_one)
    input_grad = (grad_middle + grad_residual).astype(low)

    def heads_sum(values):
        return lax.dynamic_update_slice_in_dim(
            jnp.zeros((features,), jnp.float32), column_sum(values), core * half, 0
        )

    head_rows = jnp.stack(
        [
            column_sum(grad_normed_one * unit_one),
            column_sum(grad_normed_one),
            column_sum(grad_normed_two * unit_two),
            column_sum(grad_normed_two),
            heads_sum(grad_heads[0]),
            heads_sum(grad_heads[2]),
            column_sum(grad_attended),
            column_sum(grad_top),
        ]
    )
    grad_vectors = jnp.concatenate([head_rows, bias_sums.reshape(-1, features)], axis=0)
    vector_columns = jnp.pad(grad_vectors.T.astype(low), ((0, 0), (0, LANES - vector_rows)))
    first_grad = jnp.concatenate([grad_inputs, output_sum, vector_columns], axis=1)
    first_grad = first_grad.reshape(seq_count, groups, rows_piece, -1)
    if four_chips:
        middle_owner = seq_count // 2
        split = []
        for offset in range(4):
            split.append(
                [
                    lax.dynamic_index_in_dim(part, group ^ offset, 1, keepdims=False)
                    for part in (first_grad[:middle_owner], first_grad[middle_owner:])
                ]
            )
        feed_piece = add_low(*after(feed_parts, grad_inputs))
        feed_pieces = regather_begin(feed_piece)
        split, feed_pieces = after((split, feed_pieces))
        first_state = scatter_begin_joined(*split)
        output_parts = from_chip_begin(after(output_low, split))
        first_state, output_parts = after((first_state, output_parts))
        first_state, gates = scatter_middle(first_state)
        grad_parts = from_chip_begin(after(input_grad, *gates))
        first_parts = scatter_z_begin(jnp.concatenate(scatter_end(first_state), axis=0))
        feed_mine = jnp.stack(feed_pieces)
        feed_other = swap_cores(feed_mine)
        place = jnp.stack([group, core]).astype(jnp.int32)
        new_expand, new_reduce = renew_feed(
            place,
            feed_mine,
            feed_other,
            (expand_weight, expand_moment, expand_second),
            (reduce_weight, reduce_moment, reduce_second),
        )
        first_parts, new_expand, grad_parts = after((first_parts, new_expand, grad_parts))
        first_pieces = regather_begin(add_low(*first_parts))
        first_mine = jnp.stack(first_pieces)
        first_other = swap_cores(first_mine)
        layer_output = from_chip_end(*output_parts)
        new_inputs, new_output = renew_first(
            place,
            first_mine,
            first_other,
            (inputs_weight, inputs_moment, inputs_second),
            (output_weight, output_moment, output_second),
        )
        input_grad = from_chip_end(*grad_parts)
        vector_slice = slice(wide + half, wide + half + vector_rows)
        vector_parts = first_mine[..., vector_slice].astype(jnp.float32) + first_other[
            ..., vector_slice
        ].astype(jnp.float32)
        sum_vectors = in_order(*[vector_parts[offset] for offset in range(4)], 0)
        sum_vectors = sum_vectors.reshape(owned, vector_rows).T
    else:
        first_sum = lax.psum_scatter(
            first_grad, "dp", scatter_dimension=1, axis_index_groups=same_core
        )
        layer_output, input_grad = from_chip(output_low), from_chip(input_grad)
        every_first = regather(scatter_z(first_sum))
        sum_expand = regather(scatter_z(expand_sum.reshape(seq_count, owned, -1)))
        sum_reduce = regather(scatter_z(reduce_sum.reshape(seq_count, units_piece, features)))
    def renew(weight, moment, second, gradient, step_rate, weight_decay):
        return adamw_step(
            weight, moment, second, gradient.astype(jnp.float32), step_rate, weight_decay
        )

    if not four_chips:
        sum_expand = sum_expand.reshape(dp_count, owned, seq_count, units_piece)
        sum_expand = sum_expand.transpose(1, 2, 0, 3).reshape(expand_weight.shape)
        sum_reduce = sum_reduce.reshape(reduce_weight.shape)
        sum_first = every_first.transpose(0, 2, 1, 3)
        sum_inputs = sum_first[..., :wide].reshape(groups, rows_piece, 2, 3, half)
        sum_inputs = sum_inputs.transpose(0, 1, 3, 2, 4).reshape(inputs_weight.shape)
        sum_output = sum_first[..., wide : wide + half].reshape(output_weight.shape)
        sum_vectors = sum_first[..., wide + half : wide + half + vector_rows].astype(jnp.float32)
        sum_vectors = jnp.sum(sum_vectors, axis=2).reshape(owned, vector_rows).T
        new_inputs = renew(inputs_weight, inputs_moment, inputs_second, sum_inputs, 0.03, decay_rate)
        new_output = renew(output_weight, output_moment, output_second, sum_output, 0.3, decay_rate)
        new_expand = renew(expand_weight, expand_moment, expand_second, sum_expand, 0.03, decay_rate)
        new_reduce = renew(reduce_weight, reduce_moment, reduce_second, sum_reduce, 0.02, decay_rate)
    new_vectors = renew(vector_params, vector_moment, vector_second, sum_vectors, 0.5, 0.0)
    return (
        layer_output,
        input_grad,
        *new_inputs,
        *new_output,
        *new_expand,
        *new_reduce,
        *new_vectors,
    )


def solution(mesh):
    tokens = P("dp", "seq", None)
    rows = P("seq", None)
    columns = P(None, "seq")
    in_specs = (tokens, tokens, P("dp", None)) + (rows,) * 12 + (columns,) * 3
    out_specs = (tokens, tokens) + (rows,) * 12 + (columns,) * 3
    return jax.shard_map(
        partial(on_device, mesh.shape["dp"], mesh.shape["seq"]),
        mesh=mesh,
        in_specs=in_specs,
        out_specs=out_specs,
        check_vma=False,
    )
```
